128 devices in a mesh: row: 16 (over y, x_hi, core), col: 8 (over x_lo, z).
Axes of the slice: x: 4 (x_hi: 2, x_lo: 2; x = x_hi * 2 + x_lo), y: 4, z: 4, core: 2. Of those that a mesh axis runs over, the one named last changes fastest.
Arguments:
- object_field: float32 [2, 8192, 4096], P(None, 'row', 'col'), may hold values from -6 to 6
- probe: float32 [2, 4, 256, 256], replicated, may hold values from -5 to 5
- amplitudes: float32 [16, 8, 6, 256, 256], P('row', 'col'), may hold values from 0.1 to 2
- positions: int32 [16, 8, 6, 2], P('row', 'col'), may hold values from 1 to 511, as said below
- counts: int32 [16, 8], P('row', 'col'), may hold values from 1 to 6, as said below
Outputs:
- object_new: float32 [2, 8192, 4096], P(None, 'row', 'col')
- probe_new: float32 [2, 4, 256, 256], replicated
- position_grad: float32 [16, 8, 6, 2], P('row', 'col')
The draws below stay inside these ranges and needn't reach their ends.
Inputs may be any that keep to these rules, and one draw needn't show every extreme that they name: `counts`: live scan positions of each tile; slots at or past the count are unused and ignored; some tile has all 6 slots live. `positions`: offset of a patch's first cell in its tile extended by 128 cells on each side.
All inputs are finite; a program needn't handle non-finite values.
Results may differ from the reference program's by a relative error of at most 0.0003.
Values sent between devices are 32-bit elements; how exact they have to be, the bound alone decides.
A program may use at most 192 MiB of HBM per device.

```python
import jax
import jax.numpy as jnp
from jax import lax

P_SIZE = 256
MODES = 4
HALO = 128
TILE = 512
POS_CAP = 6
NR = 8192
NC = 4096
N_ROW = 16
N_COL = 8


def draw_positions(key, part):
    upper = TILE + 2 * HALO - P_SIZE
    values = jax.random.randint(key, (N_ROW, N_COL, POS_CAP, 2), 1, upper)
    values = values.at[0, 0, 0, 0].set(1)
    values = values.at[0, 0, 0, 1].set(upper - 1)
    return values.astype(jnp.int32)


def draw_counts(key, part):
    total_tiles = N_ROW * N_COL
    low_key, pick_key = jax.random.split(key, 2)
    values = jax.random.randint(low_key, (total_tiles,), max(POS_CAP // 2, 1), POS_CAP + 1)
    chosen = jax.random.randint(pick_key, (), 0, total_tiles)
    values = values.at[chosen].set(POS_CAP)
    values = values.at[(chosen + 1) % total_tiles].set(1)
    return values.reshape(N_ROW, N_COL).astype(jnp.int32)


def shard_levels(rng, extent, cuts, smallest, high):
    level = 1.0
    for axis_at, blocks in cuts:
        steps = jax.random.uniform(jax.random.fold_in(jax.random.fold_in(rng, 6), axis_at), (blocks,), jnp.float32, smallest / len(cuts), high / len(cuts))
        level = level * jnp.repeat(jnp.exp(steps), extent[axis_at] // blocks).reshape((-1,) + (1,) * (len(extent) - 1 - axis_at))
    return level


def bell_draw(key, dims, width, most, cuts=(), kind=jnp.bfloat16):
    drawn = width * jax.random.normal(key, dims, jnp.float32)
    if cuts:
        drawn = drawn * shard_levels(key, dims, cuts, -0.22, 0.18)
    return jnp.clip(drawn, -most, most).astype(kind)


def setup_inputs(seed: int = 0) -> dict:
    arg_keys = jax.random.split(jax.random.key(seed), 6)
    object_field = bell_draw(arg_keys[0], (2, NR, NC), 1.0, 6.0, ((1, 16), (2, 8)), jnp.float32)
    probe = bell_draw(arg_keys[1], (2, MODES, P_SIZE, P_SIZE), 0.35, 5.0, (), jnp.float32)
    amplitudes = jnp.clip(0.1 + 1.9 * jax.random.uniform(arg_keys[2], (N_ROW, N_COL, POS_CAP, P_SIZE, P_SIZE), jnp.float32) ** shard_levels(arg_keys[2], (N_ROW, N_COL, POS_CAP, P_SIZE, P_SIZE), ((0, 16), (1, 8)), -0.2, 0.2), 0.1, 2.0)
    positions = draw_positions(jax.random.fold_in(arg_keys[5], 71), 0)
    counts = draw_counts(jax.random.fold_in(arg_keys[5], 71), 0)
    return {"object_field": object_field, "probe": probe, "amplitudes": amplitudes, "positions": positions, "counts": counts}


INTENSITY_FLOOR = 0.1
EPSILON = 1e-06

def reference(object_field, probe, amplitudes, positions, counts):
    padded = jnp.pad(object_field, ((0, 0), (HALO, HALO), (HALO, HALO)))
    probe_c = lax.complex(probe[0], probe[1])
    total_items = N_ROW * N_COL * POS_CAP
    items = jnp.arange(total_items, dtype=jnp.int32)
    tile_row = items // (N_COL * POS_CAP)
    tile_col = items // POS_CAP % N_COL
    slot_index = items % POS_CAP
    flat_pos = positions.reshape(total_items, 2).astype(jnp.int32)
    live_all = (slot_index < counts.reshape(-1)[tile_row * N_COL + tile_col]).astype(object_field.dtype)
    flat_amp = amplitudes.reshape(total_items, P_SIZE, P_SIZE)

    def visit_item(carry, item):
        spread, probe_grad, energy = carry
        row_start = (tile_row[item] * TILE + flat_pos[item, 0]).astype(jnp.int32)
        col_start = (tile_col[item] * TILE + flat_pos[item, 1]).astype(jnp.int32)
        window = lax.dynamic_slice(padded, (jnp.int32(0), row_start - 1, col_start - 1), (2, P_SIZE + 2, P_SIZE + 2))
        live_flag = live_all[item]
        patch_c = lax.complex(window[0, 1:-1, 1:-1], window[1, 1:-1, 1:-1])
        exit_wave = probe_c * patch_c[None]
        far_field = jnp.fft.fft2(exit_wave, norm='ortho')
        intensity = lax.optimization_barrier(jnp.sum(jnp.real(far_field) ** 2 + jnp.imag(far_field) ** 2, axis=0))
        modulus = flat_amp[item] / jnp.sqrt(jnp.maximum(intensity, INTENSITY_FLOOR))
        correction = jnp.fft.ifft2(far_field * modulus[None], norm='ortho') - exit_wave
        gradient = lax.optimization_barrier(jnp.sum(jnp.conj(probe_c) * correction, axis=0)) * live_flag
        grad_pair = jnp.stack([jnp.real(gradient), jnp.imag(gradient)])
        probe_term = jnp.conj(patch_c)[None] * correction * live_flag
        probe_grad = probe_grad + jnp.stack([jnp.real(probe_term), jnp.imag(probe_term)])
        energy = energy + live_flag * jnp.mean(jnp.real(patch_c) ** 2 + jnp.imag(patch_c) ** 2)
        corner_at = (jnp.int32(0), row_start, col_start)
        current = lax.dynamic_slice(spread, corner_at, (2, P_SIZE, P_SIZE))
        spread = lax.dynamic_update_slice(spread, current + grad_pair, corner_at)
        slope_rows = 0.5 * (window[:, 2:, 1:-1] - window[:, :-2, 1:-1])
        slope_cols = 0.5 * (window[:, 1:-1, 2:] - window[:, 1:-1, :-2])
        shift_grad = jnp.stack([jnp.sum(grad_pair * slope_rows) / P_SIZE, jnp.sum(grad_pair * slope_cols) / P_SIZE])
        return ((spread, probe_grad, energy), shift_grad)
    start_carry = (jnp.zeros(padded.shape, object_field.dtype), jnp.zeros_like(probe), jnp.zeros((), object_field.dtype))
    (spread, probe_grad, energy), shift_all = lax.scan(visit_item, start_carry, items)
    fold = spread[:, HALO:HALO + object_field.shape[1], HALO:HALO + object_field.shape[2]]
    illumination = jnp.max(lax.optimization_barrier(jnp.sum(probe * probe, axis=(0, 1))))
    object_new = object_field + fold / illumination
    probe_new = probe + probe_grad / (energy + EPSILON)
    position_grad = shift_all.reshape(N_ROW, N_COL, POS_CAP, 2)
    return (object_new, probe_new, position_grad)
```

```python
import math

import ml_dtypes
import numpy as np
import jax
import jax.numpy as jnp
from jax import lax
from jax.experimental import pallas as pl
from jax.experimental.pallas import tpu as pltpu
from jax.sharding import PartitionSpec as P

HALO = 128
INTENSITY_FLOOR = 0.1
EPSILON = 1e-06
F32 = jnp.float32
BF16 = jnp.bfloat16


def padded(x, sides, width):
    for axis, dim in sides:
        peers, length = (lax.axis_size(axis), x.shape[dim])
        up = [(i, (i + 1) % peers) for i in range(peers - 1)]
        down = [(j, i) for i, j in up]
        last = lax.slice_in_dim(x, length - width, length, axis=dim)
        first = lax.slice_in_dim(x, 0, width, axis=dim)
        before = lax.ppermute(last, axis, up)
        after = lax.ppermute(first, axis, down)
        x = jnp.concatenate([before, x, after], axis=dim)
    return x


def shifted(x, axis, by):
    peers = lax.axis_size(axis)
    pairs = [(i, i + by) for i in range(peers) if 0 <= i + by < peers]
    return lax.ppermute(x, axis, pairs)


def dft_tables(pixels):
    half = pixels // 2
    k = np.arange(half)[:, None]
    n = np.arange(half)[None, :]
    out = []
    for parity in (0, 1):
        angle = (n * (2 * k + parity) % pixels) * (2.0 * math.pi / pixels)
        c = np.cos(angle) / math.sqrt(pixels)
        s = np.sin(angle) / math.sqrt(pixels)
        out.append(np.block([[c, s], [-s, c]]))
    both = []
    for m in (out[0], out[1], out[0].T, out[1].T):
        m = m.astype(np.float32)
        hi = m.astype(ml_dtypes.bfloat16)
        lo = (m - hi.astype(np.float32)).astype(ml_dtypes.bfloat16)
        both.append(np.stack([hi, lo]))
    return np.stack(both)


def parity_table(pixels):
    half = pixels // 2
    t = np.zeros((pixels, pixels), np.float32)
    for j in range(half):
        t[2 * j, j] = 1.0
        t[2 * j + 1, half + j] = 1.0
    return t.astype(ml_dtypes.bfloat16)


def split(x):
    hi = x.astype(BF16)
    return hi, (x - hi.astype(F32)).astype(BF16)


def mm(a, b):
    return jnp.dot(a, b, preferred_element_type=F32)


def from_left(table, x):
    hi, lo = split(x)
    return mm(jnp.concatenate([table[0], table[0], table[1]], 1), jnp.concatenate([hi, lo, hi], 0))


def from_right(x, table):
    hi, lo = split(x)
    return mm(jnp.concatenate([hi, lo, hi], 1), jnp.concatenate([table[0], table[0], table[1]], 0))


def step_kernel(pos_ref, count_ref, canvas_ref, probe_ref, amp_ref, tab_ref, par_ref,
                spread_ref, pg_ref, shift_ref, energy_ref,
                win, patch, far, inten, grad, col0, col1):
    n = probe_ref.shape[2]
    h = n // 2
    modes = probe_ref.shape[1]
    slots = amp_ref.shape[0]
    spread_ref[...] = jnp.zeros_like(spread_ref)
    pg_ref[...] = jnp.zeros_like(pg_ref)
    energy_ref[0] = 0.0
    for s in range(slots):
        shift_ref[s, 0] = 0.0
        shift_ref[s, 1] = 0.0

    def visit(s, carry):
        a = pos_ref[s, 0]
        b = pos_ref[s, 1]
        base = pl.multiple_of((b - 1) // 128 * 128, 128)
        turn = (b - 1) % 128
        row = pl.multiple_of((a - 1) // 8 * 8, 8)
        row_turn = (a - 1) % 8
        power = jnp.zeros((1, 1), F32)
        for part in range(2):
            w = canvas_ref[part, pl.ds(row, n + 16), pl.ds(base, 512)]
            w = pltpu.roll(w, 512 - turn, 1)
            w = pltpu.roll(w, n + 16 - row_turn, 0)[:n + 8]
            win[part] = w[:, :384]
            p = pltpu.roll(w, 511, 1)[1:n + 1, :n]
            patch[part] = p
            power += jnp.sum(p * p, keepdims=True)
        energy_ref[0] += power[0, 0] / (n * n)

        inten[...] = jnp.zeros_like(inten)

        def forward(k, c):
            pr, pi = probe_ref[0, k], probe_ref[1, k]
            pr_, pi_ = patch[0], patch[1]
            er = pr * pr_ - pi * pi_
            ei = pr * pi_ + pi * pr_
            up = jnp.concatenate([er[:h] + er[h:], ei[:h] + ei[h:]], 0)
            dn = jnp.concatenate([er[:h] - er[h:], ei[:h] - ei[h:]], 0)
            su = from_left(tab_ref[0], up)
            sd = from_left(tab_ref[1], dn)
            zr = jnp.concatenate([su[:h], sd[:h]], 0)
            zi = jnp.concatenate([su[h:], sd[h:]], 0)
            lf = jnp.concatenate([zr[:, :h] + zr[:, h:], zi[:, :h] + zi[:, h:]], 1)
            rt = jnp.concatenate([zr[:, :h] - zr[:, h:], zi[:, :h] - zi[:, h:]], 1)
            fa = from_right(lf, tab_ref[2])
            fb = from_right(rt, tab_ref[3])
            far[k, 0] = fa
            far[k, 1] = fb
            inten[:, :h] += fa[:, :h] * fa[:, :h] + fa[:, h:] * fa[:, h:]
            inten[:, h:] += fb[:, :h] * fb[:, :h] + fb[:, h:] * fb[:, h:]
            return c

        lax.fori_loop(0, modes, forward, 0)
        hi, lo = split(amp_ref[s])
        am = mm(hi, par_ref[...]) + mm(lo, par_ref[...])
        col0[...] = am[:, :h]
        col1[...] = am[:, h:]
        am = jnp.concatenate([jnp.concatenate([col[pl.ds(p, h, 2), :] for p in range(2)], 0) for col in (col0, col1)], 1)
        inten[...] = am * lax.rsqrt(jnp.maximum(inten[...], INTENSITY_FLOOR)) - 1.0
        grad[...] = jnp.zeros_like(grad)

        def backward(k, c):
            ma, mb = inten[:, :h], inten[:, h:]
            e = from_right(far[k, 0] * jnp.concatenate([ma, ma], 1), tab_ref[0])
            o = from_right(far[k, 1] * jnp.concatenate([mb, mb], 1), tab_ref[1])
            lo = e + o
            hi = e - o
            ev = jnp.concatenate([jnp.concatenate([lo[:h, :h], hi[:h, :h]], 1),
                                  jnp.concatenate([lo[:h, h:], hi[:h, h:]], 1)], 0)
            od = jnp.concatenate([jnp.concatenate([lo[h:, :h], hi[h:, :h]], 1),
                                  jnp.concatenate([lo[h:, h:], hi[h:, h:]], 1)], 0)
            e2 = from_left(tab_ref[2], ev)
            o2 = from_left(tab_ref[3], od)
            for r, half in ((slice(0, h), e2 + o2), (slice(h, n), e2 - o2)):
                cr, ci = half[:h], half[h:]
                pr, pi = probe_ref[0, k, r], probe_ref[1, k, r]
                qr, qi = patch[0, r], patch[1, r]
                grad[0, r] += pr * cr + pi * ci
                grad[1, r] += pr * ci - pi * cr
                pg_ref[0, k, r] += qr * cr + qi * ci
                pg_ref[1, k, r] += qr * ci - qi * cr
            return c

        lax.fori_loop(0, modes, backward, 0)
        along = jnp.zeros((1, 1), F32)
        across = jnp.zeros((1, 1), F32)
        base2 = pl.multiple_of(b // 128 * 128, 128)
        row2 = pl.multiple_of(a // 8 * 8, 8)
        for part in range(2):
            g = grad[part]
            w = win[part]
            mid = pltpu.roll(w, 383, 1)[:, :n]
            along += jnp.sum(g * (mid[2:n + 2] - mid[0:n]), keepdims=True)
            nxt = pltpu.roll(w, 382, 1)[1:n + 1, :n]
            across += jnp.sum(g * (nxt - w[1:n + 1, :n]), keepdims=True)
            g = pltpu.roll(jnp.concatenate([g, jnp.zeros((n, 128), F32)], 1), b % 128, 1)
            g = pltpu.roll(jnp.concatenate([g, jnp.zeros((8, 384), F32)], 0), a % 8, 0)
            spread_ref[part, pl.ds(row2, n + 8), pl.ds(base2, 384)] += g
        shift_ref[s, 0] = along[0, 0] * (0.5 / n)
        shift_ref[s, 1] = across[0, 0] * (0.5 / n)
        return carry

    lax.fori_loop(0, count_ref[0], visit, 0)


def step(pos, count, canvas, probe, amp):
    n = probe.shape[2]
    modes = probe.shape[1]
    slots = amp.shape[0]
    rows = canvas.shape[1] - 8
    vmem = pl.BlockSpec(memory_space=pltpu.VMEM)
    smem = pl.BlockSpec(memory_space=pltpu.SMEM)
    return pl.pallas_call(
        step_kernel,
        out_shape=(
            jax.ShapeDtypeStruct((2, rows, rows), F32),
            jax.ShapeDtypeStruct(probe.shape, F32),
            jax.ShapeDtypeStruct((slots, 2), F32),
            jax.ShapeDtypeStruct((1,), F32),
        ),
        in_specs=[smem, smem, vmem, vmem, vmem, vmem, vmem],
        out_specs=(vmem, vmem, smem, smem),
        scratch_shapes=[
            pltpu.VMEM((2, n + 8, 384), F32),
            pltpu.VMEM((2, n, n), F32),
            pltpu.VMEM((modes, 2, n, n), F32),
            pltpu.VMEM((n, n), F32),
            pltpu.VMEM((2, n, n), F32),
            pltpu.VMEM((n, n // 2), F32),
            pltpu.VMEM((n, n // 2), F32),
        ],
        compiler_params=pltpu.CompilerParams(vmem_limit_bytes=50 * 2**20),
    )(pos, count, canvas, probe, amp, jnp.asarray(dft_tables(n)), jnp.asarray(parity_table(n)))


def body(object_field, probe, amplitudes, positions, counts):
    tile_cells = object_field.shape[1]
    extended = padded(object_field, (("row", 1), ("col", 2)), HALO)
    canvas = jnp.pad(extended, ((0, 0), (0, 8), (0, 128)))
    spread, probe_grad, shift, energy = step(positions[0, 0], counts[0], canvas, probe, amplitudes[0, 0])
    position_grad = shift[None, None]
    summed, total_energy = lax.psum((probe_grad, energy[0]), ("row", "col"))
    probe_new = probe + summed / (total_energy + EPSILON)
    for offset_sign in (1, -1):
        outgoing = spread[:, tile_cells + HALO :, :] if offset_sign == 1 else spread[:, :HALO, :]
        arrived = shifted(outgoing, "row", offset_sign)
        first_row = HALO if offset_sign == 1 else tile_cells
        spread = spread.at[:, first_row : first_row + HALO, :].add(arrived)
    spread = spread[:, HALO : HALO + tile_cells, :]
    for offset_sign in (1, -1):
        outgoing = spread[:, :, tile_cells + HALO :] if offset_sign == 1 else spread[:, :, :HALO]
        arrived = shifted(outgoing, "col", offset_sign)
        first_col = HALO if offset_sign == 1 else tile_cells
        spread = spread.at[:, :, first_col : first_col + HALO].add(arrived)
    folded = spread[:, :, HALO : HALO + tile_cells]
    illumination = jnp.max(jnp.sum(probe * probe, axis=(0, 1)))
    object_new = object_field + folded / illumination
    return (object_new, probe_new, position_grad)


def solution(mesh):
    return jax.shard_map(
        body,
        mesh=mesh,
        in_specs=(
            P(None, "row", "col"),
            P(),
            P("row", "col", None, None, None),
            P("row", "col", None, None),
            P("row", "col"),
        ),
        out_specs=(P(None, "row", "col"), P(), P("row", "col", None, None)),
        check_vma=False,
    )
```

```python
import functools
import math

import ml_dtypes
import numpy as np
import jax
import jax.numpy as jnp
from jax import lax
from jax.experimental import pallas as pl
from jax.experimental.pallas import tpu as pltpu
from jax.sharding import PartitionSpec as P

HALO = 128
INTENSITY_FLOOR = 0.1
EPSILON = 1e-06
F32 = jnp.float32
BF16 = jnp.bfloat16


def dft_tables(pixels):
    half = pixels // 2
    k = np.arange(half)[:, None]
    n = np.arange(half)[None, :]
    out = []
    for parity in (0, 1):
        angle = (n * (2 * k + parity) % pixels) * (2.0 * math.pi / pixels)
        c = np.cos(angle) / math.sqrt(pixels)
        s = np.sin(angle) / math.sqrt(pixels)
        out.append(np.block([[c, s], [-s, c]]))
    both = []
    for m in (out[0], out[1], out[0].T, out[1].T):
        m = m.astype(np.float32)
        hi = m.astype(ml_dtypes.bfloat16)
        lo = (m - hi.astype(np.float32)).astype(ml_dtypes.bfloat16)
        both.append(np.stack([hi, lo]))
    return np.stack(both)


def parity_table(pixels):
    half = pixels // 2
    t = np.zeros((pixels, pixels), np.float32)
    for j in range(half):
        t[2 * j, j] = 1.0
        t[2 * j + 1, half + j] = 1.0
    return t.astype(ml_dtypes.bfloat16)


def split(x):
    hi = x.astype(BF16)
    return hi, (x - hi.astype(F32)).astype(BF16)


def mm(a, b):
    return jnp.dot(a, b, preferred_element_type=F32)


def from_left(table, x):
    hi, lo = split(x)
    return mm(jnp.concatenate([table[0], table[0], table[1]], 1), jnp.concatenate([hi, lo, hi], 0))


def from_right(x, table):
    hi, lo = split(x)
    return mm(jnp.concatenate([hi, lo, hi], 1), jnp.concatenate([table[0], table[0], table[1]], 0))


def step_kernel(pos_ref, count_ref, canvas_ref, probe_ref, amp_ref, tab_ref, par_ref,
                spread_ref, pg_ref, shift_ref, energy_ref, illum_ref,
                win, patch, far, inten, grad, col0, col1):
    n = probe_ref.shape[2]
    h = n // 2
    modes = probe_ref.shape[1]
    slots = amp_ref.shape[0]
    spread_ref[...] = jnp.zeros_like(spread_ref)
    pg_ref[...] = jnp.zeros_like(pg_ref)
    energy_ref[...] = jnp.zeros_like(energy_ref)
    light = jnp.zeros((n, n), F32)
    for k in range(modes):
        for part in range(2):
            light += probe_ref[part, k] * probe_ref[part, k]
    illum_ref[0] = jnp.max(light)
    for s in range(slots):
        shift_ref[s, 0] = 0.0
        shift_ref[s, 1] = 0.0

    def visit(s, carry):
        a = pos_ref[s, 0]
        b = pos_ref[s, 1]
        base = pl.multiple_of((b - 1) // 128 * 128, 128)
        turn = (b - 1) % 128
        row = pl.multiple_of((a - 1) // 8 * 8, 8)
        row_turn = (a - 1) % 8
        power = jnp.zeros((1, 1), F32)
        for part in range(2):
            w = canvas_ref[part, pl.ds(row, n + 16), pl.ds(base, 512)]
            w = pltpu.roll(w, 512 - turn, 1)
            w = pltpu.roll(w, n + 16 - row_turn, 0)[:n + 8]
            win[part] = w[:, :384]
            p = pltpu.roll(w, 511, 1)[1:n + 1, :n]
            patch[part] = p
            power += jnp.sum(p * p, keepdims=True)
        energy_ref[...] += power / (n * n)

        inten[...] = jnp.zeros_like(inten)

        def forward(k, c):
            pr, pi = probe_ref[0, k], probe_ref[1, k]
            pr_, pi_ = patch[0], patch[1]
            er = pr * pr_ - pi * pi_
            ei = pr * pi_ + pi * pr_
            up = jnp.concatenate([er[:h] + er[h:], ei[:h] + ei[h:]], 0)
            dn = jnp.concatenate([er[:h] - er[h:], ei[:h] - ei[h:]], 0)
            su = from_left(tab_ref[0], up)
            sd = from_left(tab_ref[1], dn)
            zr = jnp.concatenate([su[:h], sd[:h]], 0)
            zi = jnp.concatenate([su[h:], sd[h:]], 0)
            lf = jnp.concatenate([zr[:, :h] + zr[:, h:], zi[:, :h] + zi[:, h:]], 1)
            rt = jnp.concatenate([zr[:, :h] - zr[:, h:], zi[:, :h] - zi[:, h:]], 1)
            fa = from_right(lf, tab_ref[2])
            fb = from_right(rt, tab_ref[3])
            far[k, 0] = fa
            far[k, 1] = fb
            inten[:, :h] += fa[:, :h] * fa[:, :h] + fa[:, h:] * fa[:, h:]
            inten[:, h:] += fb[:, :h] * fb[:, :h] + fb[:, h:] * fb[:, h:]
            return c

        lax.fori_loop(0, modes, forward, 0)
        hi, lo = split(amp_ref[s])
        am = mm(hi, par_ref[...]) + mm(lo, par_ref[...])
        col0[...] = am[:, :h]
        col1[...] = am[:, h:]
        am = jnp.concatenate([jnp.concatenate([col[pl.ds(p, h, 2), :] for p in range(2)], 0) for col in (col0, col1)], 1)
        inten[...] = am * lax.rsqrt(jnp.maximum(inten[...], INTENSITY_FLOOR)) - 1.0
        grad[...] = jnp.zeros_like(grad)

        def backward(k, c):
            ma, mb = inten[:, :h], inten[:, h:]
            e = from_right(far[k, 0] * jnp.concatenate([ma, ma], 1), tab_ref[0])
            o = from_right(far[k, 1] * jnp.concatenate([mb, mb], 1), tab_ref[1])
            lo = e + o
            hi = e - o
            ev = jnp.concatenate([jnp.concatenate([lo[:h, :h], hi[:h, :h]], 1),
                                  jnp.concatenate([lo[:h, h:], hi[:h, h:]], 1)], 0)
            od = jnp.concatenate([jnp.concatenate([lo[h:, :h], hi[h:, :h]], 1),
                                  jnp.concatenate([lo[h:, h:], hi[h:, h:]], 1)], 0)
            e2 = from_left(tab_ref[2], ev)
            o2 = from_left(tab_ref[3], od)
            for r, half in ((slice(0, h), e2 + o2), (slice(h, n), e2 - o2)):
                cr, ci = half[:h], half[h:]
                pr, pi = probe_ref[0, k, r], probe_ref[1, k, r]
                qr, qi = patch[0, r], patch[1, r]
                grad[0, r] += pr * cr + pi * ci
                grad[1, r] += pr * ci - pi * cr
                pg_ref[0, k, r] += qr * cr + qi * ci
                pg_ref[1, k, r] += qr * ci - qi * cr
            return c

        lax.fori_loop(0, modes, backward, 0)
        along = jnp.zeros((1, 1), F32)
        across = jnp.zeros((1, 1), F32)
        base2 = pl.multiple_of(b // 128 * 128, 128)
        row2 = pl.multiple_of(a // 8 * 8, 8)
        for part in range(2):
            g = grad[part]
            w = win[part]
            mid = pltpu.roll(w, 383, 1)[:, :n]
            along += jnp.sum(g * (mid[2:n + 2] - mid[0:n]), keepdims=True)
            nxt = pltpu.roll(w, 382, 1)[1:n + 1, :n]
            across += jnp.sum(g * (nxt - w[1:n + 1, :n]), keepdims=True)
            g = pltpu.roll(jnp.concatenate([g, jnp.zeros((n, 128), F32)], 1), b % 128, 1)
            g = pltpu.roll(jnp.concatenate([g, jnp.zeros((8, 384), F32)], 0), a % 8, 0)
            spread_ref[part, pl.ds(row2, n + 8), pl.ds(base2, 384)] += g
        shift_ref[s, 0] = along[0, 0] * (0.5 / n)
        shift_ref[s, 1] = across[0, 0] * (0.5 / n)
        return carry

    lax.fori_loop(0, count_ref[0], visit, 0)


def step(pos, count, canvas, probe, amp):
    n = probe.shape[2]
    modes = probe.shape[1]
    slots = amp.shape[0]
    rows = canvas.shape[1] - 8
    vmem = pl.BlockSpec(memory_space=pltpu.VMEM)
    smem = pl.BlockSpec(memory_space=pltpu.SMEM)
    return pl.pallas_call(
        step_kernel,
        out_shape=(
            jax.ShapeDtypeStruct((2, rows, rows), F32),
            jax.ShapeDtypeStruct(probe.shape, F32),
            jax.ShapeDtypeStruct((slots, 2), F32),
            jax.ShapeDtypeStruct((8, n), F32),
            jax.ShapeDtypeStruct((1,), F32),
        ),
        in_specs=[smem, smem, vmem, vmem, vmem, vmem, vmem],
        out_specs=(vmem, vmem, smem, vmem, smem),
        scratch_shapes=[
            pltpu.VMEM((2, n + 8, 384), F32),
            pltpu.VMEM((2, n, n), F32),
            pltpu.VMEM((modes, 2, n, n), F32),
            pltpu.VMEM((n, n), F32),
            pltpu.VMEM((2, n, n), F32),
            pltpu.VMEM((n, n // 2), F32),
            pltpu.VMEM((n, n // 2), F32),
        ],
        compiler_params=pltpu.CompilerParams(vmem_limit_bytes=50 * 2**20),
    )(pos, count, canvas, probe, amp, jnp.asarray(dft_tables(n)), jnp.asarray(parity_table(n)))


MESH = pl.DeviceIdType.MESH
SIDES = [(-1, 0), (1, 0), (0, -1), (0, 1), (-1, -1), (-1, 1), (1, -1), (1, 1)]


def place():
    return lax.axis_index("row"), lax.axis_index("col")


def present(side, limits):
    row, col = place()
    fits = None
    for at, by, limit in ((row, side[0], limits[0]), (col, side[1], limits[1])):
        if by:
            ok = at > 0 if by < 0 else at < limit - 1
            fits = ok if fits is None else jnp.logical_and(fits, ok)
    return fits


def neighbour(side):
    row, col = place()
    return (row + side[0], col + side[1])


def edge(by, cells):
    return pl.ds(0, cells) if by == 0 else (pl.ds(0, HALO) if by < 0 else pl.ds(cells - HALO, HALO))


def rim(by, cells):
    return pl.ds(HALO, cells) if by == 0 else (pl.ds(0, HALO) if by < 0 else pl.ds(cells + HALO, HALO))


def greet_sides(limits):
    barrier = pltpu.get_barrier_semaphore()
    total = jnp.int32(0)
    for side in SIDES:
        here = present(side, limits)
        total += here.astype(jnp.int32)

        @pl.when(here)
        def _():
            pl.semaphore_signal(barrier, inc=1, device_id=neighbour(side), device_id_type=MESH)

    return barrier, total


def halo_kernel(limits, obj_ref, canvas_ref, zeros, own_sem, zero_sems, send_sems, recv_sems):
    cells = obj_ref.shape[1]
    barrier, total = greet_sides(limits)
    own = pltpu.make_async_copy(obj_ref, canvas_ref.at[:, pl.ds(HALO, cells), pl.ds(HALO, cells)], own_sem)
    own.start()
    zeros[...] = jnp.zeros_like(zeros)
    pl.semaphore_wait(barrier, total)
    steps = []
    for i, side in enumerate(SIDES):
        here = present(side, limits)
        back = SIDES.index((-side[0], -side[1]))
        send = pltpu.make_async_remote_copy(
            src_ref=obj_ref.at[:, edge(side[0], cells), edge(side[1], cells)],
            dst_ref=canvas_ref.at[:, rim(-side[0], cells), rim(-side[1], cells)],
            send_sem=send_sems.at[i],
            recv_sem=recv_sems.at[back],
            device_id=neighbour(side),
            device_id_type=MESH,
        )
        landed = canvas_ref.at[:, rim(side[0], cells), rim(side[1], cells)]
        tall, wide = (cells if side[0] == 0 else HALO), (cells if side[1] == 0 else HALO)
        blank = pltpu.make_async_copy(zeros.at[:, pl.ds(0, tall), pl.ds(0, wide)], landed, zero_sems.at[i])
        arrive = pltpu.make_async_copy(landed, landed, recv_sems.at[i])
        steps.append((here, send, blank, arrive))

        @pl.when(here)
        def _(send=send):
            send.start()

        @pl.when(jnp.logical_not(here))
        def _(blank=blank):
            blank.start()

    for here, send, blank, arrive in steps:
        @pl.when(here)
        def _(send=send, arrive=arrive):
            send.wait_send()
            arrive.wait()

        @pl.when(jnp.logical_not(here))
        def _(blank=blank):
            blank.wait()

    own.wait()


def exchange_halo(obj, limits):
    cells = obj.shape[1]
    return pl.pallas_call(
        functools.partial(halo_kernel, limits),
        out_shape=jax.ShapeDtypeStruct((2, cells + 2 * HALO + 8, cells + 3 * HALO), F32),
        in_specs=[pl.BlockSpec(memory_space=pl.ANY)],
        out_specs=pl.BlockSpec(memory_space=pl.ANY),
        scratch_shapes=[
            pltpu.VMEM((2, cells, cells), F32),
            pltpu.SemaphoreType.DMA,
            pltpu.SemaphoreType.DMA((8,)),
            pltpu.SemaphoreType.DMA((8,)),
            pltpu.SemaphoreType.DMA((8,)),
        ],
        compiler_params=pltpu.CompilerParams(collective_id=0, has_side_effects=True, vmem_limit_bytes=16 * 2**20),
    )(obj)


def finish_kernel(limits, spread_ref, pg_ref, energy_ref, obj_ref, probe_ref, illum_ref,
                  onew_ref, pnew_ref, land_rows, land_cols, land_corners, mate_half, mate_energy, outbox, inbox,
                  fold_send, fold_recv, mate_send, mate_recv, bulk):
    cells = obj_ref.shape[1]
    row, col = place()
    core = row % 2
    mate = (row + 1 - 2 * core, col)
    pairs, cols = limits[0] // 2, limits[1]
    chips = pairs * cols
    me = row // 2 * cols + col
    chunk = pg_ref.shape[1] // chips

    def peer(d):
        pair = (row // 2 + d // cols) % pairs
        at = (col + d % cols) % cols
        return pair * cols + at, (2 * pair + core, at)

    barrier, total = greet_sides(limits)

    def greet(d, c):
        pl.semaphore_signal(barrier, inc=1, device_id=peer(d)[1], device_id_type=MESH)
        return c

    pl.semaphore_signal(barrier, inc=1, device_id=mate, device_id_type=MESH)
    lax.fori_loop(1, chips, greet, 0)
    pl.semaphore_wait(barrier, total + chips)

    def to_mate(src, dst, i):
        return pltpu.make_async_remote_copy(src_ref=src, dst_ref=dst, send_sem=mate_send.at[i], recv_sem=mate_recv.at[i],
                                            device_id=mate, device_id_type=MESH)

    first = to_mate(pg_ref.at[1 - core], mate_half, 0)
    second = to_mate(energy_ref, mate_energy, 1)
    first.start()
    second.start()
    first.wait()
    second.wait()
    warm = energy_ref[...] + mate_energy[...]

    def pack(q, c):
        rows = pl.ds(pl.multiple_of(q * chunk, chunk), chunk)
        outbox[q, pl.ds(0, chunk), :] = pg_ref[core, rows, :] + mate_half[rows, :]
        outbox[q, pl.ds(chunk, 8), :] = warm
        return c

    lax.fori_loop(0, chips, pack, 0)

    def scatter(d, c):
        q, device = peer(d)
        pltpu.make_async_remote_copy(src_ref=outbox.at[q], dst_ref=inbox.at[d - 1], send_sem=bulk.at[0], recv_sem=bulk.at[1],
                                     device_id=device, device_id_type=MESH).start()
        return c

    lax.fori_loop(1, chips, scatter, 0)

    folds = []
    for i, side in enumerate(SIDES):
        here = present(side, limits)
        back = SIDES.index((-side[0], -side[1]))
        land = land_rows.at[back] if i < 2 else land_cols.at[back - 2] if i < 4 else land_corners.at[back - 4]
        send = pltpu.make_async_remote_copy(
            src_ref=spread_ref.at[:, rim(side[0], cells), rim(side[1], cells)],
            dst_ref=land,
            send_sem=fold_send.at[i],
            recv_sem=fold_recv.at[back],
            device_id=neighbour(side),
            device_id_type=MESH,
        )
        mine = land_rows.at[i] if i < 2 else land_cols.at[i - 2] if i < 4 else land_corners.at[i - 4]
        arrive = pltpu.make_async_copy(mine, mine, fold_recv.at[i])
        folds.append((here, send, arrive, side, mine))

        @pl.when(here)
        def _(send=send):
            send.start()

    lower = inbox.at[pl.ds(0, chips - 1)]
    pltpu.make_async_copy(lower, lower, bulk.at[0]).wait()
    pltpu.make_async_copy(lower, lower, bulk.at[1]).wait()
    summed = lax.fori_loop(0, chips - 1, lambda d, c: c + inbox[d], outbox[me])
    here_rows = pl.ds(pl.multiple_of(me * chunk, chunk), chunk)
    pnew_ref[core, here_rows, :] = probe_ref[core, here_rows, :] + summed[:chunk] / (summed[chunk:chunk + 1] + EPSILON)
    out = pnew_ref.at[core, here_rows]

    def gather(d, c):
        pltpu.make_async_remote_copy(src_ref=out, dst_ref=out, send_sem=bulk.at[2], recv_sem=bulk.at[3],
                                     device_id=peer(d)[1], device_id_type=MESH).start()
        return c

    lax.fori_loop(1, chips, gather, 0)

    share = 1.0 / illum_ref[0]
    step_rows = 64

    def base(j, c):
        r = pl.ds(pl.multiple_of(j * step_rows, step_rows), step_rows)
        rr = pl.ds(pl.multiple_of(j * step_rows + HALO, step_rows), step_rows)
        for part in range(2):
            onew_ref[part, r, :] = obj_ref[part, r, :] + spread_ref[part, rr, HALO:HALO + cells] * share
        return c

    lax.fori_loop(0, cells // step_rows, base, 0)
    for here, send, arrive, side, mine in folds:
        @pl.when(here)
        def _(send=send, arrive=arrive, side=side, mine=mine):
            send.wait_send()
            arrive.wait()
            for part in range(2):
                onew_ref[part, edge(side[0], cells), edge(side[1], cells)] += mine[part] * share

    rest = pnew_ref.at[core, pl.ds(0, (chips - 1) * chunk)]
    pltpu.make_async_copy(rest, rest, bulk.at[2]).wait()
    pltpu.make_async_copy(rest, rest, bulk.at[3]).wait()
    last = to_mate(pnew_ref.at[core], pnew_ref.at[core], 2)
    last.start()
    last.wait()


def finish(spread, pg, energy, obj, probe, illum, limits):
    cells = obj.shape[1]
    rows, lanes = probe.shape[1], probe.shape[2]
    chips = limits[0] * limits[1] // 2
    chunk = rows // chips
    vmem = pl.BlockSpec(memory_space=pltpu.VMEM)
    return pl.pallas_call(
        functools.partial(finish_kernel, limits),
        out_shape=(jax.ShapeDtypeStruct(obj.shape, F32), jax.ShapeDtypeStruct(probe.shape, F32)),
        in_specs=[vmem, vmem, vmem, vmem, vmem, pl.BlockSpec(memory_space=pltpu.SMEM)],
        out_specs=(vmem, vmem),
        scratch_shapes=[
            pltpu.VMEM((2, 2, HALO, cells), F32),
            pltpu.VMEM((2, 2, cells, HALO), F32),
            pltpu.VMEM((4, 2, HALO, HALO), F32),
            pltpu.VMEM((rows, lanes), F32),
            pltpu.VMEM((8, lanes), F32),
            pltpu.VMEM((chips, chunk + 8, lanes), F32),
            pltpu.VMEM((chips, chunk + 8, lanes), F32),
            pltpu.SemaphoreType.DMA((8,)),
            pltpu.SemaphoreType.DMA((8,)),
            pltpu.SemaphoreType.DMA((3,)),
            pltpu.SemaphoreType.DMA((3,)),
            pltpu.SemaphoreType.DMA((4,)),
        ],
        compiler_params=pltpu.CompilerParams(collective_id=1, has_side_effects=True, vmem_limit_bytes=40 * 2**20),
    )(spread, pg, energy, obj, probe, illum)


def body(limits, object_field, probe, amplitudes, positions, counts):
    canvas = exchange_halo(object_field, limits)
    spread, probe_grad, shift, energy, illum = step(positions[0, 0], counts[0], canvas, probe, amplitudes[0, 0])
    n = probe.shape[2]
    flat = (2, probe.shape[1] * n, n)
    object_new, probe_new = finish(spread, probe_grad.reshape(flat), energy, object_field, probe.reshape(flat), illum, limits)
    return (object_new, probe_new.reshape(probe.shape), shift[None, None])


def solution(mesh):
    return jax.shard_map(
        functools.partial(body, (mesh.shape["row"], mesh.shape["col"])),
        mesh=mesh,
        in_specs=(
            P(None, "row", "col"),
            P(),
            P("row", "col", None, None, None),
            P("row", "col", None, None),
            P("row", "col"),
        ),
        out_specs=(P(None, "row", "col"), P(), P("row", "col", None, None)),
        check_vma=False,
    )
```

```python
import functools
import math

import ml_dtypes
import numpy as np
import jax
import jax.numpy as jnp
from jax import lax
from jax.experimental import pallas as pl
from jax.experimental.pallas import tpu as pltpu
from jax.sharding import PartitionSpec as P

HALO = 128
INTENSITY_FLOOR = 0.1
EPSILON = 1e-06
F32 = jnp.float32
BF16 = jnp.bfloat16
UNROLL = 4


def dft_tables(pixels):
    half = pixels // 2
    k = np.arange(half)[:, None]
    n = np.arange(half)[None, :]
    out = []
    for parity in (0, 1):
        angle = (n * (2 * k + parity) % pixels) * (2.0 * math.pi / pixels)
        c = np.cos(angle) / math.sqrt(pixels)
        s = np.sin(angle) / math.sqrt(pixels)
        out.append(np.block([[c, s], [-s, c]]))
    both = []
    for m in (out[0], out[1], out[0].T, out[1].T):
        m = m.astype(np.float32)
        hi = m.astype(ml_dtypes.bfloat16)
        lo = (m - hi.astype(np.float32)).astype(ml_dtypes.bfloat16)
        both.append(np.stack([hi, lo]))
    return np.stack(both)


def parity_table(pixels):
    half = pixels // 2
    t = np.zeros((pixels, pixels), np.float32)
    for j in range(half):
        t[2 * j, j] = 1.0
        t[2 * j + 1, half + j] = 1.0
    return t.astype(ml_dtypes.bfloat16)


def split(x):
    hi = x.astype(BF16)
    return hi, (x - hi.astype(F32)).astype(BF16)


def mm(a, b):
    return jnp.dot(a, b, preferred_element_type=F32)


def from_left(table, x):
    hi, lo = split(x)
    return mm(jnp.concatenate([table[0], table[0], table[1]], 1), jnp.concatenate([hi, lo, hi], 0))


def from_right(x, table):
    hi, lo = split(x)
    return mm(jnp.concatenate([hi, lo, hi], 1), jnp.concatenate([table[0], table[0], table[1]], 0))


def lane_of():
    return lax.broadcasted_iota(jnp.int32, (1, 8, 128), 2)


def row_of():
    return lax.broadcasted_iota(jnp.int32, (1, 8, 128), 1)


def cut(canvas_ref, patch, a, b):
    n = patch.shape[1]
    groups = n // 8
    t, u = b % 128, a % 8
    row = pl.multiple_of(a - u, 8)
    lane, sub = lane_of(), row_of()
    power = jnp.zeros((8, 128), F32)
    for part in range(2):
        blocks = []
        for j in range(n // 128 + 1):
            v = canvas_ref[part, pl.ds(row, n + 8), pl.ds(pl.multiple_of(b - t + j * 128, 128), 128)]
            v = pltpu.roll(v.reshape(groups + 1, 8, 128), (8 - u) % 8, 1)
            v = jnp.where(sub < 8 - u, v[:groups], v[1:])
            blocks.append(pltpu.roll(v, (128 - t) % 128, 2))
        for j in range(n // 128):
            p = jnp.where(lane < 128 - t, blocks[j], blocks[j + 1])
            power += jnp.sum(p * p, axis=0)
            patch[part, :, j * 128:(j + 1) * 128] = p.reshape(n, 128)
    return power


def lay(canvas_ref, spread_ref, grad, a, b):
    n = grad.shape[1]
    groups = n // 8
    count = n // 128
    t, u = b % 128, a % 8
    row = pl.multiple_of(a - u, 8)
    before = pl.multiple_of(jnp.maximum(a - u - 8, 0), 8)
    lane, sub = lane_of(), row_of()
    down = jnp.zeros((8, 128), F32)
    across = jnp.zeros((8, 128), F32)
    none = jnp.zeros((1, 8, 128), F32)
    for part in range(2):
        turned = [pltpu.roll(grad[part, :, j * 128:(j + 1) * 128].reshape(groups, 8, 128), t, 2) for j in range(count)]
        strips = []
        for j in range(-1, count + 1):
            at = pl.multiple_of(jnp.maximum(b - t + j * 128, 0), 128)
            strips.append(canvas_ref[part, pl.ds(row, n + 8), pl.ds(at, 128)].reshape(groups + 1, 8, 128))
        for j in range(count + 1):
            left = turned[j - 1] if j else 0.0
            g = jnp.where(lane < t, left, turned[j] if j < count else 0.0)
            g = pltpu.roll(g, u, 1)
            g = jnp.where(sub < u, jnp.concatenate([none, g], 0), jnp.concatenate([g, none], 0))
            at = pl.ds(pl.multiple_of(b - t + j * 128, 128), 128)
            spread_ref[part, pl.ds(row, n + 8), at] += g.reshape(n + 8, 128)
            v = strips[j + 1]
            first = canvas_ref[part, pl.ds(before, 8), at].reshape(1, 8, 128)
            nxt = pltpu.roll(v, 7, 1)
            prv = pltpu.roll(jnp.concatenate([first, v], 0), 1, 1)
            nxt = jnp.where(sub < 7, nxt, jnp.concatenate([nxt[1:], none], 0))
            prv = jnp.where(sub < 1, prv[:-1], prv[1:])
            down += jnp.sum(g * (nxt - prv), axis=0)
            nxt = pltpu.roll(v, 127, 2)
            prv = pltpu.roll(v, 1, 2)
            if j < count:
                nxt = jnp.where(lane < 127, nxt, pltpu.roll(strips[j + 2], 127, 2))
            prv = jnp.where(lane < 1, pltpu.roll(strips[j], 1, 2), prv)
            across += jnp.sum(g * (nxt - prv), axis=0)
    return down, across


def step_kernel(pos_ref, count_ref, canvas_ref, probe_ref, amp_ref, tab_ref, par_ref,
                spread_ref, pg_ref, shift_ref, energy_ref, illum_ref,
                patch, far, inten, grad, col0, col1, sums):
    n = probe_ref.shape[2]
    h = n // 2
    modes = probe_ref.shape[1]
    slots = amp_ref.shape[0]
    spread_ref[...] = jnp.zeros_like(spread_ref)
    pg_ref[...] = jnp.zeros_like(pg_ref)
    sums[...] = jnp.zeros_like(sums)
    light = jnp.zeros((n, n), F32)
    for k in range(modes):
        for part in range(2):
            light += probe_ref[part, k] * probe_ref[part, k]
    illum_ref[0] = jnp.max(light)

    def visit(s, carry):
        a = pos_ref[s, 0]
        b = pos_ref[s, 1]
        sums[s, 2] = cut(canvas_ref, patch, a, b)

        inten[...] = jnp.zeros_like(inten)

        def forward(k, c):
            pr, pi = probe_ref[0, k], probe_ref[1, k]
            pr_, pi_ = patch[0], patch[1]
            er = pr * pr_ - pi * pi_
            ei = pr * pi_ + pi * pr_
            up = jnp.concatenate([er[:h] + er[h:], ei[:h] + ei[h:]], 0)
            dn = jnp.concatenate([er[:h] - er[h:], ei[:h] - ei[h:]], 0)
            su = from_left(tab_ref[0], up)
            sd = from_left(tab_ref[1], dn)
            zr = jnp.concatenate([su[:h], sd[:h]], 0)
            zi = jnp.concatenate([su[h:], sd[h:]], 0)
            lf = jnp.concatenate([zr[:, :h] + zr[:, h:], zi[:, :h] + zi[:, h:]], 1)
            rt = jnp.concatenate([zr[:, :h] - zr[:, h:], zi[:, :h] - zi[:, h:]], 1)
            fa = from_right(lf, tab_ref[2])
            fb = from_right(rt, tab_ref[3])
            far[k, 0] = fa
            far[k, 1] = fb
            inten[:, :h] += fa[:, :h] * fa[:, :h] + fa[:, h:] * fa[:, h:]
            inten[:, h:] += fb[:, :h] * fb[:, :h] + fb[:, h:] * fb[:, h:]
            return c

        lax.fori_loop(0, modes, forward, 0, unroll=UNROLL)
        hi, lo = split(amp_ref[s])
        am = mm(hi, par_ref[...]) + mm(lo, par_ref[...])
        col0[...] = am[:, :h]
        col1[...] = am[:, h:]
        am = jnp.concatenate([jnp.concatenate([col[pl.ds(p, h, 2), :] for p in range(2)], 0) for col in (col0, col1)], 1)
        inten[...] = am * lax.rsqrt(jnp.maximum(inten[...], INTENSITY_FLOOR)) - 1.0
        grad[...] = jnp.zeros_like(grad)

        def backward(k, c):
            ma, mb = inten[:, :h], inten[:, h:]
            e = from_right(far[k, 0] * jnp.concatenate([ma, ma], 1), tab_ref[0])
            o = from_right(far[k, 1] * jnp.concatenate([mb, mb], 1), tab_ref[1])
            lo = e + o
            hi = e - o
            ev = jnp.concatenate([jnp.concatenate([lo[:h, :h], hi[:h, :h]], 1),
                                  jnp.concatenate([lo[:h, h:], hi[:h, h:]], 1)], 0)
            od = jnp.concatenate([jnp.concatenate([lo[h:, :h], hi[h:, :h]], 1),
                                  jnp.concatenate([lo[h:, h:], hi[h:, h:]], 1)], 0)
            e2 = from_left(tab_ref[2], ev)
            o2 = from_left(tab_ref[3], od)
            for r, half in ((slice(0, h), e2 + o2), (slice(h, n), e2 - o2)):
                cr, ci = half[:h], half[h:]
                pr, pi = probe_ref[0, k, r], probe_ref[1, k, r]
                qr, qi = patch[0, r], patch[1, r]
                grad[0, r] += pr * cr + pi * ci
                grad[1, r] += pr * ci - pi * cr
                pg_ref[0, k, r] += qr * cr + qi * ci
                pg_ref[1, k, r] += qr * ci - qi * cr
            return c

        lax.fori_loop(0, modes, backward, 0, unroll=UNROLL)
        down, across = lay(canvas_ref, spread_ref, grad, a, b)
        sums[s, 0] = down
        sums[s, 1] = across
        return carry

    lax.fori_loop(0, count_ref[0], visit, 0)
    energy = jnp.zeros((8, 128), F32)
    for s in range(slots):
        energy += sums[s, 2]
        for kind in range(2):
            shift_ref[s, kind] = jnp.sum(sums[s, kind]) * (0.5 / n)
    energy_ref[...] = jnp.broadcast_to(jnp.sum(energy, keepdims=True) / (n * n), energy.shape)


def step(pos, count, canvas, probe, amp):
    n = probe.shape[2]
    modes = probe.shape[1]
    slots = amp.shape[0]
    rows = canvas.shape[1]
    vmem = pl.BlockSpec(memory_space=pltpu.VMEM)
    smem = pl.BlockSpec(memory_space=pltpu.SMEM)
    return pl.pallas_call(
        step_kernel,
        out_shape=(
            jax.ShapeDtypeStruct((2, rows, rows), F32),
            jax.ShapeDtypeStruct(probe.shape, F32),
            jax.ShapeDtypeStruct((slots, 2), F32),
            jax.ShapeDtypeStruct((8, 128), F32),
            jax.ShapeDtypeStruct((1,), F32),
        ),
        in_specs=[smem, smem, vmem, vmem, vmem, vmem, vmem],
        out_specs=(vmem, vmem, smem, vmem, smem),
        scratch_shapes=[
            pltpu.VMEM((2, n, n), F32),
            pltpu.VMEM((modes, 2, n, n), F32),
            pltpu.VMEM((n, n), F32),
            pltpu.VMEM((2, n, n), F32),
            pltpu.VMEM((n, n // 2), F32),
            pltpu.VMEM((n, n // 2), F32),
            pltpu.VMEM((slots, 3, 8, 128), F32),
        ],
        compiler_params=pltpu.CompilerParams(vmem_limit_bytes=50 * 2**20),
    )(pos, count, canvas, probe, amp, jnp.asarray(dft_tables(n)), jnp.asarray(parity_table(n)))


MESH = pl.DeviceIdType.MESH
SIDES = [(-1, 0), (1, 0), (0, -1), (0, 1), (-1, -1), (-1, 1), (1, -1), (1, 1)]


def place():
    return lax.axis_index("row"), lax.axis_index("col")


def present(side, limits):
    row, col = place()
    fits = None
    for at, by, limit in ((row, side[0], limits[0]), (col, side[1], limits[1])):
        if by:
            ok = at > 0 if by < 0 else at < limit - 1
            fits = ok if fits is None else jnp.logical_and(fits, ok)
    return fits


def neighbour(side):
    row, col = place()
    return (row + side[0], col + side[1])


def edge(by, cells):
    return pl.ds(0, cells) if by == 0 else (pl.ds(0, HALO) if by < 0 else pl.ds(cells - HALO, HALO))


def rim(by, cells):
    return pl.ds(HALO, cells) if by == 0 else (pl.ds(0, HALO) if by < 0 else pl.ds(cells + HALO, HALO))


def greet_sides(limits):
    barrier = pltpu.get_barrier_semaphore()
    total = jnp.int32(0)
    for side in SIDES:
        here = present(side, limits)
        total += here.astype(jnp.int32)

        @pl.when(here)
        def _():
            pl.semaphore_signal(barrier, inc=1, device_id=neighbour(side), device_id_type=MESH)

    return barrier, total


def halo_kernel(limits, obj_ref, canvas_ref, zeros, own_sem, zero_sems, send_sems, recv_sems):
    cells = obj_ref.shape[1]
    barrier, total = greet_sides(limits)
    own = pltpu.make_async_copy(obj_ref, canvas_ref.at[:, pl.ds(HALO, cells), pl.ds(HALO, cells)], own_sem)
    own.start()
    zeros[...] = jnp.zeros_like(zeros)
    pl.semaphore_wait(barrier, total)
    steps = []
    for i, side in enumerate(SIDES):
        here = present(side, limits)
        back = SIDES.index((-side[0], -side[1]))
        send = pltpu.make_async_remote_copy(
            src_ref=obj_ref.at[:, edge(side[0], cells), edge(side[1], cells)],
            dst_ref=canvas_ref.at[:, rim(-side[0], cells), rim(-side[1], cells)],
            send_sem=send_sems.at[i],
            recv_sem=recv_sems.at[back],
            device_id=neighbour(side),
            device_id_type=MESH,
        )
        landed = canvas_ref.at[:, rim(side[0], cells), rim(side[1], cells)]
        tall, wide = (cells if side[0] == 0 else HALO), (cells if side[1] == 0 else HALO)
        blank = pltpu.make_async_copy(zeros.at[:, pl.ds(0, tall), pl.ds(0, wide)], landed, zero_sems.at[i])
        arrive = pltpu.make_async_copy(landed, landed, recv_sems.at[i])
        steps.append((here, send, blank, arrive))

        @pl.when(here)
        def _(send=send):
            send.start()

        @pl.when(jnp.logical_not(here))
        def _(blank=blank):
            blank.start()

    for here, send, blank, arrive in steps:
        @pl.when(here)
        def _(send=send, arrive=arrive):
            send.wait_send()
            arrive.wait()

        @pl.when(jnp.logical_not(here))
        def _(blank=blank):
            blank.wait()

    own.wait()


def exchange_halo(obj, limits):
    cells = obj.shape[1]
    return pl.pallas_call(
        functools.partial(halo_kernel, limits),
        out_shape=jax.ShapeDtypeStruct((2, cells + 2 * HALO, cells + 2 * HALO), F32),
        in_specs=[pl.BlockSpec(memory_space=pl.ANY)],
        out_specs=pl.BlockSpec(memory_space=pl.ANY),
        scratch_shapes=[
            pltpu.VMEM((2, cells, cells), F32),
            pltpu.SemaphoreType.DMA,
            pltpu.SemaphoreType.DMA((8,)),
            pltpu.SemaphoreType.DMA((8,)),
            pltpu.SemaphoreType.DMA((8,)),
        ],
        compiler_params=pltpu.CompilerParams(collective_id=0, has_side_effects=True, vmem_limit_bytes=16 * 2**20),
    )(obj)


ORDERS = [(0, 1, 2), (1, 2, 0), (2, 0, 1), (1, 0, 2)]


def spots():
    row, col = place()
    return (row // 2 % 2 * 2 + col // 4, row // 4, col % 4)


def along(axis, by):
    row, col = place()
    at = list(spots())
    at[axis] = (at[axis] + by) % 4
    return (at[1] * 4 + at[0] // 2 * 2 + row % 2, at[0] % 2 * 4 + at[2])


def finish_kernel(limits, spread_ref, pg_ref, energy_ref, obj_ref, probe_ref, illum_ref,
                  onew_ref, pnew_ref, land_rows, land_cols, land_corners, total_ref, mate_half, mate_energy, warm, heat,
                  box1, box2, box3, fold_send, fold_recv, mate_send, mate_recv, down_send, down_recv, up_send, up_recv,
                  heat_send, heat_recv):
    cells = obj_ref.shape[1]
    row, col = place()
    core = row % 2
    mate = (row + 1 - 2 * core, col)
    at = spots()
    units = len(ORDERS)
    unit = pg_ref.shape[1] // units

    barrier, total = greet_sides(limits)
    pl.semaphore_signal(barrier, inc=1, device_id=mate, device_id_type=MESH)
    for axis in range(3):
        for by in (1, 2, 3):
            pl.semaphore_signal(barrier, inc=1, device_id=along(axis, by), device_id_type=MESH)
    pl.semaphore_wait(barrier, total + 10)

    def remote(src, dst, device, send, recv):
        return pltpu.make_async_remote_copy(src_ref=src, dst_ref=dst, send_sem=send, recv_sem=recv,
                                            device_id=device, device_id_type=MESH)

    firsts = [remote(energy_ref, mate_energy, mate, mate_send.at[0], mate_recv.at[0])]
    for u in range(units):
        rows = pl.ds(u * unit, unit)
        firsts.append(remote(pg_ref.at[1 - core, rows], mate_half.at[rows], mate, mate_send.at[1 + u], mate_recv.at[1 + u]))
    for copy in firsts:
        copy.start()

    folds = []
    for i, side in enumerate(SIDES):
        here = present(side, limits)
        back = SIDES.index((-side[0], -side[1]))
        land = land_rows.at[back] if i < 2 else land_cols.at[back - 2] if i < 4 else land_corners.at[back - 4]
        send = remote(spread_ref.at[:, rim(side[0], cells), rim(side[1], cells)], land, neighbour(side),
                      fold_send.at[i], fold_recv.at[back])
        mine = land_rows.at[i] if i < 2 else land_cols.at[i - 2] if i < 4 else land_corners.at[i - 4]
        arrive = pltpu.make_async_copy(mine, mine, fold_recv.at[i])
        folds.append((here, send, arrive, side, mine))

        @pl.when(here)
        def _(send=send):
            send.start()

    def piece(u, depth, spot):
        order = ORDERS[u]
        start = u * unit
        if depth == 1:
            return pl.ds(pl.multiple_of(start + spot * (unit // 4), unit // 4), unit // 4), slice(None)
        start = start + at[order[0]] * (unit // 4)
        if depth == 2:
            return pl.ds(pl.multiple_of(start + spot * (unit // 16), unit // 16), unit // 16), slice(None)
        start = start + at[order[1]] * (unit // 16)
        return (pl.ds(pl.multiple_of(start + spot // 2 * 8, 8), 8), pl.ds(pl.multiple_of(spot % 2 * 128, 128), 128))

    def own(u, depth):
        return piece(u, depth, at[ORDERS[u][depth - 1]])

    boxes = (box1, box2, box3)
    waiting = []

    def down(u, depth):
        axis = ORDERS[u][depth - 1]
        out = []
        for by in (1, 2, 3):
            copy = remote(total_ref.at[piece(u, depth, (at[axis] + by) % 4)], boxes[depth - 1].at[u, by - 1], along(axis, by),
                          down_send.at[u, depth - 1, by - 1], down_recv.at[u, depth - 1, by - 1])
            copy.start()
            out.append(copy)
        waiting.extend(out)
        return out

    def pass_heat(axis):
        out = []
        for by in (1, 2, 3):
            copy = remote(warm.at[axis], heat.at[axis, by - 1], along(axis, by), heat_send.at[axis, by - 1], heat_recv.at[axis, by - 1])
            copy.start()
            out.append(copy)
        waiting.extend(out)
        return out

    firsts[0].wait_recv()
    warm[0] = energy_ref[...] + mate_energy[...]
    hot = pass_heat(0)
    flying = []
    for u in range(units):
        rows = pl.ds(u * unit, unit)
        firsts[1 + u].wait_recv()
        total_ref[rows, :] = pg_ref[core, rows, :] + mate_half[rows, :]
        flying.append(down(u, 1))
    waiting.extend(firsts)

    share = 1.0 / illum_ref[0]
    step_rows = 64

    def base(j, c):
        r = pl.ds(pl.multiple_of(j * step_rows, step_rows), step_rows)
        rr = pl.ds(pl.multiple_of(j * step_rows + HALO, step_rows), step_rows)
        for part in range(2):
            onew_ref[part, r, :] = obj_ref[part, r, :] + spread_ref[part, rr, HALO:HALO + cells] * share
        return c

    lax.fori_loop(0, cells // step_rows, base, 0)

    for depth in (1, 2, 3):
        for copy in hot:
            copy.wait_recv()
        fresh = warm[depth - 1] + heat[depth - 1, 0] + heat[depth - 1, 1] + heat[depth - 1, 2]
        if depth < 3:
            warm[depth] = fresh
            hot = pass_heat(depth)
        for u in range(units):
            for copy in flying[u]:
                copy.wait_recv()
            box = boxes[depth - 1]
            where = own(u, depth)
            summed = total_ref[where] + box[u, 0] + box[u, 1] + box[u, 2]
            if depth < 3:
                total_ref[where] = summed
                flying[u] = down(u, depth + 1)
            else:
                pnew_ref[(core,) + where] = probe_ref[(core,) + where] + summed / (fresh[:, :128] + EPSILON)

    def up(u, depth):
        axis = ORDERS[u][depth - 1]
        spot = pnew_ref.at[(core,) + own(u, depth)]
        out = []
        for by in (1, 2, 3):
            landed = pnew_ref.at[(core,) + piece(u, depth, (at[axis] + 4 - by) % 4)]
            copy = remote(spot, spot, along(axis, by), up_send.at[u, depth - 1, by - 1], up_recv.at[u, depth - 1, by - 1])
            copy.start()
            waiting.append(copy)
            out.append(pltpu.make_async_copy(landed, landed, up_recv.at[u, depth - 1, by - 1]))
        return out

    for u in range(units):
        flying[u] = up(u, 3)
    lasts = []
    for depth in (3, 2, 1):
        for u in range(units):
            for copy in flying[u]:
                copy.wait()
            if depth > 1:
                flying[u] = up(u, depth - 1)
            else:
                rows = pl.ds(u * unit, unit)
                done = pnew_ref.at[core, rows]
                copy = remote(done, done, mate, mate_send.at[5 + u], mate_recv.at[5 + u])
                copy.start()
                waiting.append(copy)
                got = pnew_ref.at[1 - core, rows]
                lasts.append(pltpu.make_async_copy(got, got, mate_recv.at[5 + u]))

    for here, send, arrive, side, mine in folds:
        @pl.when(here)
        def _(send=send, arrive=arrive, side=side, mine=mine):
            send.wait_send()
            arrive.wait()
            for part in range(2):
                onew_ref[part, edge(side[0], cells), edge(side[1], cells)] += mine[part] * share

    for copy in lasts:
        copy.wait()
    for copy in waiting:
        copy.wait_send()


def finish(spread, pg, energy, obj, probe, illum, limits):
    cells = obj.shape[1]
    rows, lanes = probe.shape[1], probe.shape[2]
    units = len(ORDERS)
    unit = rows // units
    vmem = pl.BlockSpec(memory_space=pltpu.VMEM)
    dma = pltpu.SemaphoreType.DMA
    return pl.pallas_call(
        functools.partial(finish_kernel, limits),
        out_shape=(jax.ShapeDtypeStruct(obj.shape, F32), jax.ShapeDtypeStruct(probe.shape, F32)),
        in_specs=[vmem, vmem, vmem, vmem, vmem, pl.BlockSpec(memory_space=pltpu.SMEM)],
        out_specs=(vmem, vmem),
        scratch_shapes=[
            pltpu.VMEM((2, 2, HALO, cells), F32),
            pltpu.VMEM((2, 2, cells, HALO), F32),
            pltpu.VMEM((4, 2, HALO, HALO), F32),
            pltpu.VMEM((rows, lanes), F32),
            pltpu.VMEM((rows, lanes), F32),
            pltpu.VMEM((8, 128), F32),
            pltpu.VMEM((3, 8, 128), F32),
            pltpu.VMEM((3, 3, 8, 128), F32),
            pltpu.VMEM((units, 3, unit // 4, lanes), F32),
            pltpu.VMEM((units, 3, unit // 16, lanes), F32),
            pltpu.VMEM((units, 3, 8, 128), F32),
            dma((8,)), dma((8,)), dma((9,)), dma((9,)),
            dma((units, 3, 3)), dma((units, 3, 3)), dma((units, 3, 3)), dma((units, 3, 3)),
            dma((3, 3)), dma((3, 3)),
        ],
        compiler_params=pltpu.CompilerParams(collective_id=1, has_side_effects=True, vmem_limit_bytes=40 * 2**20),
    )(spread, pg, energy, obj, probe, illum)


def body(limits, object_field, probe, amplitudes, positions, counts):
    canvas = exchange_halo(object_field, limits)
    spread, probe_grad, shift, energy, illum = step(positions[0, 0], counts[0], canvas, probe, amplitudes[0, 0])
    n = probe.shape[2]
    flat = (2, probe.shape[1] * n, n)
    object_new, probe_new = finish(spread, probe_grad.reshape(flat), energy, object_field, probe.reshape(flat), illum, limits)
    return (object_new, probe_new.reshape(probe.shape), shift[None, None])


def solution(mesh):
    return jax.shard_map(
        functools.partial(body, (mesh.shape["row"], mesh.shape["col"])),
        mesh=mesh,
        in_specs=(
            P(None, "row", "col"),
            P(),
            P("row", "col", None, None, None),
            P("row", "col", None, None),
            P("row", "col"),
        ),
        out_specs=(P(None, "row", "col"), P(), P("row", "col", None, None)),
        check_vma=False,
    )
```

```python
import functools
import math

import ml_dtypes
import numpy as np
import jax
import jax.numpy as jnp
from jax import lax
from jax.experimental import pallas as pl
from jax.experimental.pallas import tpu as pltpu
from jax.sharding import PartitionSpec as P

HALO = 128
INTENSITY_FLOOR = 0.1
EPSILON = 1e-06
F32 = jnp.float32
BF16 = jnp.bfloat16
UNROLL = 4


def dft_tables(pixels):
    half = pixels // 2
    k = np.arange(half)[:, None]
    n = np.arange(half)[None, :]
    out = []
    for parity in (0, 1):
        angle = (n * (2 * k + parity) % pixels) * (2.0 * math.pi / pixels)
        c = np.cos(angle) / math.sqrt(pixels)
        s = np.sin(angle) / math.sqrt(pixels)
        out.append(np.block([[c, s], [-s, c]]))
    both = []
    for m in (out[0], out[1], out[0].T, out[1].T):
        m = m.astype(np.float32)
        hi = m.astype(ml_dtypes.bfloat16)
        lo = (m - hi.astype(np.float32)).astype(ml_dtypes.bfloat16)
        both.append(np.stack([hi, lo]))
    return np.stack(both)


def parity_table(pixels):
    half = pixels // 2
    t = np.zeros((pixels, pixels), np.float32)
    for j in range(half):
        t[2 * j, j] = 1.0
        t[2 * j + 1, half + j] = 1.0
    return t.astype(ml_dtypes.bfloat16)


def split(x):
    hi = x.astype(BF16)
    return hi, (x - hi.astype(F32)).astype(BF16)


def mm(a, b):
    return jnp.dot(a, b, preferred_element_type=F32)


def from_left(table, x):
    hi, lo = split(x)
    return mm(jnp.concatenate([table[0], table[0], table[1]], 1), jnp.concatenate([hi, lo, hi], 0))


def from_right(x, table):
    hi, lo = split(x)
    return mm(jnp.concatenate([hi, lo, hi], 1), jnp.concatenate([table[0], table[0], table[1]], 0))


def lane_of():
    return lax.broadcasted_iota(jnp.int32, (1, 8, 128), 2)


def row_of():
    return lax.broadcasted_iota(jnp.int32, (1, 8, 128), 1)


def cut(canvas_ref, patch, a, b):
    n = patch.shape[1]
    groups = n // 8
    t, u = b % 128, a % 8
    row = pl.multiple_of(a - u, 8)
    lane, sub = lane_of(), row_of()
    power = jnp.zeros((8, 128), F32)
    for part in range(2):
        blocks = []
        for j in range(n // 128 + 1):
            v = canvas_ref[part, pl.ds(row, n + 8), pl.ds(pl.multiple_of(b - t + j * 128, 128), 128)]
            v = pltpu.roll(v.reshape(groups + 1, 8, 128), (8 - u) % 8, 1)
            v = jnp.where(sub < 8 - u, v[:groups], v[1:])
            blocks.append(pltpu.roll(v, (128 - t) % 128, 2))
        for j in range(n // 128):
            p = jnp.where(lane < 128 - t, blocks[j], blocks[j + 1])
            power += jnp.sum(p * p, axis=0)
            patch[part, :, j * 128:(j + 1) * 128] = p.reshape(n, 128)
    return power


def lay(canvas_ref, spread_ref, grad, a, b):
    n = grad.shape[1]
    groups = n // 8
    count = n // 128
    t, u = b % 128, a % 8
    row = pl.multiple_of(a - u, 8)
    before = pl.multiple_of(jnp.maximum(a - u - 8, 0), 8)
    lane, sub = lane_of(), row_of()
    down = jnp.zeros((8, 128), F32)
    across = jnp.zeros((8, 128), F32)
    none = jnp.zeros((1, 8, 128), F32)
    for part in range(2):
        turned = [pltpu.roll(grad[part, :, j * 128:(j + 1) * 128].reshape(groups, 8, 128), t, 2) for j in range(count)]
        strips = []
        for j in range(-1, count + 1):
            at = pl.multiple_of(jnp.maximum(b - t + j * 128, 0), 128)
            strips.append(canvas_ref[part, pl.ds(row, n + 8), pl.ds(at, 128)].reshape(groups + 1, 8, 128))
        for j in range(count + 1):
            left = turned[j - 1] if j else 0.0
            g = jnp.where(lane < t, left, turned[j] if j < count else 0.0)
            g = pltpu.roll(g, u, 1)
            g = jnp.where(sub < u, jnp.concatenate([none, g], 0), jnp.concatenate([g, none], 0))
            at = pl.ds(pl.multiple_of(b - t + j * 128, 128), 128)
            spread_ref[part, pl.ds(row, n + 8), at] += g.reshape(n + 8, 128)
            v = strips[j + 1]
            first = canvas_ref[part, pl.ds(before, 8), at].reshape(1, 8, 128)
            nxt = pltpu.roll(v, 7, 1)
            prv = pltpu.roll(jnp.concatenate([first, v], 0), 1, 1)
            nxt = jnp.where(sub < 7, nxt, jnp.concatenate([nxt[1:], none], 0))
            prv = jnp.where(sub < 1, prv[:-1], prv[1:])
            down += jnp.sum(g * (nxt - prv), axis=0)
            nxt = pltpu.roll(v, 127, 2)
            prv = pltpu.roll(v, 1, 2)
            if j < count:
                nxt = jnp.where(lane < 127, nxt, pltpu.roll(strips[j + 2], 127, 2))
            prv = jnp.where(lane < 1, pltpu.roll(strips[j], 1, 2), prv)
            across += jnp.sum(g * (nxt - prv), axis=0)
    return down, across


def step_kernel(pos_ref, count_ref, canvas_ref, probe_ref, amp_ref, tab_ref, par_ref,
                spread_ref, pg_ref, shift_ref, energy_ref, illum_ref,
                patch, far, inten, grad, col0, col1, sums):
    n = probe_ref.shape[2]
    h = n // 2
    modes = probe_ref.shape[1]
    slots = amp_ref.shape[0]
    spread_ref[...] = jnp.zeros_like(spread_ref)
    pg_ref[...] = jnp.zeros_like(pg_ref)
    sums[...] = jnp.zeros_like(sums)
    light = jnp.zeros((n, n), F32)
    for k in range(modes):
        for part in range(2):
            light += probe_ref[part, k] * probe_ref[part, k]
    illum_ref[0] = jnp.max(light)

    def visit(s, carry):
        a = pos_ref[s, 0]
        b = pos_ref[s, 1]
        sums[s, 2] = cut(canvas_ref, patch, a, b)

        inten[...] = jnp.zeros_like(inten)

        def forward(k, c):
            pr, pi = probe_ref[0, k], probe_ref[1, k]
            pr_, pi_ = patch[0], patch[1]
            er = pr * pr_ - pi * pi_
            ei = pr * pi_ + pi * pr_
            up = jnp.concatenate([er[:h] + er[h:], ei[:h] + ei[h:]], 0)
            dn = jnp.concatenate([er[:h] - er[h:], ei[:h] - ei[h:]], 0)
            su = from_left(tab_ref[0], up)
            sd = from_left(tab_ref[1], dn)
            zr = jnp.concatenate([su[:h], sd[:h]], 0)
            zi = jnp.concatenate([su[h:], sd[h:]], 0)
            lf = jnp.concatenate([zr[:, :h] + zr[:, h:], zi[:, :h] + zi[:, h:]], 1)
            rt = jnp.concatenate([zr[:, :h] - zr[:, h:], zi[:, :h] - zi[:, h:]], 1)
            fa = from_right(lf, tab_ref[2])
            fb = from_right(rt, tab_ref[3])
            far[k, 0] = fa
            far[k, 1] = fb
            inten[:, :h] += fa[:, :h] * fa[:, :h] + fa[:, h:] * fa[:, h:]
            inten[:, h:] += fb[:, :h] * fb[:, :h] + fb[:, h:] * fb[:, h:]
            return c

        lax.fori_loop(0, modes, forward, 0, unroll=UNROLL)
        hi, lo = split(amp_ref[s])
        am = mm(hi, par_ref[...]) + mm(lo, par_ref[...])
        col0[...] = am[:, :h]
        col1[...] = am[:, h:]
        am = jnp.concatenate([jnp.concatenate([col[pl.ds(p, h, 2), :] for p in range(2)], 0) for col in (col0, col1)], 1)
        inten[...] = am * lax.rsqrt(jnp.maximum(inten[...], INTENSITY_FLOOR)) - 1.0
        grad[...] = jnp.zeros_like(grad)

        def backward(k, c):
            ma, mb = inten[:, :h], inten[:, h:]
            e = from_right(far[k, 0] * jnp.concatenate([ma, ma], 1), tab_ref[0])
            o = from_right(far[k, 1] * jnp.concatenate([mb, mb], 1), tab_ref[1])
            lo = e + o
            hi = e - o
            ev = jnp.concatenate([jnp.concatenate([lo[:h, :h], hi[:h, :h]], 1),
                                  jnp.concatenate([lo[:h, h:], hi[:h, h:]], 1)], 0)
            od = jnp.concatenate([jnp.concatenate([lo[h:, :h], hi[h:, :h]], 1),
                                  jnp.concatenate([lo[h:, h:], hi[h:, h:]], 1)], 0)
            e2 = from_left(tab_ref[2], ev)
            o2 = from_left(tab_ref[3], od)
            for r, half in ((slice(0, h), e2 + o2), (slice(h, n), e2 - o2)):
                cr, ci = half[:h], half[h:]
                pr, pi = probe_ref[0, k, r], probe_ref[1, k, r]
                qr, qi = patch[0, r], patch[1, r]
                grad[0, r] += pr * cr + pi * ci
                grad[1, r] += pr * ci - pi * cr
                pg_ref[0, k, r] += qr * cr + qi * ci
                pg_ref[1, k, r] += qr * ci - qi * cr
            return c

        lax.fori_loop(0, modes, backward, 0, unroll=UNROLL)
        down, across = lay(canvas_ref, spread_ref, grad, a, b)
        sums[s, 0] = down
        sums[s, 1] = across
        return carry

    lax.fori_loop(0, count_ref[0], visit, 0)
    energy = jnp.zeros((8, 128), F32)
    for s in range(slots):
        energy += sums[s, 2]
        for kind in range(2):
            shift_ref[s, kind] = jnp.sum(sums[s, kind]) * (0.5 / n)
    energy_ref[...] = jnp.broadcast_to(jnp.sum(energy, keepdims=True) / (n * n), energy.shape)


def step(pos, count, canvas, probe, amp):
    n = probe.shape[2]
    modes = probe.shape[1]
    slots = amp.shape[0]
    rows = canvas.shape[1]
    vmem = pl.BlockSpec(memory_space=pltpu.VMEM)
    smem = pl.BlockSpec(memory_space=pltpu.SMEM)
    return pl.pallas_call(
        step_kernel,
        out_shape=(
            jax.ShapeDtypeStruct((2, rows, rows), F32),
            jax.ShapeDtypeStruct(probe.shape, F32),
            jax.ShapeDtypeStruct((slots, 2), F32),
            jax.ShapeDtypeStruct((8, 128), F32),
            jax.ShapeDtypeStruct((1,), F32),
        ),
        in_specs=[smem, smem, vmem, vmem, vmem, vmem, vmem],
        out_specs=(vmem, vmem, smem, vmem, smem),
        scratch_shapes=[
            pltpu.VMEM((2, n, n), F32),
            pltpu.VMEM((modes, 2, n, n), F32),
            pltpu.VMEM((n, n), F32),
            pltpu.VMEM((2, n, n), F32),
            pltpu.VMEM((n, n // 2), F32),
            pltpu.VMEM((n, n // 2), F32),
            pltpu.VMEM((slots, 3, 8, 128), F32),
        ],
        compiler_params=pltpu.CompilerParams(vmem_limit_bytes=50 * 2**20),
    )(pos, count, canvas, probe, amp, jnp.asarray(dft_tables(n)), jnp.asarray(parity_table(n)))


MESH = pl.DeviceIdType.MESH


def place():
    return lax.axis_index("row"), lax.axis_index("col")


def remote(src, dst, device, send, recv):
    return pltpu.make_async_remote_copy(src_ref=src, dst_ref=dst, send_sem=send, recv_sem=recv,
                                        device_id=device, device_id_type=MESH)


def landed(ref, sem):
    return pltpu.make_async_copy(ref, ref, sem)


def roles(limits):
    row, col = place()
    rows, cols = limits
    core = row % 2
    seam = cols // 2
    up, down = row > 0, row < rows - 1
    outer = jnp.where(core == 0, row - 1, row + 1)
    has_outer = jnp.logical_and(outer >= 0, outer < rows)
    near = {-1: jnp.logical_and(col > 0, col != seam), 1: jnp.logical_and(col < cols - 1, col != seam - 1)}
    at_seam = {-1: col == seam, 1: col == seam - 1}
    has = {-1: col > 0, 1: col < cols - 1}
    relay = {0: col == cols - 1, 1: col == 0}
    return dict(row=row, col=col, core=core, mate=(row + 1 - 2 * core, col), outer=(outer, col), has_outer=has_outer,
                near=near, at_seam=at_seam, has=has, relay=relay, seam=seam, cols=cols)


def greet(r):
    barrier = pltpu.get_barrier_semaphore()
    row, col, cols, seam = r["row"], r["col"], r["cols"], r["seam"]
    seam_any = jnp.logical_or(r["at_seam"][-1], r["at_seam"][1])
    relay_any = jnp.logical_or(r["relay"][0], r["relay"][1])
    pl.semaphore_signal(barrier, inc=1, device_id=r["mate"], device_id_type=MESH)
    total = jnp.int32(1)

    def to(cond, device):
        @pl.when(cond)
        def _():
            pl.semaphore_signal(barrier, inc=1, device_id=device, device_id_type=MESH)

        return cond.astype(jnp.int32)

    total += to(r["has_outer"], r["outer"])
    for dc in (-1, 1):
        total += to(r["has"][dc], (row, col + dc))
    for target in (0, cols - 1):
        total += to(seam_any, (row, target))
    for target in (seam - 1, seam):
        total += to(relay_any, (row, target))
    return barrier, total


def when(cond, *actions):
    @pl.when(cond)
    def _():
        for action in actions:
            action()


def halo_kernel(limits, obj_ref, canvas_ref, zeros, passing, own_sem, zero_sems, row_send, row_recv, col_send, col_recv,
                seam_send, seam_recv, pass_send, pass_recv, corner_send, corner_recv):
    cells = obj_ref.shape[1]
    half = cells // 2
    r = roles(limits)
    row, col, core, seam, cols = r["row"], r["col"], r["core"], r["seam"], r["cols"]
    barrier, total = greet(r)
    own = pltpu.make_async_copy(obj_ref, canvas_ref.at[:, pl.ds(HALO, cells), pl.ds(HALO, cells)], own_sem)
    own.start()
    zeros[...] = jnp.zeros_like(zeros)
    pl.semaphore_wait(barrier, total)

    outer_from = pl.multiple_of(jnp.where(core == 0, 0, cells - HALO), HALO)
    inner_from = pl.multiple_of(jnp.where(core == 0, cells - HALO, 0), HALO)
    outer_at = pl.multiple_of(jnp.where(core == 0, 0, cells + HALO), HALO)
    inner_at = pl.multiple_of(jnp.where(core == 0, cells + HALO, 0), HALO)
    strips = ((0, HALO), (cells - HALO, HALO), (HALO, cells - 2 * HALO))
    edge_from = {-1: 0, 1: cells - HALO}
    rim_at = {-1: 0, 1: cells + HALO}
    side = {-1: 0, 1: 1}

    def canvas(top, tall, left, wide):
        return canvas_ref.at[:, pl.ds(top, tall), pl.ds(left, wide)]

    def tile(top, tall, left, wide):
        return obj_ref.at[:, pl.ds(top, tall), pl.ds(left, wide)]

    edges = {}
    seams = {}
    for dc in (-1, 1):
        edges[dc] = remote(tile(0, cells, edge_from[dc], HALO), canvas(HALO, cells, rim_at[-dc], HALO), (row, col + dc),
                           col_send.at[side[dc]], col_recv.at[side[-dc]])
        when(r["near"][dc], edges[dc].start)
        pair = []
        for part, target in ((0, cols - 1), (1, 0)):
            pair.append(remote(tile(part * half, half, edge_from[dc], HALO), passing.at[side[dc]], (row, target),
                               seam_send.at[part], seam_recv.at[side[dc]]))
        seams[dc] = pair
        when(r["at_seam"][dc], pair[0].start, pair[1].start)

    inner = remote(tile(inner_from, HALO, 0, cells), canvas(outer_at_of_mate(inner_at, cells), HALO, HALO, cells), r["mate"],
                   row_send.at[3], row_recv.at[3])
    inner.start()
    outers = []
    for i, (left, wide) in enumerate(strips):
        copy = remote(tile(outer_from, HALO, left, wide), canvas(outer_at_of_mate(outer_at, cells), HALO, HALO + left, wide), r["outer"],
                      row_send.at[i], row_recv.at[i])
        outers.append(copy)
        when(r["has_outer"], copy.start)
    blanks = []
    for i, (cond, ref) in enumerate((
        (jnp.logical_not(r["has_outer"]), canvas(outer_at, HALO, 0, cells + 2 * HALO)),
        (jnp.logical_not(r["has"][-1]), canvas(HALO, cells, 0, HALO)),
        (jnp.logical_not(r["has"][1]), canvas(HALO, cells, cells + HALO, HALO)),
    )):
        source = zeros.at[:, pl.ds(0, HALO), :] if i == 0 else zeros.at[:, pl.ds(0, cells), pl.ds(0, HALO)]
        copy = pltpu.make_async_copy(source, ref, zero_sems.at[i])
        blanks.append((cond, copy))
        when(cond, copy.start)
    for dc in (-1, 1):
        for k, top in ((0, inner_at), (1, outer_at)):
            need = jnp.logical_not(r["has"][dc])
            if k:
                need = jnp.logical_and(need, r["has_outer"])
            copy = pltpu.make_async_copy(zeros.at[:, pl.ds(0, HALO), pl.ds(0, HALO)], canvas(top, HALO, rim_at[dc], HALO),
                                         zero_sems.at[3 + 2 * side[dc] + k])
            blanks.append((need, copy))
            when(need, copy.start)

    def forward(part, dc):
        target = seam if dc == 1 else seam - 1
        return remote(passing.at[side[dc]], canvas(HALO + part * half, half, rim_at[-dc], HALO), (row, target),
                      pass_send.at[side[dc]], pass_recv.at[part])

    def relay(part, dc):
        when(r["relay"][part], landed(passing.at[side[dc]], seam_recv.at[side[dc]]).wait, forward(part, dc).start)

    relay(0, -1)
    relay(1, 1)
    corners = {}
    for dc in (-1, 1):
        i = side[dc]
        strip = canvas(outer_at, HALO, HALO + edge_from[dc], HALO)
        give = jnp.logical_and(r["has_outer"], r["has"][dc])
        corners[dc] = (give, remote(strip, canvas(outer_at, HALO, rim_at[-dc], HALO), (row, col + dc),
                                    corner_send.at[i], corner_recv.at[1 - i]))
        when(r["has_outer"], landed(strip, row_recv.at[i]).wait)
        when(give, corners[dc][1].start)
    relay(0, 1)
    relay(1, -1)
    inside = {}
    for dc in (-1, 1):
        i = side[dc]
        near_mate = pl.multiple_of(inner_from + HALO, HALO)
        when(r["near"][dc], landed(canvas(HALO, cells, rim_at[dc], HALO), col_recv.at[i]).wait)
        for part in range(2):
            when(r["at_seam"][dc], landed(canvas(HALO + part * half, half, rim_at[dc], HALO), pass_recv.at[part]).wait)
        inside[dc] = remote(canvas(near_mate, HALO, rim_at[dc], HALO), canvas(outer_at_of_mate(inner_at, cells), HALO, rim_at[dc], HALO),
                            r["mate"], corner_send.at[2 + i], corner_recv.at[2 + i])
        when(r["has"][dc], inside[dc].start)

    inner.wait_send()
    landed(canvas(inner_at, HALO, HALO, cells), row_recv.at[3]).wait()
    when(r["has_outer"], *[copy.wait_send for copy in outers])
    when(r["has_outer"], landed(canvas(outer_at, HALO, HALO + strips[2][0], strips[2][1]), row_recv.at[2]).wait)
    for dc in (-1, 1):
        i = side[dc]
        when(r["near"][dc], edges[dc].wait_send)
        when(r["at_seam"][dc], seams[dc][0].wait_send, seams[dc][1].wait_send)
        for part in range(2):
            when(r["relay"][part], forward(part, dc).wait_send)
        when(corners[dc][0], corners[dc][1].wait_send, landed(canvas(outer_at, HALO, rim_at[dc], HALO), corner_recv.at[i]).wait)
        when(r["has"][dc], inside[dc].wait_send, landed(canvas(inner_at, HALO, rim_at[dc], HALO), corner_recv.at[2 + i]).wait)
    for cond, copy in blanks:
        when(cond, copy.wait)
    own.wait()


def outer_at_of_mate(at, cells):
    return pl.multiple_of(cells + HALO - at, HALO)


def exchange_halo(obj, limits):
    cells = obj.shape[1]
    dma = pltpu.SemaphoreType.DMA
    return pl.pallas_call(
        functools.partial(halo_kernel, limits),
        out_shape=jax.ShapeDtypeStruct((2, cells + 2 * HALO, cells + 2 * HALO), F32),
        in_specs=[pl.BlockSpec(memory_space=pl.ANY)],
        out_specs=pl.BlockSpec(memory_space=pl.ANY),
        scratch_shapes=[
            pltpu.VMEM((2, cells, cells + 2 * HALO), F32),
            pltpu.VMEM((2, 2, cells // 2, HALO), F32),
            dma, dma((7,)), dma((4,)), dma((4,)), dma((2,)), dma((2,)), dma((2,)), dma((2,)), dma((2,)), dma((2,)),
            dma((4,)), dma((4,)),
        ],
        compiler_params=pltpu.CompilerParams(collective_id=0, has_side_effects=True, vmem_limit_bytes=16 * 2**20),
    )(obj)


SIDES = [(-1, 0), (1, 0), (0, -1), (0, 1), (-1, -1), (-1, 1), (1, -1), (1, 1)]


def present(side, limits):
    row, col = place()
    fits = None
    for at, by, limit in ((row, side[0], limits[0]), (col, side[1], limits[1])):
        if by:
            ok = at > 0 if by < 0 else at < limit - 1
            fits = ok if fits is None else jnp.logical_and(fits, ok)
    return fits


def neighbour(side):
    row, col = place()
    return (row + side[0], col + side[1])


def edge(by, cells):
    return pl.ds(0, cells) if by == 0 else (pl.ds(0, HALO) if by < 0 else pl.ds(cells - HALO, HALO))


def rim(by, cells):
    return pl.ds(HALO, cells) if by == 0 else (pl.ds(0, HALO) if by < 0 else pl.ds(cells + HALO, HALO))


def greet_sides(limits):
    barrier = pltpu.get_barrier_semaphore()
    total = jnp.int32(0)
    for side in SIDES:
        here = present(side, limits)
        total += here.astype(jnp.int32)

        @pl.when(here)
        def _():
            pl.semaphore_signal(barrier, inc=1, device_id=neighbour(side), device_id_type=MESH)

    return barrier, total


ORDERS = [(0, 1, 2), (1, 2, 0), (2, 0, 1), (1, 0, 2)]


def spots():
    row, col = place()
    return (row // 2 % 2 * 2 + col // 4, row // 4, col % 4)


def along(axis, by):
    row, col = place()
    at = list(spots())
    at[axis] = (at[axis] + by) % 4
    return (at[1] * 4 + at[0] // 2 * 2 + row % 2, at[0] % 2 * 4 + at[2])


def finish_kernel(limits, spread_ref, pg_ref, energy_ref, obj_ref, probe_ref, illum_ref,
                  onew_ref, pnew_ref, land_rows, land_cols, land_corners, total_ref, mate_half, mate_energy, warm, heat,
                  box1, box2, box3, fold_send, fold_recv, mate_send, mate_recv, down_send, down_recv, up_send, up_recv,
                  heat_send, heat_recv):
    cells = obj_ref.shape[1]
    row, col = place()
    core = row % 2
    mate = (row + 1 - 2 * core, col)
    at = spots()
    units = len(ORDERS)
    unit = pg_ref.shape[1] // units

    barrier, total = greet_sides(limits)
    pl.semaphore_signal(barrier, inc=1, device_id=mate, device_id_type=MESH)
    for axis in range(3):
        for by in (1, 2, 3):
            pl.semaphore_signal(barrier, inc=1, device_id=along(axis, by), device_id_type=MESH)
    pl.semaphore_wait(barrier, total + 10)

    def remote(src, dst, device, send, recv):
        return pltpu.make_async_remote_copy(src_ref=src, dst_ref=dst, send_sem=send, recv_sem=recv,
                                            device_id=device, device_id_type=MESH)

    firsts = [remote(energy_ref, mate_energy, mate, mate_send.at[0], mate_recv.at[0])]
    for u in range(units):
        rows = pl.ds(u * unit, unit)
        firsts.append(remote(pg_ref.at[1 - core, rows], mate_half.at[rows], mate, mate_send.at[1 + u], mate_recv.at[1 + u]))
    for copy in firsts:
        copy.start()

    folds = []
    for i, side in enumerate(SIDES):
        here = present(side, limits)
        back = SIDES.index((-side[0], -side[1]))
        land = land_rows.at[back] if i < 2 else land_cols.at[back - 2] if i < 4 else land_corners.at[back - 4]
        send = remote(spread_ref.at[:, rim(side[0], cells), rim(side[1], cells)], land, neighbour(side),
                      fold_send.at[i], fold_recv.at[back])
        mine = land_rows.at[i] if i < 2 else land_cols.at[i - 2] if i < 4 else land_corners.at[i - 4]
        arrive = pltpu.make_async_copy(mine, mine, fold_recv.at[i])
        folds.append((here, send, arrive, side, mine))

        @pl.when(here)
        def _(send=send):
            send.start()

    def piece(u, depth, spot):
        order = ORDERS[u]
        start = u * unit
        if depth == 1:
            return pl.ds(pl.multiple_of(start + spot * (unit // 4), unit // 4), unit // 4), slice(None)
        start = start + at[order[0]] * (unit // 4)
        if depth == 2:
            return pl.ds(pl.multiple_of(start + spot * (unit // 16), unit // 16), unit // 16), slice(None)
        start = start + at[order[1]] * (unit // 16)
        return (pl.ds(pl.multiple_of(start + spot // 2 * 8, 8), 8), pl.ds(pl.multiple_of(spot % 2 * 128, 128), 128))

    def own(u, depth):
        return piece(u, depth, at[ORDERS[u][depth - 1]])

    boxes = (box1, box2, box3)
    waiting = []

    def down(u, depth):
        axis = ORDERS[u][depth - 1]
        out = []
        for by in (1, 2, 3):
            copy = remote(total_ref.at[piece(u, depth, (at[axis] + by) % 4)], boxes[depth - 1].at[u, by - 1], along(axis, by),
                          down_send.at[u, depth - 1, by - 1], down_recv.at[u, depth - 1, by - 1])
            copy.start()
            out.append(copy)
        waiting.extend(out)
        return out

    def pass_heat(axis):
        out = []
        for by in (1, 2, 3):
            copy = remote(warm.at[axis], heat.at[axis, by - 1], along(axis, by), heat_send.at[axis, by - 1], heat_recv.at[axis, by - 1])
            copy.start()
            out.append(copy)
        waiting.extend(out)
        return out

    firsts[0].wait_recv()
    warm[0] = energy_ref[...] + mate_energy[...]
    hot = pass_heat(0)
    flying = []
    for u in range(units):
        rows = pl.ds(u * unit, unit)
        firsts[1 + u].wait_recv()
        total_ref[rows, :] = pg_ref[core, rows, :] + mate_half[rows, :]
        flying.append(down(u, 1))
    waiting.extend(firsts)

    share = 1.0 / illum_ref[0]
    step_rows = 64

    def base(j, c):
        r = pl.ds(pl.multiple_of(j * step_rows, step_rows), step_rows)
        rr = pl.ds(pl.multiple_of(j * step_rows + HALO, step_rows), step_rows)
        for part in range(2):
            onew_ref[part, r, :] = obj_ref[part, r, :] + spread_ref[part, rr, HALO:HALO + cells] * share
        return c

    lax.fori_loop(0, cells // step_rows, base, 0)

    for depth in (1, 2, 3):
        for copy in hot:
            copy.wait_recv()
        fresh = warm[depth - 1] + heat[depth - 1, 0] + heat[depth - 1, 1] + heat[depth - 1, 2]
        if depth < 3:
            warm[depth] = fresh
            hot = pass_heat(depth)
        for u in range(units):
            for copy in flying[u]:
                copy.wait_recv()
            box = boxes[depth - 1]
            where = own(u, depth)
            summed = total_ref[where] + box[u, 0] + box[u, 1] + box[u, 2]
            if depth < 3:
                total_ref[where] = summed
                flying[u] = down(u, depth + 1)
            else:
                pnew_ref[(core,) + where] = probe_ref[(core,) + where] + summed / (fresh[:, :128] + EPSILON)

    def up(u, depth):
        axis = ORDERS[u][depth - 1]
        spot = pnew_ref.at[(core,) + own(u, depth)]
        out = []
        for by in (1, 2, 3):
            landed = pnew_ref.at[(core,) + piece(u, depth, (at[axis] + 4 - by) % 4)]
            copy = remote(spot, spot, along(axis, by), up_send.at[u, depth - 1, by - 1], up_recv.at[u, depth - 1, by - 1])
            copy.start()
            waiting.append(copy)
            out.append(pltpu.make_async_copy(landed, landed, up_recv.at[u, depth - 1, by - 1]))
        return out

    for u in range(units):
        flying[u] = up(u, 3)
    lasts = []
    for depth in (3, 2, 1):
        for u in range(units):
            for copy in flying[u]:
                copy.wait()
            if depth > 1:
                flying[u] = up(u, depth - 1)
            else:
                rows = pl.ds(u * unit, unit)
                done = pnew_ref.at[core, rows]
                copy = remote(done, done, mate, mate_send.at[5 + u], mate_recv.at[5 + u])
                copy.start()
                waiting.append(copy)
                got = pnew_ref.at[1 - core, rows]
                lasts.append(pltpu.make_async_copy(got, got, mate_recv.at[5 + u]))

    for here, send, arrive, side, mine in folds:
        @pl.when(here)
        def _(send=send, arrive=arrive, side=side, mine=mine):
            send.wait_send()
            arrive.wait()
            for part in range(2):
                onew_ref[part, edge(side[0], cells), edge(side[1], cells)] += mine[part] * share

    for copy in lasts:
        copy.wait()
    for copy in waiting:
        copy.wait_send()


def finish(spread, pg, energy, obj, probe, illum, limits):
    cells = obj.shape[1]
    rows, lanes = probe.shape[1], probe.shape[2]
    units = len(ORDERS)
    unit = rows // units
    vmem = pl.BlockSpec(memory_space=pltpu.VMEM)
    dma = pltpu.SemaphoreType.DMA
    return pl.pallas_call(
        functools.partial(finish_kernel, limits),
        out_shape=(jax.ShapeDtypeStruct(obj.shape, F32), jax.ShapeDtypeStruct(probe.shape, F32)),
        in_specs=[vmem, vmem, vmem, vmem, vmem, pl.BlockSpec(memory_space=pltpu.SMEM)],
        out_specs=(vmem, vmem),
        scratch_shapes=[
            pltpu.VMEM((2, 2, HALO, cells), F32),
            pltpu.VMEM((2, 2, cells, HALO), F32),
            pltpu.VMEM((4, 2, HALO, HALO), F32),
            pltpu.VMEM((rows, lanes), F32),
            pltpu.VMEM((rows, lanes), F32),
            pltpu.VMEM((8, 128), F32),
            pltpu.VMEM((3, 8, 128), F32),
            pltpu.VMEM((3, 3, 8, 128), F32),
            pltpu.VMEM((units, 3, unit // 4, lanes), F32),
            pltpu.VMEM((units, 3, unit // 16, lanes), F32),
            pltpu.VMEM((units, 3, 8, 128), F32),
            dma((8,)), dma((8,)), dma((9,)), dma((9,)),
            dma((units, 3, 3)), dma((units, 3, 3)), dma((units, 3, 3)), dma((units, 3, 3)),
            dma((3, 3)), dma((3, 3)),
        ],
        compiler_params=pltpu.CompilerParams(collective_id=1, has_side_effects=True, vmem_limit_bytes=40 * 2**20),
    )(spread, pg, energy, obj, probe, illum)


def body(limits, object_field, probe, amplitudes, positions, counts):
    canvas = exchange_halo(object_field, limits)
    spread, probe_grad, shift, energy, illum = step(positions[0, 0], counts[0], canvas, probe, amplitudes[0, 0])
    n = probe.shape[2]
    flat = (2, probe.shape[1] * n, n)
    object_new, probe_new = finish(spread, probe_grad.reshape(flat), energy, object_field, probe.reshape(flat), illum, limits)
    return (object_new, probe_new.reshape(probe.shape), shift[None, None])


def solution(mesh):
    return jax.shard_map(
        functools.partial(body, (mesh.shape["row"], mesh.shape["col"])),
        mesh=mesh,
        in_specs=(
            P(None, "row", "col"),
            P(),
            P("row", "col", None, None, None),
            P("row", "col", None, None),
            P("row", "col"),
        ),
        out_specs=(P(None, "row", "col"), P(), P("row", "col", None, None)),
        check_vma=False,
    )
```

```python
import functools
import math

import ml_dtypes
import numpy as np
import jax
import jax.numpy as jnp
from jax import lax
from jax.experimental import pallas as pl
from jax.experimental.pallas import tpu as pltpu
from jax.sharding import PartitionSpec as P

HALO = 128
INTENSITY_FLOOR = 0.1
EPSILON = 1e-06
F32 = jnp.float32
BF16 = jnp.bfloat16
UNROLL = 4


def dft_tables(pixels):
    half = pixels // 2
    k = np.arange(half)[:, None]
    n = np.arange(half)[None, :]
    out = []
    for parity in (0, 1):
        angle = (n * (2 * k + parity) % pixels) * (2.0 * math.pi / pixels)
        c = np.cos(angle) / math.sqrt(pixels)
        s = np.sin(angle) / math.sqrt(pixels)
        out.append(np.block([[c, s], [-s, c]]))
    both = []
    for m in (out[0], out[1], out[0].T, out[1].T):
        m = m.astype(np.float32)
        hi = m.astype(ml_dtypes.bfloat16)
        lo = (m - hi.astype(np.float32)).astype(ml_dtypes.bfloat16)
        both.append(np.stack([hi, lo]))
    return np.stack(both)


def parity_table(pixels):
    half = pixels // 2
    t = np.zeros((pixels, pixels), np.float32)
    for j in range(half):
        t[2 * j, j] = 1.0
        t[2 * j + 1, half + j] = 1.0
    return t.astype(ml_dtypes.bfloat16)


def split(x):
    hi = x.astype(BF16)
    return hi, (x - hi.astype(F32)).astype(BF16)


def mm(a, b):
    return jnp.dot(a, b, preferred_element_type=F32)


def from_left(table, x):
    hi, lo = split(x)
    return mm(jnp.concatenate([table[0], table[0], table[1]], 1), jnp.concatenate([hi, lo, hi], 0))


def from_right(x, table):
    hi, lo = split(x)
    return mm(jnp.concatenate([hi, lo, hi], 1), jnp.concatenate([table[0], table[0], table[1]], 0))


def lane_of():
    return lax.broadcasted_iota(jnp.int32, (1, 8, 128), 2)


def row_of():
    return lax.broadcasted_iota(jnp.int32, (1, 8, 128), 1)


def cut(canvas_ref, patch, a, b):
    n = patch.shape[1]
    groups = n // 8
    t, u = b % 128, a % 8
    row = pl.multiple_of(a - u, 8)
    lane, sub = lane_of(), row_of()
    power = jnp.zeros((8, 128), F32)
    for part in range(2):
        blocks = []
        for j in range(n // 128 + 1):
            v = canvas_ref[part, pl.ds(row, n + 8), pl.ds(pl.multiple_of(b - t + j * 128, 128), 128)]
            v = pltpu.roll(v.reshape(groups + 1, 8, 128), (8 - u) % 8, 1)
            v = jnp.where(sub < 8 - u, v[:groups], v[1:])
            blocks.append(pltpu.roll(v, (128 - t) % 128, 2))
        for j in range(n // 128):
            p = jnp.where(lane < 128 - t, blocks[j], blocks[j + 1])
            power += jnp.sum(p * p, axis=0)
            patch[part, :, j * 128:(j + 1) * 128] = p.reshape(n, 128)
    return power


def lay(canvas_ref, spread_ref, grad, a, b):
    n = grad.shape[1]
    groups = n // 8
    count = n // 128
    t, u = b % 128, a % 8
    row = pl.multiple_of(a - u, 8)
    before = pl.multiple_of(jnp.maximum(a - u - 8, 0), 8)
    lane, sub = lane_of(), row_of()
    down = jnp.zeros((8, 128), F32)
    across = jnp.zeros((8, 128), F32)
    none = jnp.zeros((1, 8, 128), F32)
    for part in range(2):
        turned = [pltpu.roll(grad[part, :, j * 128:(j + 1) * 128].reshape(groups, 8, 128), t, 2) for j in range(count)]
        strips = []
        for j in range(-1, count + 1):
            at = pl.multiple_of(jnp.maximum(b - t + j * 128, 0), 128)
            strips.append(canvas_ref[part, pl.ds(row, n + 8), pl.ds(at, 128)].reshape(groups + 1, 8, 128))
        for j in range(count + 1):
            left = turned[j - 1] if j else 0.0
            g = jnp.where(lane < t, left, turned[j] if j < count else 0.0)
            g = pltpu.roll(g, u, 1)
            g = jnp.where(sub < u, jnp.concatenate([none, g], 0), jnp.concatenate([g, none], 0))
            at = pl.ds(pl.multiple_of(b - t + j * 128, 128), 128)
            spread_ref[part, pl.ds(row, n + 8), at] += g.reshape(n + 8, 128)
            v = strips[j + 1]
            first = canvas_ref[part, pl.ds(before, 8), at].reshape(1, 8, 128)
            nxt = pltpu.roll(v, 7, 1)
            prv = pltpu.roll(jnp.concatenate([first, v], 0), 1, 1)
            nxt = jnp.where(sub < 7, nxt, jnp.concatenate([nxt[1:], none], 0))
            prv = jnp.where(sub < 1, prv[:-1], prv[1:])
            down += jnp.sum(g * (nxt - prv), axis=0)
            nxt = pltpu.roll(v, 127, 2)
            prv = pltpu.roll(v, 1, 2)
            if j < count:
                nxt = jnp.where(lane < 127, nxt, pltpu.roll(strips[j + 2], 127, 2))
            prv = jnp.where(lane < 1, pltpu.roll(strips[j], 1, 2), prv)
            across += jnp.sum(g * (nxt - prv), axis=0)
    return down, across


def step_kernel(pos_ref, count_ref, canvas_ref, probe_ref, amp_ref, tab_ref, par_ref,
                spread_ref, pg_ref, shift_ref, energy_ref, illum_ref,
                patch, far, inten, grad, col0, col1, sums):
    n = probe_ref.shape[2]
    h = n // 2
    modes = probe_ref.shape[1]
    slots = amp_ref.shape[0]
    spread_ref[...] = jnp.zeros_like(spread_ref)
    pg_ref[...] = jnp.zeros_like(pg_ref)
    sums[...] = jnp.zeros_like(sums)
    light = jnp.zeros((n, n), F32)
    for k in range(modes):
        for part in range(2):
            light += probe_ref[part, k] * probe_ref[part, k]
    illum_ref[0] = jnp.max(light)

    def visit(s, carry):
        a = pos_ref[s, 0]
        b = pos_ref[s, 1]
        sums[s, 2] = cut(canvas_ref, patch, a, b)

        inten[...] = jnp.zeros_like(inten)

        def forward(k, c):
            pr, pi = probe_ref[0, k], probe_ref[1, k]
            pr_, pi_ = patch[0], patch[1]
            er = pr * pr_ - pi * pi_
            ei = pr * pi_ + pi * pr_
            up = jnp.concatenate([er[:h] + er[h:], ei[:h] + ei[h:]], 0)
            dn = jnp.concatenate([er[:h] - er[h:], ei[:h] - ei[h:]], 0)
            su = from_left(tab_ref[0], up)
            sd = from_left(tab_ref[1], dn)
            zr = jnp.concatenate([su[:h], sd[:h]], 0)
            zi = jnp.concatenate([su[h:], sd[h:]], 0)
            lf = jnp.concatenate([zr[:, :h] + zr[:, h:], zi[:, :h] + zi[:, h:]], 1)
            rt = jnp.concatenate([zr[:, :h] - zr[:, h:], zi[:, :h] - zi[:, h:]], 1)
            fa = from_right(lf, tab_ref[2])
            fb = from_right(rt, tab_ref[3])
            far[k, 0] = fa
            far[k, 1] = fb
            inten[:, :h] += fa[:, :h] * fa[:, :h] + fa[:, h:] * fa[:, h:]
            inten[:, h:] += fb[:, :h] * fb[:, :h] + fb[:, h:] * fb[:, h:]
            return c

        lax.fori_loop(0, modes, forward, 0, unroll=UNROLL)
        hi, lo = split(amp_ref[s])
        am = mm(hi, par_ref[...]) + mm(lo, par_ref[...])
        col0[...] = am[:, :h]
        col1[...] = am[:, h:]
        am = jnp.concatenate([jnp.concatenate([col[pl.ds(p, h, 2), :] for p in range(2)], 0) for col in (col0, col1)], 1)
        inten[...] = am * lax.rsqrt(jnp.maximum(inten[...], INTENSITY_FLOOR)) - 1.0
        grad[...] = jnp.zeros_like(grad)

        def backward(k, c):
            ma, mb = inten[:, :h], inten[:, h:]
            e = from_right(far[k, 0] * jnp.concatenate([ma, ma], 1), tab_ref[0])
            o = from_right(far[k, 1] * jnp.concatenate([mb, mb], 1), tab_ref[1])
            lo = e + o
            hi = e - o
            ev = jnp.concatenate([jnp.concatenate([lo[:h, :h], hi[:h, :h]], 1),
                                  jnp.concatenate([lo[:h, h:], hi[:h, h:]], 1)], 0)
            od = jnp.concatenate([jnp.concatenate([lo[h:, :h], hi[h:, :h]], 1),
                                  jnp.concatenate([lo[h:, h:], hi[h:, h:]], 1)], 0)
            e2 = from_left(tab_ref[2], ev)
            o2 = from_left(tab_ref[3], od)
            for r, half in ((slice(0, h), e2 + o2), (slice(h, n), e2 - o2)):
                cr, ci = half[:h], half[h:]
                pr, pi = probe_ref[0, k, r], probe_ref[1, k, r]
                qr, qi = patch[0, r], patch[1, r]
                grad[0, r] += pr * cr + pi * ci
                grad[1, r] += pr * ci - pi * cr
                pg_ref[0, k, r] += qr * cr + qi * ci
                pg_ref[1, k, r] += qr * ci - qi * cr
            return c

        lax.fori_loop(0, modes, backward, 0, unroll=UNROLL)
        down, across = lay(canvas_ref, spread_ref, grad, a, b)
        sums[s, 0] = down
        sums[s, 1] = across
        return carry

    lax.fori_loop(0, count_ref[0], visit, 0)
    energy = jnp.zeros((8, 128), F32)
    for s in range(slots):
        energy += sums[s, 2]
        for kind in range(2):
            shift_ref[s, kind] = jnp.sum(sums[s, kind]) * (0.5 / n)
    energy_ref[...] = jnp.broadcast_to(jnp.sum(energy, keepdims=True) / (n * n), energy.shape)


def step(pos, count, canvas, probe, amp):
    n = probe.shape[2]
    modes = probe.shape[1]
    slots = amp.shape[0]
    rows = canvas.shape[1]
    vmem = pl.BlockSpec(memory_space=pltpu.VMEM)
    smem = pl.BlockSpec(memory_space=pltpu.SMEM)
    return pl.pallas_call(
        step_kernel,
        out_shape=(
            jax.ShapeDtypeStruct((2, rows, rows), F32),
            jax.ShapeDtypeStruct(probe.shape, F32),
            jax.ShapeDtypeStruct((slots, 2), F32),
            jax.ShapeDtypeStruct((8, 128), F32),
            jax.ShapeDtypeStruct((1,), F32),
        ),
        in_specs=[smem, smem, vmem, vmem, vmem, vmem, vmem],
        out_specs=(vmem, vmem, smem, vmem, smem),
        scratch_shapes=[
            pltpu.VMEM((2, n, n), F32),
            pltpu.VMEM((modes, 2, n, n), F32),
            pltpu.VMEM((n, n), F32),
            pltpu.VMEM((2, n, n), F32),
            pltpu.VMEM((n, n // 2), F32),
            pltpu.VMEM((n, n // 2), F32),
            pltpu.VMEM((slots, 3, 8, 128), F32),
        ],
        compiler_params=pltpu.CompilerParams(vmem_limit_bytes=50 * 2**20),
    )(pos, count, canvas, probe, amp, jnp.asarray(dft_tables(n)), jnp.asarray(parity_table(n)))


MESH = pl.DeviceIdType.MESH


def place():
    return lax.axis_index("row"), lax.axis_index("col")


def remote(src, dst, device, send, recv):
    return pltpu.make_async_remote_copy(src_ref=src, dst_ref=dst, send_sem=send, recv_sem=recv,
                                        device_id=device, device_id_type=MESH)


def landed(ref, sem):
    return pltpu.make_async_copy(ref, ref, sem)


def roles(limits):
    row, col = place()
    rows, cols = limits
    core = row % 2
    seam = cols // 2
    up, down = row > 0, row < rows - 1
    outer = jnp.where(core == 0, row - 1, row + 1)
    has_outer = jnp.logical_and(outer >= 0, outer < rows)
    near = {-1: jnp.logical_and(col > 0, col != seam), 1: jnp.logical_and(col < cols - 1, col != seam - 1)}
    at_seam = {-1: col == seam, 1: col == seam - 1}
    has = {-1: col > 0, 1: col < cols - 1}
    relay = {0: col == cols - 1, 1: col == 0}
    return dict(row=row, col=col, core=core, mate=(row + 1 - 2 * core, col), outer=(outer, col), has_outer=has_outer,
                near=near, at_seam=at_seam, has=has, relay=relay, seam=seam, cols=cols)


def greet(r):
    barrier = pltpu.get_barrier_semaphore()
    row, col, cols, seam = r["row"], r["col"], r["cols"], r["seam"]
    seam_any = jnp.logical_or(r["at_seam"][-1], r["at_seam"][1])
    relay_any = jnp.logical_or(r["relay"][0], r["relay"][1])
    pl.semaphore_signal(barrier, inc=1, device_id=r["mate"], device_id_type=MESH)
    total = jnp.int32(1)

    def to(cond, device):
        @pl.when(cond)
        def _():
            pl.semaphore_signal(barrier, inc=1, device_id=device, device_id_type=MESH)

        return cond.astype(jnp.int32)

    total += to(r["has_outer"], r["outer"])
    for dc in (-1, 1):
        total += to(r["has"][dc], (row, col + dc))
    for target in (0, cols - 1):
        total += to(seam_any, (row, target))
    for target in (seam - 1, seam):
        total += to(relay_any, (row, target))
    return barrier, total


def when(cond, *actions):
    @pl.when(cond)
    def _():
        for action in actions:
            action()


def halo_kernel(limits, obj_ref, canvas_ref, zeros, passing, own_sem, zero_sems, row_send, row_recv, col_send, col_recv,
                seam_send, seam_recv, pass_send, pass_recv, corner_send, corner_recv):
    cells = obj_ref.shape[1]
    half = cells // 2
    r = roles(limits)
    row, col, core, seam, cols = r["row"], r["col"], r["core"], r["seam"], r["cols"]
    barrier, total = greet(r)
    own = pltpu.make_async_copy(obj_ref, canvas_ref.at[:, pl.ds(HALO, cells), pl.ds(HALO, cells)], own_sem)
    own.start()
    zeros[...] = jnp.zeros_like(zeros)
    pl.semaphore_wait(barrier, total)

    outer_from = pl.multiple_of(jnp.where(core == 0, 0, cells - HALO), HALO)
    inner_from = pl.multiple_of(jnp.where(core == 0, cells - HALO, 0), HALO)
    outer_at = pl.multiple_of(jnp.where(core == 0, 0, cells + HALO), HALO)
    inner_at = pl.multiple_of(jnp.where(core == 0, cells + HALO, 0), HALO)
    strips = ((0, HALO), (cells - HALO, HALO), (HALO, cells - 2 * HALO))
    edge_from = {-1: 0, 1: cells - HALO}
    rim_at = {-1: 0, 1: cells + HALO}
    side = {-1: 0, 1: 1}

    def canvas(top, tall, left, wide):
        return canvas_ref.at[:, pl.ds(top, tall), pl.ds(left, wide)]

    def tile(top, tall, left, wide):
        return obj_ref.at[:, pl.ds(top, tall), pl.ds(left, wide)]

    edges = {}
    seams = {}
    for dc in (-1, 1):
        edges[dc] = remote(tile(0, cells, edge_from[dc], HALO), canvas(HALO, cells, rim_at[-dc], HALO), (row, col + dc),
                           col_send.at[side[dc]], col_recv.at[side[-dc]])
        when(r["near"][dc], edges[dc].start)
        pair = []
        for part, target in ((0, cols - 1), (1, 0)):
            pair.append(remote(tile(part * half, half, edge_from[dc], HALO), passing.at[side[dc]], (row, target),
                               seam_send.at[part], seam_recv.at[side[dc]]))
        seams[dc] = pair
        when(r["at_seam"][dc], pair[0].start, pair[1].start)

    inner = remote(tile(inner_from, HALO, 0, cells), canvas(outer_at_of_mate(inner_at, cells), HALO, HALO, cells), r["mate"],
                   row_send.at[3], row_recv.at[3])
    inner.start()
    outers = []
    for i, (left, wide) in enumerate(strips):
        copy = remote(tile(outer_from, HALO, left, wide), canvas(outer_at_of_mate(outer_at, cells), HALO, HALO + left, wide), r["outer"],
                      row_send.at[i], row_recv.at[i])
        outers.append(copy)
        when(r["has_outer"], copy.start)
    blanks = []
    for i, (cond, ref) in enumerate((
        (jnp.logical_not(r["has_outer"]), canvas(outer_at, HALO, 0, cells + 2 * HALO)),
        (jnp.logical_not(r["has"][-1]), canvas(HALO, cells, 0, HALO)),
        (jnp.logical_not(r["has"][1]), canvas(HALO, cells, cells + HALO, HALO)),
    )):
        source = zeros.at[:, pl.ds(0, HALO), :] if i == 0 else zeros.at[:, pl.ds(0, cells), pl.ds(0, HALO)]
        copy = pltpu.make_async_copy(source, ref, zero_sems.at[i])
        blanks.append((cond, copy))
        when(cond, copy.start)
    for dc in (-1, 1):
        for k, top in ((0, inner_at), (1, outer_at)):
            need = jnp.logical_not(r["has"][dc])
            if k:
                need = jnp.logical_and(need, r["has_outer"])
            copy = pltpu.make_async_copy(zeros.at[:, pl.ds(0, HALO), pl.ds(0, HALO)], canvas(top, HALO, rim_at[dc], HALO),
                                         zero_sems.at[3 + 2 * side[dc] + k])
            blanks.append((need, copy))
            when(need, copy.start)

    def forward(part, dc):
        target = seam if dc == 1 else seam - 1
        return remote(passing.at[side[dc]], canvas(HALO + part * half, half, rim_at[-dc], HALO), (row, target),
                      pass_send.at[side[dc]], pass_recv.at[part])

    def relay(part, dc):
        when(r["relay"][part], landed(passing.at[side[dc]], seam_recv.at[side[dc]]).wait, forward(part, dc).start)

    relay(0, -1)
    relay(1, 1)
    corners = {}
    for dc in (-1, 1):
        i = side[dc]
        strip = canvas(outer_at, HALO, HALO + edge_from[dc], HALO)
        give = jnp.logical_and(r["has_outer"], r["has"][dc])
        corners[dc] = (give, remote(strip, canvas(outer_at, HALO, rim_at[-dc], HALO), (row, col + dc),
                                    corner_send.at[i], corner_recv.at[1 - i]))
        when(r["has_outer"], landed(strip, row_recv.at[i]).wait)
        when(give, corners[dc][1].start)
    relay(0, 1)
    relay(1, -1)
    inside = {}
    for dc in (-1, 1):
        i = side[dc]
        near_mate = pl.multiple_of(inner_from + HALO, HALO)
        when(r["near"][dc], landed(canvas(HALO, cells, rim_at[dc], HALO), col_recv.at[i]).wait)
        for part in range(2):
            when(r["at_seam"][dc], landed(canvas(HALO + part * half, half, rim_at[dc], HALO), pass_recv.at[part]).wait)
        inside[dc] = remote(canvas(near_mate, HALO, rim_at[dc], HALO), canvas(outer_at_of_mate(inner_at, cells), HALO, rim_at[dc], HALO),
                            r["mate"], corner_send.at[2 + i], corner_recv.at[2 + i])
        when(r["has"][dc], inside[dc].start)

    inner.wait_send()
    landed(canvas(inner_at, HALO, HALO, cells), row_recv.at[3]).wait()
    when(r["has_outer"], *[copy.wait_send for copy in outers])
    when(r["has_outer"], landed(canvas(outer_at, HALO, HALO + strips[2][0], strips[2][1]), row_recv.at[2]).wait)
    for dc in (-1, 1):
        i = side[dc]
        when(r["near"][dc], edges[dc].wait_send)
        when(r["at_seam"][dc], seams[dc][0].wait_send, seams[dc][1].wait_send)
        for part in range(2):
            when(r["relay"][part], forward(part, dc).wait_send)
        when(corners[dc][0], corners[dc][1].wait_send, landed(canvas(outer_at, HALO, rim_at[dc], HALO), corner_recv.at[i]).wait)
        when(r["has"][dc], inside[dc].wait_send, landed(canvas(inner_at, HALO, rim_at[dc], HALO), corner_recv.at[2 + i]).wait)
    for cond, copy in blanks:
        when(cond, copy.wait)
    own.wait()


def outer_at_of_mate(at, cells):
    return pl.multiple_of(cells + HALO - at, HALO)


def exchange_halo(obj, limits):
    cells = obj.shape[1]
    dma = pltpu.SemaphoreType.DMA
    return pl.pallas_call(
        functools.partial(halo_kernel, limits),
        out_shape=jax.ShapeDtypeStruct((2, cells + 2 * HALO, cells + 2 * HALO), F32),
        in_specs=[pl.BlockSpec(memory_space=pl.ANY)],
        out_specs=pl.BlockSpec(memory_space=pl.ANY),
        scratch_shapes=[
            pltpu.VMEM((2, cells, cells + 2 * HALO), F32),
            pltpu.VMEM((2, 2, cells // 2, HALO), F32),
            dma, dma((7,)), dma((4,)), dma((4,)), dma((2,)), dma((2,)), dma((2,)), dma((2,)), dma((2,)), dma((2,)),
            dma((4,)), dma((4,)),
        ],
        compiler_params=pltpu.CompilerParams(collective_id=0, has_side_effects=True, vmem_limit_bytes=16 * 2**20),
    )(obj)


def place():
    return lax.axis_index("row"), lax.axis_index("col")


def remote(src, dst, device, send, recv):
    return pltpu.make_async_remote_copy(src_ref=src, dst_ref=dst, send_sem=send, recv_sem=recv,
                                        device_id=device, device_id_type=MESH)


def landed(ref, sem):
    return pltpu.make_async_copy(ref, ref, sem)


def roles(limits):
    row, col = place()
    rows, cols = limits
    core = row % 2
    seam = cols // 2
    up, down = row > 0, row < rows - 1
    outer = jnp.where(core == 0, row - 1, row + 1)
    has_outer = jnp.logical_and(outer >= 0, outer < rows)
    near = {-1: jnp.logical_and(col > 0, col != seam), 1: jnp.logical_and(col < cols - 1, col != seam - 1)}
    at_seam = {-1: col == seam, 1: col == seam - 1}
    has = {-1: col > 0, 1: col < cols - 1}
    relay = {0: col == cols - 1, 1: col == 0}
    return dict(row=row, col=col, core=core, mate=(row + 1 - 2 * core, col), outer=(outer, col), has_outer=has_outer,
                near=near, at_seam=at_seam, has=has, relay=relay, seam=seam, cols=cols)


def greet(r):
    barrier = pltpu.get_barrier_semaphore()
    row, col, cols, seam = r["row"], r["col"], r["cols"], r["seam"]
    seam_any = jnp.logical_or(r["at_seam"][-1], r["at_seam"][1])
    relay_any = jnp.logical_or(r["relay"][0], r["relay"][1])
    pl.semaphore_signal(barrier, inc=1, device_id=r["mate"], device_id_type=MESH)
    total = jnp.int32(1)

    def to(cond, device):
        @pl.when(cond)
        def _():
            pl.semaphore_signal(barrier, inc=1, device_id=device, device_id_type=MESH)

        return cond.astype(jnp.int32)

    total += to(r["has_outer"], r["outer"])
    for dc in (-1, 1):
        total += to(r["has"][dc], (row, col + dc))
    for target in (0, cols - 1):
        total += to(seam_any, (row, target))
    for target in (seam - 1, seam):
        total += to(relay_any, (row, target))
    return barrier, total


def when(cond, *actions):
    @pl.when(cond)
    def _():
        for action in actions:
            action()


def halo_kernel(limits, obj_ref, canvas_ref, zeros, passing, own_sem, zero_sems, row_send, row_recv, col_send, col_recv,
                seam_send, seam_recv, pass_send, pass_recv, corner_send, corner_recv):
    cells = obj_ref.shape[1]
    half = cells // 2
    r = roles(limits)
    row, col, core, seam, cols = r["row"], r["col"], r["core"], r["seam"], r["cols"]
    barrier, total = greet(r)
    own = pltpu.make_async_copy(obj_ref, canvas_ref.at[:, pl.ds(HALO, cells), pl.ds(HALO, cells)], own_sem)
    own.start()
    zeros[...] = jnp.zeros_like(zeros)
    pl.semaphore_wait(barrier, total)

    outer_from = pl.multiple_of(jnp.where(core == 0, 0, cells - HALO), HALO)
    inner_from = pl.multiple_of(jnp.where(core == 0, cells - HALO, 0), HALO)
    outer_at = pl.multiple_of(jnp.where(core == 0, 0, cells + HALO), HALO)
    inner_at = pl.multiple_of(jnp.where(core == 0, cells + HALO, 0), HALO)
    strips = ((0, HALO), (cells - HALO, HALO), (HALO, cells - 2 * HALO))
    edge_from = {-1: 0, 1: cells - HALO}
    rim_at = {-1: 0, 1: cells + HALO}
    side = {-1: 0, 1: 1}

    def canvas(top, tall, left, wide):
        return canvas_ref.at[:, pl.ds(top, tall), pl.ds(left, wide)]

    def tile(top, tall, left, wide):
        return obj_ref.at[:, pl.ds(top, tall), pl.ds(left, wide)]

    edges = {}
    seams = {}
    for dc in (-1, 1):
        edges[dc] = remote(tile(0, cells, edge_from[dc], HALO), canvas(HALO, cells, rim_at[-dc], HALO), (row, col + dc),
                           col_send.at[side[dc]], col_recv.at[side[-dc]])
        when(r["near"][dc], edges[dc].start)
        pair = []
        for part, target in ((0, cols - 1), (1, 0)):
            pair.append(remote(tile(part * half, half, edge_from[dc], HALO), passing.at[side[dc]], (row, target),
                               seam_send.at[part], seam_recv.at[side[dc]]))
        seams[dc] = pair
        when(r["at_seam"][dc], pair[0].start, pair[1].start)

    inner = remote(tile(inner_from, HALO, 0, cells), canvas(outer_at_of_mate(inner_at, cells), HALO, HALO, cells), r["mate"],
                   row_send.at[3], row_recv.at[3])
    inner.start()
    outers = []
    for i, (left, wide) in enumerate(strips):
        copy = remote(tile(outer_from, HALO, left, wide), canvas(outer_at_of_mate(outer_at, cells), HALO, HALO + left, wide), r["outer"],
                      row_send.at[i], row_recv.at[i])
        outers.append(copy)
        when(r["has_outer"], copy.start)
    blanks = []
    for i, (cond, ref) in enumerate((
        (jnp.logical_not(r["has_outer"]), canvas(outer_at, HALO, 0, cells + 2 * HALO)),
        (jnp.logical_not(r["has"][-1]), canvas(HALO, cells, 0, HALO)),
        (jnp.logical_not(r["has"][1]), canvas(HALO, cells, cells + HALO, HALO)),
    )):
        source = zeros.at[:, pl.ds(0, HALO), :] if i == 0 else zeros.at[:, pl.ds(0, cells), pl.ds(0, HALO)]
        copy = pltpu.make_async_copy(source, ref, zero_sems.at[i])
        blanks.append((cond, copy))
        when(cond, copy.start)
    for dc in (-1, 1):
        for k, top in ((0, inner_at), (1, outer_at)):
            need = jnp.logical_not(r["has"][dc])
            if k:
                need = jnp.logical_and(need, r["has_outer"])
            copy = pltpu.make_async_copy(zeros.at[:, pl.ds(0, HALO), pl.ds(0, HALO)], canvas(top, HALO, rim_at[dc], HALO),
                                         zero_sems.at[3 + 2 * side[dc] + k])
            blanks.append((need, copy))
            when(need, copy.start)

    def forward(part, dc):
        target = seam if dc == 1 else seam - 1
        return remote(passing.at[side[dc]], canvas(HALO + part * half, half, rim_at[-dc], HALO), (row, target),
                      pass_send.at[side[dc]], pass_recv.at[part])

    def relay(part, dc):
        when(r["relay"][part], landed(passing.at[side[dc]], seam_recv.at[side[dc]]).wait, forward(part, dc).start)

    relay(0, -1)
    relay(1, 1)
    corners = {}
    for dc in (-1, 1):
        i = side[dc]
        strip = canvas(outer_at, HALO, HALO + edge_from[dc], HALO)
        give = jnp.logical_and(r["has_outer"], r["has"][dc])
        corners[dc] = (give, remote(strip, canvas(outer_at, HALO, rim_at[-dc], HALO), (row, col + dc),
                                    corner_send.at[i], corner_recv.at[1 - i]))
        when(r["has_outer"], landed(strip, row_recv.at[i]).wait)
        when(give, corners[dc][1].start)
    relay(0, 1)
    relay(1, -1)
    inside = {}
    for dc in (-1, 1):
        i = side[dc]
        near_mate = pl.multiple_of(inner_from + HALO, HALO)
        when(r["near"][dc], landed(canvas(HALO, cells, rim_at[dc], HALO), col_recv.at[i]).wait)
        for part in range(2):
            when(r["at_seam"][dc], landed(canvas(HALO + part * half, half, rim_at[dc], HALO), pass_recv.at[part]).wait)
        inside[dc] = remote(canvas(near_mate, HALO, rim_at[dc], HALO), canvas(outer_at_of_mate(inner_at, cells), HALO, rim_at[dc], HALO),
                            r["mate"], corner_send.at[2 + i], corner_recv.at[2 + i])
        when(r["has"][dc], inside[dc].start)

    inner.wait_send()
    landed(canvas(inner_at, HALO, HALO, cells), row_recv.at[3]).wait()
    when(r["has_outer"], *[copy.wait_send for copy in outers])
    when(r["has_outer"], landed(canvas(outer_at, HALO, HALO + strips[2][0], strips[2][1]), row_recv.at[2]).wait)
    for dc in (-1, 1):
        i = side[dc]
        when(r["near"][dc], edges[dc].wait_send)
        when(r["at_seam"][dc], seams[dc][0].wait_send, seams[dc][1].wait_send)
        for part in range(2):
            when(r["relay"][part], forward(part, dc).wait_send)
        when(corners[dc][0], corners[dc][1].wait_send, landed(canvas(outer_at, HALO, rim_at[dc], HALO), corner_recv.at[i]).wait)
        when(r["has"][dc], inside[dc].wait_send, landed(canvas(inner_at, HALO, rim_at[dc], HALO), corner_recv.at[2 + i]).wait)
    for cond, copy in blanks:
        when(cond, copy.wait)
    own.wait()


def outer_at_of_mate(at, cells):
    return pl.multiple_of(cells + HALO - at, HALO)


def exchange_halo(obj, limits):
    cells = obj.shape[1]
    dma = pltpu.SemaphoreType.DMA
    return pl.pallas_call(
        functools.partial(halo_kernel, limits),
        out_shape=jax.ShapeDtypeStruct((2, cells + 2 * HALO, cells + 2 * HALO), F32),
        in_specs=[pl.BlockSpec(memory_space=pl.ANY)],
        out_specs=pl.BlockSpec(memory_space=pl.ANY),
        scratch_shapes=[
            pltpu.VMEM((2, cells, cells + 2 * HALO), F32),
            pltpu.VMEM((2, 2, cells // 2, HALO), F32),
            dma, dma((7,)), dma((4,)), dma((4,)), dma((2,)), dma((2,)), dma((2,)), dma((2,)), dma((2,)), dma((2,)),
            dma((4,)), dma((4,)),
        ],
        compiler_params=pltpu.CompilerParams(collective_id=0, has_side_effects=True, vmem_limit_bytes=16 * 2**20),
    )(obj)


SIDES = [(-1, 0), (1, 0), (0, -1), (0, 1), (-1, -1), (-1, 1), (1, -1), (1, 1)]


ORDERS = [(0, 1, 2), (1, 2, 0), (2, 0, 1), (1, 0, 2)]


def spots():
    row, col = place()
    return (row // 2 % 2 * 2 + col // 4, row // 4, col % 4)


def along(axis, by):
    row, col = place()
    at = list(spots())
    at[axis] = (at[axis] + by) % 4
    return (at[1] * 4 + at[0] // 2 * 2 + row % 2, at[0] % 2 * 4 + at[2])


def finish_kernel(limits, spread_ref, pg_ref, energy_ref, obj_ref, probe_ref, illum_ref,
                  onew_ref, pnew_ref, land_rows, land_cols, land_inner, land_outer, out_cols, out_ends, passing, total_ref, mate_half, mate_energy, warm, heat,
                  box1, box2, box3, seam_send, seam_recv, pass_send, pass_recv, near_send, near_recv, row_send, row_recv,
                  corner_send, corner_recv, mate_send, mate_recv, down_send, down_recv, up_send, up_recv,
                  heat_send, heat_recv):
    cells = obj_ref.shape[1]
    row, col = place()
    core = row % 2
    mate = (row + 1 - 2 * core, col)
    at = spots()
    units = len(ORDERS)
    unit = pg_ref.shape[1] // units

    r = roles(limits)
    barrier, total = greet(r)
    pl.semaphore_signal(barrier, inc=1, device_id=mate, device_id_type=MESH)
    for axis in range(3):
        for by in (1, 2, 3):
            pl.semaphore_signal(barrier, inc=1, device_id=along(axis, by), device_id_type=MESH)
    pl.semaphore_wait(barrier, total + 10)

    firsts = [remote(energy_ref, mate_energy, mate, mate_send.at[0], mate_recv.at[0])]
    for u in range(units):
        rows = pl.ds(u * unit, unit)
        firsts.append(remote(pg_ref.at[1 - core, rows], mate_half.at[rows], mate, mate_send.at[1 + u], mate_recv.at[1 + u]))
    half = cells // 2
    seam, cols = r["seam"], r["cols"]
    outer_from = pl.multiple_of(jnp.where(core == 0, 0, cells - HALO), HALO)
    inner_from = pl.multiple_of(jnp.where(core == 0, cells - HALO, 0), HALO)
    outer_at = pl.multiple_of(jnp.where(core == 0, 0, cells + HALO), HALO)
    inner_at = pl.multiple_of(jnp.where(core == 0, cells + HALO, 0), HALO)
    edge_from = {-1: 0, 1: cells - HALO}
    rim_at = {-1: 0, 1: cells + HALO}
    side = {-1: 0, 1: 1}
    inside, nears, seams, ends, corners = {}, {}, {}, {}, {}

    def region(top, tall, left, wide):
        return spread_ref.at[:, pl.ds(top, tall), pl.ds(left, wide)]

    for dc in (-1, 1):
        i = side[dc]
        inside[dc] = remote(region(inner_at, HALO, rim_at[dc], HALO), land_inner.at[i], mate, corner_send.at[i], corner_recv.at[i])
        when(r["has"][dc], inside[dc].start)
    for copy in firsts:
        copy.start()
    for dc in (-1, 1):
        i = side[dc]

        @pl.when(r["has"][dc])
        def _(dc=dc, i=i):
            inside[dc].wait_recv()
            for part in range(2):
                out_cols[i, part] = spread_ref[part, HALO:HALO + cells, rim_at[dc]:rim_at[dc] + HALO]
                out_cols[i, part, pl.ds(inner_from, HALO), :] += land_inner[i, part]

        seams[dc] = [remote(out_cols.at[i, :, pl.ds(part * half, half), :], passing.at[i], (row, target),
                            seam_send.at[part], seam_recv.at[i]) for part, target in ((0, cols - 1), (1, 0))]
        when(r["at_seam"][dc], seams[dc][0].start, seams[dc][1].start)

    inner = remote(region(inner_at, HALO, HALO, cells), land_rows.at[1], mate, row_send.at[3], row_recv.at[3])
    middle = remote(region(outer_at, HALO, 2 * HALO, cells - 2 * HALO), land_rows.at[0, :, :, pl.ds(HALO, cells - 2 * HALO)], r["outer"],
                    row_send.at[2], row_recv.at[2])

    def start_fold():
        for dc in (-1, 1):
            i = side[dc]
            corners[dc] = (jnp.logical_and(r["has_outer"], r["has"][dc]),
                           remote(region(outer_at, HALO, rim_at[dc], HALO), land_outer.at[1 - i], (row, col + dc),
                                  corner_send.at[2 + i], corner_recv.at[3 - i]))
            when(corners[dc][0], corners[dc][1].start)
        when(r["has_outer"], middle.start)
        for dc in (-1, 1):
            i = side[dc]
            nears[dc] = remote(out_cols.at[i], land_cols.at[1 - i], (row, col + dc), near_send.at[i], near_recv.at[1 - i])
            when(r["near"][dc], nears[dc].start)
        inner.start()

    def forward(part, dc):
        i = side[dc]
        target = seam if dc == 1 else seam - 1
        return remote(passing.at[i], land_cols.at[1 - i, :, pl.ds(part * half, half), :], (row, target), pass_send.at[i], pass_recv.at[part])

    def relay(part, dc):
        when(r["relay"][part], landed(passing.at[side[dc]], seam_recv.at[side[dc]]).wait, forward(part, dc).start)

    def send_ends():
        for dc in (-1, 1):
            i = side[dc]
            ends[dc] = remote(out_ends.at[i], land_rows.at[0, :, :, pl.ds(edge_from[dc], HALO)], r["outer"], row_send.at[i], row_recv.at[i])

            @pl.when(r["has_outer"])
            def _(dc=dc, i=i):
                left = HALO + edge_from[dc]
                for part in range(2):
                    out_ends[i, part] = spread_ref[part, pl.ds(outer_at, HALO), left:left + HALO]

                @pl.when(r["has"][dc])
                def _():
                    landed(land_outer.at[i], corner_recv.at[2 + i]).wait()
                    for part in range(2):
                        out_ends[i, part] += land_outer[i, part]

                ends[dc].start()

    def piece(u, depth, spot):
        order = ORDERS[u]
        start = u * unit
        if depth == 1:
            return pl.ds(pl.multiple_of(start + spot * (unit // 4), unit // 4), unit // 4), slice(None)
        start = start + at[order[0]] * (unit // 4)
        if depth == 2:
            return pl.ds(pl.multiple_of(start + spot * (unit // 16), unit // 16), unit // 16), slice(None)
        start = start + at[order[1]] * (unit // 16)
        return (pl.ds(pl.multiple_of(start + spot // 2 * 8, 8), 8), pl.ds(pl.multiple_of(spot % 2 * 128, 128), 128))

    def own(u, depth):
        return piece(u, depth, at[ORDERS[u][depth - 1]])

    boxes = (box1, box2, box3)
    waiting = []

    def down(u, depth):
        axis = ORDERS[u][depth - 1]
        out = []
        for by in (1, 2, 3):
            copy = remote(total_ref.at[piece(u, depth, (at[axis] + by) % 4)], boxes[depth - 1].at[u, by - 1], along(axis, by),
                          down_send.at[u, depth - 1, by - 1], down_recv.at[u, depth - 1, by - 1])
            copy.start()
            out.append(copy)
        waiting.extend(out)
        return out

    def pass_heat(axis):
        out = []
        for by in (1, 2, 3):
            copy = remote(warm.at[axis], heat.at[axis, by - 1], along(axis, by), heat_send.at[axis, by - 1], heat_recv.at[axis, by - 1])
            copy.start()
            out.append(copy)
        waiting.extend(out)
        return out

    firsts[0].wait_recv()
    warm[0] = energy_ref[...] + mate_energy[...]
    hot = pass_heat(0)
    flying = []
    for u in range(units):
        rows = pl.ds(u * unit, unit)
        firsts[1 + u].wait_recv()
        total_ref[rows, :] = pg_ref[core, rows, :] + mate_half[rows, :]
        flying.append(down(u, 1))
    waiting.extend(firsts)
    start_fold()

    share = 1.0 / illum_ref[0]
    step_rows = 64

    def base(j, c):
        r = pl.ds(pl.multiple_of(j * step_rows, step_rows), step_rows)
        rr = pl.ds(pl.multiple_of(j * step_rows + HALO, step_rows), step_rows)
        for part in range(2):
            onew_ref[part, r, :] = obj_ref[part, r, :] + spread_ref[part, rr, HALO:HALO + cells] * share
        return c

    lax.fori_loop(0, cells // step_rows, base, 0)
    relay(0, -1)
    relay(1, 1)

    for depth in (1, 2, 3):
        if depth == 2:
            send_ends()
        if depth == 3:
            relay(0, 1)
            relay(1, -1)
        for copy in hot:
            copy.wait_recv()
        fresh = warm[depth - 1] + heat[depth - 1, 0] + heat[depth - 1, 1] + heat[depth - 1, 2]
        if depth < 3:
            warm[depth] = fresh
            hot = pass_heat(depth)
        for u in range(units):
            for copy in flying[u]:
                copy.wait_recv()
            box = boxes[depth - 1]
            where = own(u, depth)
            summed = total_ref[where] + box[u, 0] + box[u, 1] + box[u, 2]
            if depth < 3:
                total_ref[where] = summed
                flying[u] = down(u, depth + 1)
            else:
                pnew_ref[(core,) + where] = probe_ref[(core,) + where] + summed / (fresh[:, :128] + EPSILON)

    def up(u, depth):
        axis = ORDERS[u][depth - 1]
        spot = pnew_ref.at[(core,) + own(u, depth)]
        out = []
        for by in (1, 2, 3):
            landed = pnew_ref.at[(core,) + piece(u, depth, (at[axis] + 4 - by) % 4)]
            copy = remote(spot, spot, along(axis, by), up_send.at[u, depth - 1, by - 1], up_recv.at[u, depth - 1, by - 1])
            copy.start()
            waiting.append(copy)
            out.append(pltpu.make_async_copy(landed, landed, up_recv.at[u, depth - 1, by - 1]))
        return out

    for u in range(units):
        flying[u] = up(u, 3)
    lasts = []
    for depth in (3, 2, 1):
        for u in range(units):
            for copy in flying[u]:
                copy.wait()
            if depth > 1:
                flying[u] = up(u, depth - 1)
            else:
                rows = pl.ds(u * unit, unit)
                done = pnew_ref.at[core, rows]
                copy = remote(done, done, mate, mate_send.at[5 + u], mate_recv.at[5 + u])
                copy.start()
                waiting.append(copy)
                got = pnew_ref.at[1 - core, rows]
                lasts.append(pltpu.make_async_copy(got, got, mate_recv.at[5 + u]))

    inner.wait()
    for part in range(2):
        onew_ref[part, pl.ds(inner_from, HALO), :] += land_rows[1, part] * share

    @pl.when(r["has_outer"])
    def _():
        middle.wait()
        for dc in (-1, 1):
            ends[dc].wait()
        for part in range(2):
            onew_ref[part, pl.ds(outer_from, HALO), :] += land_rows[0, part] * share

    for dc in (-1, 1):
        i = side[dc]
        when(r["near"][dc], nears[dc].wait_send, landed(land_cols.at[i], near_recv.at[i]).wait)
        when(r["at_seam"][dc], seams[dc][0].wait_send, seams[dc][1].wait_send)
        for part in range(2):
            when(r["at_seam"][dc], landed(land_cols.at[i, :, pl.ds(part * half, half), :], pass_recv.at[part]).wait)
            when(r["relay"][part], forward(part, dc).wait_send)
        when(corners[dc][0], corners[dc][1].wait_send)

        @pl.when(r["has"][dc])
        def _(dc=dc, i=i):
            inside[dc].wait_send()
            for part in range(2):
                onew_ref[part, :, edge_from[dc]:edge_from[dc] + HALO] += land_cols[i, part] * share

    for copy in lasts:
        copy.wait()
    for copy in waiting:
        copy.wait_send()


def finish(spread, pg, energy, obj, probe, illum, limits):
    cells = obj.shape[1]
    rows, lanes = probe.shape[1], probe.shape[2]
    units = len(ORDERS)
    unit = rows // units
    vmem = pl.BlockSpec(memory_space=pltpu.VMEM)
    dma = pltpu.SemaphoreType.DMA
    return pl.pallas_call(
        functools.partial(finish_kernel, limits),
        out_shape=(jax.ShapeDtypeStruct(obj.shape, F32), jax.ShapeDtypeStruct(probe.shape, F32)),
        in_specs=[vmem, vmem, vmem, vmem, vmem, pl.BlockSpec(memory_space=pltpu.SMEM)],
        out_specs=(vmem, vmem),
        scratch_shapes=[
            pltpu.VMEM((2, 2, HALO, cells), F32),
            pltpu.VMEM((2, 2, cells, HALO), F32),
            pltpu.VMEM((2, 2, HALO, HALO), F32),
            pltpu.VMEM((2, 2, HALO, HALO), F32),
            pltpu.VMEM((2, 2, cells, HALO), F32),
            pltpu.VMEM((2, 2, HALO, HALO), F32),
            pltpu.VMEM((2, 2, cells // 2, HALO), F32),
            pltpu.VMEM((rows, lanes), F32),
            pltpu.VMEM((rows, lanes), F32),
            pltpu.VMEM((8, 128), F32),
            pltpu.VMEM((3, 8, 128), F32),
            pltpu.VMEM((3, 3, 8, 128), F32),
            pltpu.VMEM((units, 3, unit // 4, lanes), F32),
            pltpu.VMEM((units, 3, unit // 16, lanes), F32),
            pltpu.VMEM((units, 3, 8, 128), F32),
            dma((2,)), dma((2,)), dma((2,)), dma((2,)), dma((2,)), dma((2,)), dma((4,)), dma((4,)), dma((4,)), dma((4,)),
            dma((9,)), dma((9,)),
            dma((units, 3, 3)), dma((units, 3, 3)), dma((units, 3, 3)), dma((units, 3, 3)),
            dma((3, 3)), dma((3, 3)),
        ],
        compiler_params=pltpu.CompilerParams(collective_id=1, has_side_effects=True, vmem_limit_bytes=48 * 2**20),
    )(spread, pg, energy, obj, probe, illum)


def body(limits, object_field, probe, amplitudes, positions, counts):
    canvas = exchange_halo(object_field, limits)
    spread, probe_grad, shift, energy, illum = step(positions[0, 0], counts[0], canvas, probe, amplitudes[0, 0])
    n = probe.shape[2]
    flat = (2, probe.shape[1] * n, n)
    object_new, probe_new = finish(spread, probe_grad.reshape(flat), energy, object_field, probe.reshape(flat), illum, limits)
    return (object_new, probe_new.reshape(probe.shape), shift[None, None])


def solution(mesh):
    return jax.shard_map(
        functools.partial(body, (mesh.shape["row"], mesh.shape["col"])),
        mesh=mesh,
        in_specs=(
            P(None, "row", "col"),
            P(),
            P("row", "col", None, None, None),
            P("row", "col", None, None),
            P("row", "col"),
        ),
        out_specs=(P(None, "row", "col"), P(), P("row", "col", None, None)),
        check_vma=False,
    )
```

```python
import functools
import math

import ml_dtypes
import numpy as np
import jax
import jax.numpy as jnp
from jax import lax
from jax.experimental import pallas as pl
from jax.experimental.pallas import tpu as pltpu
from jax.sharding import PartitionSpec as P

HALO = 128
INTENSITY_FLOOR = 0.1
EPSILON = 1e-06
F32 = jnp.float32
BF16 = jnp.bfloat16
UNROLL = 4


def dft_tables(pixels):
    half = pixels // 2
    k = np.arange(half)[:, None]
    n = np.arange(half)[None, :]
    out = []
    for parity in (0, 1):
        angle = (n * (2 * k + parity) % pixels) * (2.0 * math.pi / pixels)
        c = np.cos(angle) / math.sqrt(pixels)
        s = np.sin(angle) / math.sqrt(pixels)
        out.append(np.block([[c, s], [-s, c]]))
    both = []
    for m in (out[0], out[1], out[0].T, out[1].T):
        m = m.astype(np.float32)
        hi = m.astype(ml_dtypes.bfloat16)
        lo = (m - hi.astype(np.float32)).astype(ml_dtypes.bfloat16)
        both.append(np.stack([hi, lo]))
    return np.stack(both)


def parity_table(pixels):
    half = pixels // 2
    t = np.zeros((pixels, pixels), np.float32)
    for j in range(half):
        t[2 * j, j] = 1.0
        t[2 * j + 1, half + j] = 1.0
    return t.astype(ml_dtypes.bfloat16)


def split(x):
    hi = x.astype(BF16)
    return hi, (x - hi.astype(F32)).astype(BF16)


def mm(a, b):
    return jnp.dot(a, b, preferred_element_type=F32)


def from_left(table, x):
    hi, lo = split(x)
    return mm(jnp.concatenate([table[0], table[0], table[1]], 1), jnp.concatenate([hi, lo, hi], 0))


def from_right(x, table):
    hi, lo = split(x)
    return mm(jnp.concatenate([hi, lo, hi], 1), jnp.concatenate([table[0], table[0], table[1]], 0))


def lane_of():
    return lax.broadcasted_iota(jnp.int32, (1, 8, 128), 2)


def row_of():
    return lax.broadcasted_iota(jnp.int32, (1, 8, 128), 1)


def cut(canvas_ref, patch, a, b):
    n = patch.shape[1]
    groups = n // 8
    t, u = b % 128, a % 8
    row = pl.multiple_of(a - u, 8)
    lane, sub = lane_of(), row_of()
    power = jnp.zeros((8, 128), F32)
    for part in range(2):
        blocks = []
        for j in range(n // 128 + 1):
            v = canvas_ref[part, pl.ds(row, n + 8), pl.ds(pl.multiple_of(b - t + j * 128, 128), 128)]
            v = pltpu.roll(v.reshape(groups + 1, 8, 128), (8 - u) % 8, 1)
            v = jnp.where(sub < 8 - u, v[:groups], v[1:])
            blocks.append(pltpu.roll(v, (128 - t) % 128, 2))
        for j in range(n // 128):
            p = jnp.where(lane < 128 - t, blocks[j], blocks[j + 1])
            power += jnp.sum(p * p, axis=0)
            patch[part, :, j * 128:(j + 1) * 128] = p.reshape(n, 128)
    return power


def lay(canvas_ref, spread_ref, grad, a, b):
    n = grad.shape[1]
    groups = n // 8
    count = n // 128
    t, u = b % 128, a % 8
    row = pl.multiple_of(a - u, 8)
    before = pl.multiple_of(jnp.maximum(a - u - 8, 0), 8)
    lane, sub = lane_of(), row_of()
    down = jnp.zeros((8, 128), F32)
    across = jnp.zeros((8, 128), F32)
    none = jnp.zeros((1, 8, 128), F32)
    for part in range(2):
        turned = [pltpu.roll(grad[part, :, j * 128:(j + 1) * 128].reshape(groups, 8, 128), t, 2) for j in range(count)]
        strips = []
        for j in range(-1, count + 1):
            at = pl.multiple_of(jnp.maximum(b - t + j * 128, 0), 128)
            strips.append(canvas_ref[part, pl.ds(row, n + 8), pl.ds(at, 128)].reshape(groups + 1, 8, 128))
        for j in range(count + 1):
            left = turned[j - 1] if j else 0.0
            g = jnp.where(lane < t, left, turned[j] if j < count else 0.0)
            g = pltpu.roll(g, u, 1)
            g = jnp.where(sub < u, jnp.concatenate([none, g], 0), jnp.concatenate([g, none], 0))
            at = pl.ds(pl.multiple_of(b - t + j * 128, 128), 128)
            spread_ref[part, pl.ds(row, n + 8), at] += g.reshape(n + 8, 128)
            v = strips[j + 1]
            first = canvas_ref[part, pl.ds(before, 8), at].reshape(1, 8, 128)
            nxt = pltpu.roll(v, 7, 1)
            prv = pltpu.roll(jnp.concatenate([first, v], 0), 1, 1)
            nxt = jnp.where(sub < 7, nxt, jnp.concatenate([nxt[1:], none], 0))
            prv = jnp.where(sub < 1, prv[:-1], prv[1:])
            down += jnp.sum(g * (nxt - prv), axis=0)
            nxt = pltpu.roll(v, 127, 2)
            prv = pltpu.roll(v, 1, 2)
            if j < count:
                nxt = jnp.where(lane < 127, nxt, pltpu.roll(strips[j + 2], 127, 2))
            prv = jnp.where(lane < 1, pltpu.roll(strips[j], 1, 2), prv)
            across += jnp.sum(g * (nxt - prv), axis=0)
    return down, across


def step_kernel(pos_ref, count_ref, canvas_ref, probe_ref, amp_ref, tab_ref, par_ref,
                spread_ref, pg_ref, shift_ref, energy_ref, illum_ref,
                patch, far, inten, grad, col0, col1, sums):
    n = probe_ref.shape[2]
    h = n // 2
    modes = probe_ref.shape[1]
    slots = amp_ref.shape[0]
    spread_ref[...] = jnp.zeros_like(spread_ref)
    pg_ref[...] = jnp.zeros_like(pg_ref)
    sums[...] = jnp.zeros_like(sums)
    light = jnp.zeros((n, n), F32)
    for k in range(modes):
        for part in range(2):
            light += probe_ref[part, k] * probe_ref[part, k]
    illum_ref[0] = jnp.max(light)

    def visit(s, carry):
        a = pos_ref[s, 0]
        b = pos_ref[s, 1]
        sums[s, 2] = cut(canvas_ref, patch, a, b)

        inten[...] = jnp.zeros_like(inten)

        def forward(k, c):
            pr, pi = probe_ref[0, k], probe_ref[1, k]
            pr_, pi_ = patch[0], patch[1]
            er = pr * pr_ - pi * pi_
            ei = pr * pi_ + pi * pr_
            up = jnp.concatenate([er[:h] + er[h:], ei[:h] + ei[h:]], 0)
            dn = jnp.concatenate([er[:h] - er[h:], ei[:h] - ei[h:]], 0)
            su = from_left(tab_ref[0], up)
            sd = from_left(tab_ref[1], dn)
            zr = jnp.concatenate([su[:h], sd[:h]], 0)
            zi = jnp.concatenate([su[h:], sd[h:]], 0)
            lf = jnp.concatenate([zr[:, :h] + zr[:, h:], zi[:, :h] + zi[:, h:]], 1)
            rt = jnp.concatenate([zr[:, :h] - zr[:, h:], zi[:, :h] - zi[:, h:]], 1)
            fa = from_right(lf, tab_ref[2])
            fb = from_right(rt, tab_ref[3])
            far[k, 0] = fa
            far[k, 1] = fb
            inten[:, :h] += fa[:, :h] * fa[:, :h] + fa[:, h:] * fa[:, h:]
            inten[:, h:] += fb[:, :h] * fb[:, :h] + fb[:, h:] * fb[:, h:]
            return c

        lax.fori_loop(0, modes, forward, 0, unroll=UNROLL)
        hi, lo = split(amp_ref[s])
        am = mm(hi, par_ref[...]) + mm(lo, par_ref[...])
        col0[...] = am[:, :h]
        col1[...] = am[:, h:]
        am = jnp.concatenate([jnp.concatenate([col[pl.ds(p, h, 2), :] for p in range(2)], 0) for col in (col0, col1)], 1)
        inten[...] = am * lax.rsqrt(jnp.maximum(inten[...], INTENSITY_FLOOR)) - 1.0
        grad[...] = jnp.zeros_like(grad)

        def backward(k, c):
            ma, mb = inten[:, :h], inten[:, h:]
            e = from_right(far[k, 0] * jnp.concatenate([ma, ma], 1), tab_ref[0])
            o = from_right(far[k, 1] * jnp.concatenate([mb, mb], 1), tab_ref[1])
            lo = e + o
            hi = e - o
            ev = jnp.concatenate([jnp.concatenate([lo[:h, :h], hi[:h, :h]], 1),
                                  jnp.concatenate([lo[:h, h:], hi[:h, h:]], 1)], 0)
            od = jnp.concatenate([jnp.concatenate([lo[h:, :h], hi[h:, :h]], 1),
                                  jnp.concatenate([lo[h:, h:], hi[h:, h:]], 1)], 0)
            e2 = from_left(tab_ref[2], ev)
            o2 = from_left(tab_ref[3], od)
            for r, half in ((slice(0, h), e2 + o2), (slice(h, n), e2 - o2)):
                cr, ci = half[:h], half[h:]
                pr, pi = probe_ref[0, k, r], probe_ref[1, k, r]
                qr, qi = patch[0, r], patch[1, r]
                grad[0, r] += pr * cr + pi * ci
                grad[1, r] += pr * ci - pi * cr
                pg_ref[0, k, r] += qr * cr + qi * ci
                pg_ref[1, k, r] += qr * ci - qi * cr
            return c

        lax.fori_loop(0, modes, backward, 0, unroll=UNROLL)
        down, across = lay(canvas_ref, spread_ref, grad, a, b)
        sums[s, 0] = down
        sums[s, 1] = across
        return carry

    lax.fori_loop(0, count_ref[0], visit, 0)
    energy = jnp.zeros((8, 128), F32)
    for s in range(slots):
        energy += sums[s, 2]
        for kind in range(2):
            shift_ref[s, kind] = jnp.sum(sums[s, kind]) * (0.5 / n)
    energy_ref[...] = jnp.broadcast_to(jnp.sum(energy, keepdims=True) / (n * n), energy.shape)


def step(pos, count, canvas, probe, amp):
    n = probe.shape[2]
    modes = probe.shape[1]
    slots = amp.shape[0]
    rows = canvas.shape[1]
    vmem = pl.BlockSpec(memory_space=pltpu.VMEM)
    smem = pl.BlockSpec(memory_space=pltpu.SMEM)
    return pl.pallas_call(
        step_kernel,
        out_shape=(
            jax.ShapeDtypeStruct((2, rows, rows), F32),
            jax.ShapeDtypeStruct(probe.shape, F32),
            jax.ShapeDtypeStruct((slots, 2), F32),
            jax.ShapeDtypeStruct((8, 128), F32),
            jax.ShapeDtypeStruct((1,), F32),
        ),
        in_specs=[smem, smem, vmem, vmem, vmem, vmem, vmem],
        out_specs=(vmem, vmem, smem, vmem, smem),
        scratch_shapes=[
            pltpu.VMEM((2, n, n), F32),
            pltpu.VMEM((modes, 2, n, n), F32),
            pltpu.VMEM((n, n), F32),
            pltpu.VMEM((2, n, n), F32),
            pltpu.VMEM((n, n // 2), F32),
            pltpu.VMEM((n, n // 2), F32),
            pltpu.VMEM((slots, 3, 8, 128), F32),
        ],
        compiler_params=pltpu.CompilerParams(vmem_limit_bytes=60 * 2**20),
    )(pos, count, canvas, probe, amp, jnp.asarray(dft_tables(n)), jnp.asarray(parity_table(n)))


MESH = pl.DeviceIdType.MESH


def place():
    return lax.axis_index("row"), lax.axis_index("col")


def remote(src, dst, device, send, recv):
    return pltpu.make_async_remote_copy(src_ref=src, dst_ref=dst, send_sem=send, recv_sem=recv,
                                        device_id=device, device_id_type=MESH)


def landed(ref, sem):
    return pltpu.make_async_copy(ref, ref, sem)


def roles(limits):
    row, col = place()
    rows, cols = limits
    core = row % 2
    seam = cols // 2
    up, down = row > 0, row < rows - 1
    outer = jnp.where(core == 0, row - 1, row + 1)
    has_outer = jnp.logical_and(outer >= 0, outer < rows)
    near = {-1: jnp.logical_and(col > 0, col != seam), 1: jnp.logical_and(col < cols - 1, col != seam - 1)}
    at_seam = {-1: col == seam, 1: col == seam - 1}
    has = {-1: col > 0, 1: col < cols - 1}
    relay = {0: col == cols - 1, 1: col == 0}
    return dict(row=row, col=col, core=core, mate=(row + 1 - 2 * core, col), outer=(outer, col), has_outer=has_outer,
                near=near, at_seam=at_seam, has=has, relay=relay, seam=seam, cols=cols)


def greet(r):
    barrier = pltpu.get_barrier_semaphore()
    row, col, cols, seam = r["row"], r["col"], r["cols"], r["seam"]
    seam_any = jnp.logical_or(r["at_seam"][-1], r["at_seam"][1])
    relay_any = jnp.logical_or(r["relay"][0], r["relay"][1])
    pl.semaphore_signal(barrier, inc=1, device_id=r["mate"], device_id_type=MESH)
    total = jnp.int32(1)

    def to(cond, device):
        @pl.when(cond)
        def _():
            pl.semaphore_signal(barrier, inc=1, device_id=device, device_id_type=MESH)

        return cond.astype(jnp.int32)

    total += to(r["has_outer"], r["outer"])
    for dc in (-1, 1):
        total += to(r["has"][dc], (row, col + dc))
    for target in (0, cols - 1):
        total += to(seam_any, (row, target))
    for target in (seam - 1, seam):
        total += to(relay_any, (row, target))
    return barrier, total


def when(cond, *actions):
    @pl.when(cond)
    def _():
        for action in actions:
            action()


def halo_kernel(limits, source_ref, canvas_ref, obj_ref, zeros, passing, load_sem, own_sem, zero_sems, row_send, row_recv, col_send, col_recv,
                seam_send, seam_recv, pass_send, pass_recv, corner_send, corner_recv):
    cells = obj_ref.shape[1]
    half = cells // 2
    load = pltpu.make_async_copy(source_ref, obj_ref, load_sem)
    load.start()
    r = roles(limits)
    row, col, core, seam, cols = r["row"], r["col"], r["core"], r["seam"], r["cols"]
    barrier, total = greet(r)
    own = pltpu.make_async_copy(obj_ref, canvas_ref.at[:, pl.ds(HALO, cells), pl.ds(HALO, cells)], own_sem)
    zeros[...] = jnp.zeros_like(zeros)
    load.wait()
    own.start()
    pl.semaphore_wait(barrier, total)

    outer_from = pl.multiple_of(jnp.where(core == 0, 0, cells - HALO), HALO)
    inner_from = pl.multiple_of(jnp.where(core == 0, cells - HALO, 0), HALO)
    outer_at = pl.multiple_of(jnp.where(core == 0, 0, cells + HALO), HALO)
    inner_at = pl.multiple_of(jnp.where(core == 0, cells + HALO, 0), HALO)
    strips = ((0, HALO), (cells - HALO, HALO), (HALO, cells - 2 * HALO))
    edge_from = {-1: 0, 1: cells - HALO}
    rim_at = {-1: 0, 1: cells + HALO}
    side = {-1: 0, 1: 1}

    def canvas(top, tall, left, wide):
        return canvas_ref.at[:, pl.ds(top, tall), pl.ds(left, wide)]

    def tile(top, tall, left, wide):
        return obj_ref.at[:, pl.ds(top, tall), pl.ds(left, wide)]

    edges = {}
    seams = {}
    for dc in (-1, 1):
        edges[dc] = remote(tile(0, cells, edge_from[dc], HALO), canvas(HALO, cells, rim_at[-dc], HALO), (row, col + dc),
                           col_send.at[side[dc]], col_recv.at[side[-dc]])
        when(r["near"][dc], edges[dc].start)
        pair = []
        for part, target in ((0, cols - 1), (1, 0)):
            pair.append(remote(tile(part * half, half, edge_from[dc], HALO), passing.at[side[dc]], (row, target),
                               seam_send.at[part], seam_recv.at[side[dc]]))
        seams[dc] = pair
        when(r["at_seam"][dc], pair[0].start, pair[1].start)

    inner = remote(tile(inner_from, HALO, 0, cells), canvas(outer_at_of_mate(inner_at, cells), HALO, HALO, cells), r["mate"],
                   row_send.at[3], row_recv.at[3])
    inner.start()
    outers = []
    for i, (left, wide) in enumerate(strips):
        copy = remote(tile(outer_from, HALO, left, wide), canvas(outer_at_of_mate(outer_at, cells), HALO, HALO + left, wide), r["outer"],
                      row_send.at[i], row_recv.at[i])
        outers.append(copy)
        when(r["has_outer"], copy.start)
    blanks = []
    for i, (cond, ref) in enumerate((
        (jnp.logical_not(r["has_outer"]), canvas(outer_at, HALO, 0, cells + 2 * HALO)),
        (jnp.logical_not(r["has"][-1]), canvas(HALO, cells, 0, HALO)),
        (jnp.logical_not(r["has"][1]), canvas(HALO, cells, cells + HALO, HALO)),
    )):
        source = zeros.at[:, pl.ds(0, HALO), :] if i == 0 else zeros.at[:, pl.ds(0, cells), pl.ds(0, HALO)]
        copy = pltpu.make_async_copy(source, ref, zero_sems.at[i])
        blanks.append((cond, copy))
        when(cond, copy.start)
    for dc in (-1, 1):
        for k, top in ((0, inner_at), (1, outer_at)):
            need = jnp.logical_not(r["has"][dc])
            if k:
                need = jnp.logical_and(need, r["has_outer"])
            copy = pltpu.make_async_copy(zeros.at[:, pl.ds(0, HALO), pl.ds(0, HALO)], canvas(top, HALO, rim_at[dc], HALO),
                                         zero_sems.at[3 + 2 * side[dc] + k])
            blanks.append((need, copy))
            when(need, copy.start)

    def forward(part, dc):
        target = seam if dc == 1 else seam - 1
        return remote(passing.at[side[dc]], canvas(HALO + part * half, half, rim_at[-dc], HALO), (row, target),
                      pass_send.at[side[dc]], pass_recv.at[part])

    def relay(part, dc):
        when(r["relay"][part], landed(passing.at[side[dc]], seam_recv.at[side[dc]]).wait, forward(part, dc).start)

    relay(0, -1)
    relay(1, 1)
    corners = {}
    for dc in (-1, 1):
        i = side[dc]
        strip = canvas(outer_at, HALO, HALO + edge_from[dc], HALO)
        give = jnp.logical_and(r["has_outer"], r["has"][dc])
        corners[dc] = (give, remote(strip, canvas(outer_at, HALO, rim_at[-dc], HALO), (row, col + dc),
                                    corner_send.at[i], corner_recv.at[1 - i]))
        when(r["has_outer"], landed(strip, row_recv.at[i]).wait)
        when(give, corners[dc][1].start)
    relay(0, 1)
    relay(1, -1)
    inside = {}
    for dc in (-1, 1):
        i = side[dc]
        near_mate = pl.multiple_of(inner_from + HALO, HALO)
        when(r["near"][dc], landed(canvas(HALO, cells, rim_at[dc], HALO), col_recv.at[i]).wait)
        for part in range(2):
            when(r["at_seam"][dc], landed(canvas(HALO + part * half, half, rim_at[dc], HALO), pass_recv.at[part]).wait)
        inside[dc] = remote(canvas(near_mate, HALO, rim_at[dc], HALO), canvas(outer_at_of_mate(inner_at, cells), HALO, rim_at[dc], HALO),
                            r["mate"], corner_send.at[2 + i], corner_recv.at[2 + i])
        when(r["has"][dc], inside[dc].start)

    inner.wait_send()
    landed(canvas(inner_at, HALO, HALO, cells), row_recv.at[3]).wait()
    when(r["has_outer"], *[copy.wait_send for copy in outers])
    when(r["has_outer"], landed(canvas(outer_at, HALO, HALO + strips[2][0], strips[2][1]), row_recv.at[2]).wait)
    for dc in (-1, 1):
        i = side[dc]
        when(r["near"][dc], edges[dc].wait_send)
        when(r["at_seam"][dc], seams[dc][0].wait_send, seams[dc][1].wait_send)
        for part in range(2):
            when(r["relay"][part], forward(part, dc).wait_send)
        when(corners[dc][0], corners[dc][1].wait_send, landed(canvas(outer_at, HALO, rim_at[dc], HALO), corner_recv.at[i]).wait)
        when(r["has"][dc], inside[dc].wait_send, landed(canvas(inner_at, HALO, rim_at[dc], HALO), corner_recv.at[2 + i]).wait)
    for cond, copy in blanks:
        when(cond, copy.wait)
    own.wait()


def outer_at_of_mate(at, cells):
    return pl.multiple_of(cells + HALO - at, HALO)


def exchange_halo(obj, limits):
    cells = obj.shape[1]
    dma = pltpu.SemaphoreType.DMA
    return pl.pallas_call(
        functools.partial(halo_kernel, limits),
        out_shape=jax.ShapeDtypeStruct((2, cells + 2 * HALO, cells + 2 * HALO), F32),
        in_specs=[pl.BlockSpec(memory_space=pl.ANY)],
        out_specs=pl.BlockSpec(memory_space=pl.ANY),
        scratch_shapes=[
            pltpu.VMEM((2, cells, cells), F32),
            pltpu.VMEM((2, cells, cells + 2 * HALO), F32),
            pltpu.VMEM((2, 2, cells // 2, HALO), F32),
            dma, dma, dma((7,)), dma((4,)), dma((4,)), dma((2,)), dma((2,)), dma((2,)), dma((2,)), dma((2,)), dma((2,)),
            dma((4,)), dma((4,)),
        ],
        compiler_params=pltpu.CompilerParams(collective_id=0, has_side_effects=True, vmem_limit_bytes=60 * 2**20),
    )(obj)


def place():
    return lax.axis_index("row"), lax.axis_index("col")


def remote(src, dst, device, send, recv):
    return pltpu.make_async_remote_copy(src_ref=src, dst_ref=dst, send_sem=send, recv_sem=recv,
                                        device_id=device, device_id_type=MESH)


def landed(ref, sem):
    return pltpu.make_async_copy(ref, ref, sem)


def roles(limits):
    row, col = place()
    rows, cols = limits
    core = row % 2
    seam = cols // 2
    up, down = row > 0, row < rows - 1
    outer = jnp.where(core == 0, row - 1, row + 1)
    has_outer = jnp.logical_and(outer >= 0, outer < rows)
    near = {-1: jnp.logical_and(col > 0, col != seam), 1: jnp.logical_and(col < cols - 1, col != seam - 1)}
    at_seam = {-1: col == seam, 1: col == seam - 1}
    has = {-1: col > 0, 1: col < cols - 1}
    relay = {0: col == cols - 1, 1: col == 0}
    return dict(row=row, col=col, core=core, mate=(row + 1 - 2 * core, col), outer=(outer, col), has_outer=has_outer,
                near=near, at_seam=at_seam, has=has, relay=relay, seam=seam, cols=cols)


def greet(r):
    barrier = pltpu.get_barrier_semaphore()
    row, col, cols, seam = r["row"], r["col"], r["cols"], r["seam"]
    seam_any = jnp.logical_or(r["at_seam"][-1], r["at_seam"][1])
    relay_any = jnp.logical_or(r["relay"][0], r["relay"][1])
    pl.semaphore_signal(barrier, inc=1, device_id=r["mate"], device_id_type=MESH)
    total = jnp.int32(1)

    def to(cond, device):
        @pl.when(cond)
        def _():
            pl.semaphore_signal(barrier, inc=1, device_id=device, device_id_type=MESH)

        return cond.astype(jnp.int32)

    total += to(r["has_outer"], r["outer"])
    for dc in (-1, 1):
        total += to(r["has"][dc], (row, col + dc))
    for target in (0, cols - 1):
        total += to(seam_any, (row, target))
    for target in (seam - 1, seam):
        total += to(relay_any, (row, target))
    return barrier, total


def when(cond, *actions):
    @pl.when(cond)
    def _():
        for action in actions:
            action()


def halo_kernel(limits, source_ref, canvas_ref, obj_ref, zeros, passing, load_sem, own_sem, zero_sems, row_send, row_recv, col_send, col_recv,
                seam_send, seam_recv, pass_send, pass_recv, corner_send, corner_recv):
    cells = obj_ref.shape[1]
    half = cells // 2
    load = pltpu.make_async_copy(source_ref, obj_ref, load_sem)
    load.start()
    r = roles(limits)
    row, col, core, seam, cols = r["row"], r["col"], r["core"], r["seam"], r["cols"]
    barrier, total = greet(r)
    own = pltpu.make_async_copy(obj_ref, canvas_ref.at[:, pl.ds(HALO, cells), pl.ds(HALO, cells)], own_sem)
    zeros[...] = jnp.zeros_like(zeros)
    load.wait()
    own.start()
    pl.semaphore_wait(barrier, total)

    outer_from = pl.multiple_of(jnp.where(core == 0, 0, cells - HALO), HALO)
    inner_from = pl.multiple_of(jnp.where(core == 0, cells - HALO, 0), HALO)
    outer_at = pl.multiple_of(jnp.where(core == 0, 0, cells + HALO), HALO)
    inner_at = pl.multiple_of(jnp.where(core == 0, cells + HALO, 0), HALO)
    strips = ((0, HALO), (cells - HALO, HALO), (HALO, cells - 2 * HALO))
    edge_from = {-1: 0, 1: cells - HALO}
    rim_at = {-1: 0, 1: cells + HALO}
    side = {-1: 0, 1: 1}

    def canvas(top, tall, left, wide):
        return canvas_ref.at[:, pl.ds(top, tall), pl.ds(left, wide)]

    def tile(top, tall, left, wide):
        return obj_ref.at[:, pl.ds(top, tall), pl.ds(left, wide)]

    edges = {}
    seams = {}
    for dc in (-1, 1):
        edges[dc] = remote(tile(0, cells, edge_from[dc], HALO), canvas(HALO, cells, rim_at[-dc], HALO), (row, col + dc),
                           col_send.at[side[dc]], col_recv.at[side[-dc]])
        when(r["near"][dc], edges[dc].start)
        pair = []
        for part, target in ((0, cols - 1), (1, 0)):
            pair.append(remote(tile(part * half, half, edge_from[dc], HALO), passing.at[side[dc]], (row, target),
                               seam_send.at[part], seam_recv.at[side[dc]]))
        seams[dc] = pair
        when(r["at_seam"][dc], pair[0].start, pair[1].start)

    inner = remote(tile(inner_from, HALO, 0, cells), canvas(outer_at_of_mate(inner_at, cells), HALO, HALO, cells), r["mate"],
                   row_send.at[3], row_recv.at[3])
    inner.start()
    outers = []
    for i, (left, wide) in enumerate(strips):
        copy = remote(tile(outer_from, HALO, left, wide), canvas(outer_at_of_mate(outer_at, cells), HALO, HALO + left, wide), r["outer"],
                      row_send.at[i], row_recv.at[i])
        outers.append(copy)
        when(r["has_outer"], copy.start)
    blanks = []
    for i, (cond, ref) in enumerate((
        (jnp.logical_not(r["has_outer"]), canvas(outer_at, HALO, 0, cells + 2 * HALO)),
        (jnp.logical_not(r["has"][-1]), canvas(HALO, cells, 0, HALO)),
        (jnp.logical_not(r["has"][1]), canvas(HALO, cells, cells + HALO, HALO)),
    )):
        source = zeros.at[:, pl.ds(0, HALO), :] if i == 0 else zeros.at[:, pl.ds(0, cells), pl.ds(0, HALO)]
        copy = pltpu.make_async_copy(source, ref, zero_sems.at[i])
        blanks.append((cond, copy))
        when(cond, copy.start)
    for dc in (-1, 1):
        for k, top in ((0, inner_at), (1, outer_at)):
            need = jnp.logical_not(r["has"][dc])
            if k:
                need = jnp.logical_and(need, r["has_outer"])
            copy = pltpu.make_async_copy(zeros.at[:, pl.ds(0, HALO), pl.ds(0, HALO)], canvas(top, HALO, rim_at[dc], HALO),
                                         zero_sems.at[3 + 2 * side[dc] + k])
            blanks.append((need, copy))
            when(need, copy.start)

    def forward(part, dc):
        target = seam if dc == 1 else seam - 1
        return remote(passing.at[side[dc]], canvas(HALO + part * half, half, rim_at[-dc], HALO), (row, target),
                      pass_send.at[side[dc]], pass_recv.at[part])

    def relay(part, dc):
        when(r["relay"][part], landed(passing.at[side[dc]], seam_recv.at[side[dc]]).wait, forward(part, dc).start)

    relay(0, -1)
    relay(1, 1)
    corners = {}
    for dc in (-1, 1):
        i = side[dc]
        strip = canvas(outer_at, HALO, HALO + edge_from[dc], HALO)
        give = jnp.logical_and(r["has_outer"], r["has"][dc])
        corners[dc] = (give, remote(strip, canvas(outer_at, HALO, rim_at[-dc], HALO), (row, col + dc),
                                    corner_send.at[i], corner_recv.at[1 - i]))
        when(r["has_outer"], landed(strip, row_recv.at[i]).wait)
        when(give, corners[dc][1].start)
    relay(0, 1)
    relay(1, -1)
    inside = {}
    for dc in (-1, 1):
        i = side[dc]
        near_mate = pl.multiple_of(inner_from + HALO, HALO)
        when(r["near"][dc], landed(canvas(HALO, cells, rim_at[dc], HALO), col_recv.at[i]).wait)
        for part in range(2):
            when(r["at_seam"][dc], landed(canvas(HALO + part * half, half, rim_at[dc], HALO), pass_recv.at[part]).wait)
        inside[dc] = remote(canvas(near_mate, HALO, rim_at[dc], HALO), canvas(outer_at_of_mate(inner_at, cells), HALO, rim_at[dc], HALO),
                            r["mate"], corner_send.at[2 + i], corner_recv.at[2 + i])
        when(r["has"][dc], inside[dc].start)

    inner.wait_send()
    landed(canvas(inner_at, HALO, HALO, cells), row_recv.at[3]).wait()
    when(r["has_outer"], *[copy.wait_send for copy in outers])
    when(r["has_outer"], landed(canvas(outer_at, HALO, HALO + strips[2][0], strips[2][1]), row_recv.at[2]).wait)
    for dc in (-1, 1):
        i = side[dc]
        when(r["near"][dc], edges[dc].wait_send)
        when(r["at_seam"][dc], seams[dc][0].wait_send, seams[dc][1].wait_send)
        for part in range(2):
            when(r["relay"][part], forward(part, dc).wait_send)
        when(corners[dc][0], corners[dc][1].wait_send, landed(canvas(outer_at, HALO, rim_at[dc], HALO), corner_recv.at[i]).wait)
        when(r["has"][dc], inside[dc].wait_send, landed(canvas(inner_at, HALO, rim_at[dc], HALO), corner_recv.at[2 + i]).wait)
    for cond, copy in blanks:
        when(cond, copy.wait)
    own.wait()


def outer_at_of_mate(at, cells):
    return pl.multiple_of(cells + HALO - at, HALO)


def exchange_halo(obj, limits):
    cells = obj.shape[1]
    dma = pltpu.SemaphoreType.DMA
    return pl.pallas_call(
        functools.partial(halo_kernel, limits),
        out_shape=jax.ShapeDtypeStruct((2, cells + 2 * HALO, cells + 2 * HALO), F32),
        in_specs=[pl.BlockSpec(memory_space=pl.ANY)],
        out_specs=pl.BlockSpec(memory_space=pl.ANY),
        scratch_shapes=[
            pltpu.VMEM((2, cells, cells), F32),
            pltpu.VMEM((2, cells, cells + 2 * HALO), F32),
            pltpu.VMEM((2, 2, cells // 2, HALO), F32),
            dma, dma, dma((7,)), dma((4,)), dma((4,)), dma((2,)), dma((2,)), dma((2,)), dma((2,)), dma((2,)), dma((2,)),
            dma((4,)), dma((4,)),
        ],
        compiler_params=pltpu.CompilerParams(collective_id=0, has_side_effects=True, vmem_limit_bytes=60 * 2**20),
    )(obj)


SIDES = [(-1, 0), (1, 0), (0, -1), (0, 1), (-1, -1), (-1, 1), (1, -1), (1, 1)]


ORDERS = [(0, 1, 2), (1, 2, 0), (2, 0, 1), (1, 0, 2)]


def spots():
    row, col = place()
    return (row // 2 % 2 * 2 + col // 4, row // 4, col % 4)


def along(axis, by):
    row, col = place()
    at = list(spots())
    at[axis] = (at[axis] + by) % 4
    return (at[1] * 4 + at[0] // 2 * 2 + row % 2, at[0] % 2 * 4 + at[2])


def finish_kernel(limits, spread_ref, pg_ref, energy_ref, obj_ref, probe_ref, illum_ref,
                  onew_ref, pnew_ref, land_rows, land_cols, land_inner, land_outer, out_cols, out_ends, passing, total_ref, mate_half, mate_energy, warm, heat,
                  box1, box2, box3, seam_send, seam_recv, pass_send, pass_recv, near_send, near_recv, row_send, row_recv,
                  corner_send, corner_recv, mate_send, mate_recv, down_send, down_recv, up_send, up_recv,
                  heat_send, heat_recv):
    cells = obj_ref.shape[1]
    row, col = place()
    core = row % 2
    mate = (row + 1 - 2 * core, col)
    at = spots()
    units = len(ORDERS)
    unit = pg_ref.shape[1] // units

    r = roles(limits)
    barrier, total = greet(r)
    pl.semaphore_signal(barrier, inc=1, device_id=mate, device_id_type=MESH)
    for axis in range(3):
        for by in (1, 2, 3):
            pl.semaphore_signal(barrier, inc=1, device_id=along(axis, by), device_id_type=MESH)
    pl.semaphore_wait(barrier, total + 10)

    firsts = [remote(energy_ref, mate_energy, mate, mate_send.at[0], mate_recv.at[0])]
    for u in range(units):
        rows = pl.ds(u * unit, unit)
        firsts.append(remote(pg_ref.at[1 - core, rows], mate_half.at[rows], mate, mate_send.at[1 + u], mate_recv.at[1 + u]))
    half = cells // 2
    seam, cols = r["seam"], r["cols"]
    outer_from = pl.multiple_of(jnp.where(core == 0, 0, cells - HALO), HALO)
    inner_from = pl.multiple_of(jnp.where(core == 0, cells - HALO, 0), HALO)
    outer_at = pl.multiple_of(jnp.where(core == 0, 0, cells + HALO), HALO)
    inner_at = pl.multiple_of(jnp.where(core == 0, cells + HALO, 0), HALO)
    edge_from = {-1: 0, 1: cells - HALO}
    rim_at = {-1: 0, 1: cells + HALO}
    side = {-1: 0, 1: 1}
    inside, nears, seams, ends, corners = {}, {}, {}, {}, {}

    def region(top, tall, left, wide):
        return spread_ref.at[:, pl.ds(top, tall), pl.ds(left, wide)]

    for dc in (-1, 1):
        i = side[dc]
        inside[dc] = remote(region(inner_at, HALO, rim_at[dc], HALO), land_inner.at[i], mate, corner_send.at[i], corner_recv.at[i])
        when(r["has"][dc], inside[dc].start)
    for copy in firsts:
        copy.start()
    for dc in (-1, 1):
        i = side[dc]

        @pl.when(r["has"][dc])
        def _(dc=dc, i=i):
            inside[dc].wait_recv()
            for part in range(2):
                out_cols[i, part] = spread_ref[part, HALO:HALO + cells, rim_at[dc]:rim_at[dc] + HALO]
                out_cols[i, part, pl.ds(inner_from, HALO), :] += land_inner[i, part]

        seams[dc] = [remote(out_cols.at[i, :, pl.ds(part * half, half), :], passing.at[i], (row, target),
                            seam_send.at[part], seam_recv.at[i]) for part, target in ((0, cols - 1), (1, 0))]
        when(r["at_seam"][dc], seams[dc][0].start, seams[dc][1].start)

    inner = remote(region(inner_at, HALO, HALO, cells), land_rows.at[1], mate, row_send.at[3], row_recv.at[3])
    middle = remote(region(outer_at, HALO, 2 * HALO, cells - 2 * HALO), land_rows.at[0, :, :, pl.ds(HALO, cells - 2 * HALO)], r["outer"],
                    row_send.at[2], row_recv.at[2])

    def start_fold():
        for dc in (-1, 1):
            i = side[dc]
            corners[dc] = (jnp.logical_and(r["has_outer"], r["has"][dc]),
                           remote(region(outer_at, HALO, rim_at[dc], HALO), land_outer.at[1 - i], (row, col + dc),
                                  corner_send.at[2 + i], corner_recv.at[3 - i]))
            when(corners[dc][0], corners[dc][1].start)
        when(r["has_outer"], middle.start)
        for dc in (-1, 1):
            i = side[dc]
            nears[dc] = remote(out_cols.at[i], land_cols.at[1 - i], (row, col + dc), near_send.at[i], near_recv.at[1 - i])
            when(r["near"][dc], nears[dc].start)
        inner.start()

    def forward(part, dc):
        i = side[dc]
        target = seam if dc == 1 else seam - 1
        return remote(passing.at[i], land_cols.at[1 - i, :, pl.ds(part * half, half), :], (row, target), pass_send.at[i], pass_recv.at[part])

    def relay(part, dc):
        when(r["relay"][part], landed(passing.at[side[dc]], seam_recv.at[side[dc]]).wait, forward(part, dc).start)

    def send_ends():
        for dc in (-1, 1):
            i = side[dc]
            ends[dc] = remote(out_ends.at[i], land_rows.at[0, :, :, pl.ds(edge_from[dc], HALO)], r["outer"], row_send.at[i], row_recv.at[i])

            @pl.when(r["has_outer"])
            def _(dc=dc, i=i):
                left = HALO + edge_from[dc]
                for part in range(2):
                    out_ends[i, part] = spread_ref[part, pl.ds(outer_at, HALO), left:left + HALO]

                @pl.when(r["has"][dc])
                def _():
                    landed(land_outer.at[i], corner_recv.at[2 + i]).wait()
                    for part in range(2):
                        out_ends[i, part] += land_outer[i, part]

                ends[dc].start()

    def piece(u, depth, spot):
        order = ORDERS[u]
        start = u * unit
        if depth == 1:
            return pl.ds(pl.multiple_of(start + spot * (unit // 4), unit // 4), unit // 4), slice(None)
        start = start + at[order[0]] * (unit // 4)
        if depth == 2:
            return pl.ds(pl.multiple_of(start + spot * (unit // 16), unit // 16), unit // 16), slice(None)
        start = start + at[order[1]] * (unit // 16)
        return (pl.ds(pl.multiple_of(start + spot // 2 * 8, 8), 8), pl.ds(pl.multiple_of(spot % 2 * 128, 128), 128))

    def own(u, depth):
        return piece(u, depth, at[ORDERS[u][depth - 1]])

    boxes = (box1, box2, box3)
    waiting = []

    def down(u, depth):
        axis = ORDERS[u][depth - 1]
        out = []
        for by in (1, 2, 3):
            copy = remote(total_ref.at[piece(u, depth, (at[axis] + by) % 4)], boxes[depth - 1].at[u, by - 1], along(axis, by),
                          down_send.at[u, depth - 1, by - 1], down_recv.at[u, depth - 1, by - 1])
            copy.start()
            out.append(copy)
        waiting.extend(out)
        return out

    def pass_heat(axis):
        out = []
        for by in (1, 2, 3):
            copy = remote(warm.at[axis], heat.at[axis, by - 1], along(axis, by), heat_send.at[axis, by - 1], heat_recv.at[axis, by - 1])
            copy.start()
            out.append(copy)
        waiting.extend(out)
        return out

    firsts[0].wait_recv()
    warm[0] = energy_ref[...] + mate_energy[...]
    hot = pass_heat(0)
    flying = []
    for u in range(units):
        rows = pl.ds(u * unit, unit)
        firsts[1 + u].wait_recv()
        total_ref[rows, :] = pg_ref[core, rows, :] + mate_half[rows, :]
        flying.append(down(u, 1))
    waiting.extend(firsts)
    start_fold()

    share = 1.0 / illum_ref[0]
    step_rows = 64

    def base(j, c):
        r = pl.ds(pl.multiple_of(j * step_rows, step_rows), step_rows)
        rr = pl.ds(pl.multiple_of(j * step_rows + HALO, step_rows), step_rows)
        for part in range(2):
            onew_ref[part, r, :] = obj_ref[part, r, :] + spread_ref[part, rr, HALO:HALO + cells] * share
        return c

    lax.fori_loop(0, cells // step_rows, base, 0)
    relay(0, -1)
    relay(1, 1)

    for depth in (1, 2, 3):
        if depth == 2:
            send_ends()
        if depth == 3:
            relay(0, 1)
            relay(1, -1)
        for copy in hot:
            copy.wait_recv()
        fresh = warm[depth - 1] + heat[depth - 1, 0] + heat[depth - 1, 1] + heat[depth - 1, 2]
        if depth < 3:
            warm[depth] = fresh
            hot = pass_heat(depth)
        for u in range(units):
            for copy in flying[u]:
                copy.wait_recv()
            box = boxes[depth - 1]
            where = own(u, depth)
            summed = total_ref[where] + box[u, 0] + box[u, 1] + box[u, 2]
            if depth < 3:
                total_ref[where] = summed
                flying[u] = down(u, depth + 1)
            else:
                pnew_ref[(core,) + where] = probe_ref[(core,) + where] + summed / (fresh[:, :128] + EPSILON)

    def up(u, depth):
        axis = ORDERS[u][depth - 1]
        spot = pnew_ref.at[(core,) + own(u, depth)]
        out = []
        for by in (1, 2, 3):
            landed = pnew_ref.at[(core,) + piece(u, depth, (at[axis] + 4 - by) % 4)]
            copy = remote(spot, spot, along(axis, by), up_send.at[u, depth - 1, by - 1], up_recv.at[u, depth - 1, by - 1])
            copy.start()
            waiting.append(copy)
            out.append(pltpu.make_async_copy(landed, landed, up_recv.at[u, depth - 1, by - 1]))
        return out

    for u in range(units):
        flying[u] = up(u, 3)
    lasts = []
    for depth in (3, 2, 1):
        for u in range(units):
            for copy in flying[u]:
                copy.wait()
            if depth > 1:
                flying[u] = up(u, depth - 1)
            else:
                rows = pl.ds(u * unit, unit)
                done = pnew_ref.at[core, rows]
                copy = remote(done, done, mate, mate_send.at[5 + u], mate_recv.at[5 + u])
                copy.start()
                waiting.append(copy)
                got = pnew_ref.at[1 - core, rows]
                lasts.append(pltpu.make_async_copy(got, got, mate_recv.at[5 + u]))

    inner.wait()
    for part in range(2):
        onew_ref[part, pl.ds(inner_from, HALO), :] += land_rows[1, part] * share

    @pl.when(r["has_outer"])
    def _():
        middle.wait()
        for dc in (-1, 1):
            ends[dc].wait()
        for part in range(2):
            onew_ref[part, pl.ds(outer_from, HALO), :] += land_rows[0, part] * share

    for dc in (-1, 1):
        i = side[dc]
        when(r["near"][dc], nears[dc].wait_send, landed(land_cols.at[i], near_recv.at[i]).wait)
        when(r["at_seam"][dc], seams[dc][0].wait_send, seams[dc][1].wait_send)
        for part in range(2):
            when(r["at_seam"][dc], landed(land_cols.at[i, :, pl.ds(part * half, half), :], pass_recv.at[part]).wait)
            when(r["relay"][part], forward(part, dc).wait_send)
        when(corners[dc][0], corners[dc][1].wait_send)

        @pl.when(r["has"][dc])
        def _(dc=dc, i=i):
            inside[dc].wait_send()
            for part in range(2):
                onew_ref[part, :, edge_from[dc]:edge_from[dc] + HALO] += land_cols[i, part] * share

    for copy in lasts:
        copy.wait()
    for copy in waiting:
        copy.wait_send()


def finish(spread, pg, energy, obj, probe, illum, limits):
    cells = obj.shape[1]
    rows, lanes = probe.shape[1], probe.shape[2]
    units = len(ORDERS)
    unit = rows // units
    vmem = pl.BlockSpec(memory_space=pltpu.VMEM)
    dma = pltpu.SemaphoreType.DMA
    return pl.pallas_call(
        functools.partial(finish_kernel, limits),
        out_shape=(jax.ShapeDtypeStruct(obj.shape, F32), jax.ShapeDtypeStruct(probe.shape, F32)),
        in_specs=[vmem, vmem, vmem, vmem, vmem, pl.BlockSpec(memory_space=pltpu.SMEM)],
        out_specs=(vmem, vmem),
        scratch_shapes=[
            pltpu.VMEM((2, 2, HALO, cells), F32),
            pltpu.VMEM((2, 2, cells, HALO), F32),
            pltpu.VMEM((2, 2, HALO, HALO), F32),
            pltpu.VMEM((2, 2, HALO, HALO), F32),
            pltpu.VMEM((2, 2, cells, HALO), F32),
            pltpu.VMEM((2, 2, HALO, HALO), F32),
            pltpu.VMEM((2, 2, cells // 2, HALO), F32),
            pltpu.VMEM((rows, lanes), F32),
            pltpu.VMEM((rows, lanes), F32),
            pltpu.VMEM((8, 128), F32),
            pltpu.VMEM((3, 8, 128), F32),
            pltpu.VMEM((3, 3, 8, 128), F32),
            pltpu.VMEM((units, 3, unit // 4, lanes), F32),
            pltpu.VMEM((units, 3, unit // 16, lanes), F32),
            pltpu.VMEM((units, 3, 8, 128), F32),
            dma((2,)), dma((2,)), dma((2,)), dma((2,)), dma((2,)), dma((2,)), dma((4,)), dma((4,)), dma((4,)), dma((4,)),
            dma((9,)), dma((9,)),
            dma((units, 3, 3)), dma((units, 3, 3)), dma((units, 3, 3)), dma((units, 3, 3)),
            dma((3, 3)), dma((3, 3)),
        ],
        compiler_params=pltpu.CompilerParams(collective_id=1, has_side_effects=True, vmem_limit_bytes=60 * 2**20),
    )(spread, pg, energy, obj, probe, illum)


def body(limits, object_field, probe, amplitudes, positions, counts):
    canvas = exchange_halo(object_field, limits)
    spread, probe_grad, shift, energy, illum = step(positions[0, 0], counts[0], canvas, probe, amplitudes[0, 0])
    n = probe.shape[2]
    flat = (2, probe.shape[1] * n, n)
    object_new, probe_new = finish(spread, probe_grad.reshape(flat), energy, object_field, probe.reshape(flat), illum, limits)
    return (object_new, probe_new.reshape(probe.shape), shift[None, None])


def solution(mesh):
    return jax.shard_map(
        functools.partial(body, (mesh.shape["row"], mesh.shape["col"])),
        mesh=mesh,
        in_specs=(
            P(None, "row", "col"),
            P(),
            P("row", "col", None, None, None),
            P("row", "col", None, None),
            P("row", "col"),
        ),
        out_specs=(P(None, "row", "col"), P(), P("row", "col", None, None)),
        check_vma=False,
    )
```

```python
import functools
import math

import ml_dtypes
import numpy as np
import jax
import jax.numpy as jnp
from jax import lax
from jax.experimental import pallas as pl
from jax.experimental.pallas import tpu as pltpu
from jax.sharding import PartitionSpec as P

HALO = 128
INTENSITY_FLOOR = 0.1
EPSILON = 1e-06
F32 = jnp.float32
BF16 = jnp.bfloat16
UNROLL = 4


def dft_tables(pixels):
    half = pixels // 2
    k = np.arange(half)[:, None]
    n = np.arange(half)[None, :]
    out = []
    for parity in (0, 1):
        angle = (n * (2 * k + parity) % pixels) * (2.0 * math.pi / pixels)
        c = np.cos(angle) / math.sqrt(pixels)
        s = np.sin(angle) / math.sqrt(pixels)
        out.append(np.block([[c, s], [-s, c]]))
    both = []
    for m in (out[0], out[1], out[0].T, out[1].T):
        m = m.astype(np.float32)
        hi = m.astype(ml_dtypes.bfloat16)
        lo = (m - hi.astype(np.float32)).astype(ml_dtypes.bfloat16)
        both.append(np.stack([hi, lo]))
    return np.stack(both)


def parity_table(pixels):
    half = pixels // 2
    t = np.zeros((pixels, pixels), np.float32)
    for j in range(half):
        t[2 * j, j] = 1.0
        t[2 * j + 1, half + j] = 1.0
    return t.astype(ml_dtypes.bfloat16)


def split(x):
    hi = x.astype(BF16)
    return hi, (x - hi.astype(F32)).astype(BF16)


def mm(a, b):
    return jnp.dot(a, b, preferred_element_type=F32)


def from_left(table, x):
    hi, lo = split(x)
    return mm(jnp.concatenate([table[0], table[0], table[1]], 1), jnp.concatenate([hi, lo, hi], 0))


def from_right(x, table):
    hi, lo = split(x)
    return mm(jnp.concatenate([hi, lo, hi], 1), jnp.concatenate([table[0], table[0], table[1]], 0))


def lane_of():
    return lax.broadcasted_iota(jnp.int32, (1, 8, 128), 2)


def row_of():
    return lax.broadcasted_iota(jnp.int32, (1, 8, 128), 1)


def cut(canvas_ref, patch, a, b):
    n = patch.shape[1]
    groups = n // 8
    t, u = b % 128, a % 8
    row = pl.multiple_of(a - u, 8)
    lane, sub = lane_of(), row_of()
    power = jnp.zeros((8, 128), F32)
    for part in range(2):
        blocks = []
        for j in range(n // 128 + 1):
            v = canvas_ref[part, pl.ds(row, n + 8), pl.ds(pl.multiple_of(b - t + j * 128, 128), 128)]
            v = pltpu.roll(v.reshape(groups + 1, 8, 128), (8 - u) % 8, 1)
            v = jnp.where(sub < 8 - u, v[:groups], v[1:])
            blocks.append(pltpu.roll(v, (128 - t) % 128, 2))
        for j in range(n // 128):
            p = jnp.where(lane < 128 - t, blocks[j], blocks[j + 1])
            power += jnp.sum(p * p, axis=0)
            patch[part, :, j * 128:(j + 1) * 128] = p.reshape(n, 128)
    return power


def lay(canvas_ref, spread_ref, grad, a, b):
    n = grad.shape[1]
    groups = n // 8
    count = n // 128
    t, u = b % 128, a % 8
    row = pl.multiple_of(a - u, 8)
    before = pl.multiple_of(jnp.maximum(a - u - 8, 0), 8)
    lane, sub = lane_of(), row_of()
    down = jnp.zeros((8, 128), F32)
    across = jnp.zeros((8, 128), F32)
    none = jnp.zeros((1, 8, 128), F32)
    for part in range(2):
        turned = [pltpu.roll(grad[part, :, j * 128:(j + 1) * 128].reshape(groups, 8, 128), t, 2) for j in range(count)]
        strips = []
        for j in range(-1, count + 1):
            at = pl.multiple_of(jnp.maximum(b - t + j * 128, 0), 128)
            strips.append(canvas_ref[part, pl.ds(row, n + 8), pl.ds(at, 128)].reshape(groups + 1, 8, 128))
        for j in range(count + 1):
            left = turned[j - 1] if j else 0.0
            g = jnp.where(lane < t, left, turned[j] if j < count else 0.0)
            g = pltpu.roll(g, u, 1)
            g = jnp.where(sub < u, jnp.concatenate([none, g], 0), jnp.concatenate([g, none], 0))
            at = pl.ds(pl.multiple_of(b - t + j * 128, 128), 128)
            spread_ref[part, pl.ds(row, n + 8), at] += g.reshape(n + 8, 128)
            v = strips[j + 1]
            first = canvas_ref[part, pl.ds(before, 8), at].reshape(1, 8, 128)
            nxt = pltpu.roll(v, 7, 1)
            prv = pltpu.roll(jnp.concatenate([first, v], 0), 1, 1)
            nxt = jnp.where(sub < 7, nxt, jnp.concatenate([nxt[1:], none], 0))
            prv = jnp.where(sub < 1, prv[:-1], prv[1:])
            down += jnp.sum(g * (nxt - prv), axis=0)
            nxt = pltpu.roll(v, 127, 2)
            prv = pltpu.roll(v, 1, 2)
            if j < count:
                nxt = jnp.where(lane < 127, nxt, pltpu.roll(strips[j + 2], 127, 2))
            prv = jnp.where(lane < 1, pltpu.roll(strips[j], 1, 2), prv)
            across += jnp.sum(g * (nxt - prv), axis=0)
    return down, across


def step_kernel(pos_ref, count_ref, canvas_ref, probe_ref, amp_ref, tab_ref,
                spread_ref, pg_ref, shift_ref, energy_ref, illum_ref,
                patch, far, inten, grad, sums):
    n = probe_ref.shape[2]
    h = n // 2
    modes = probe_ref.shape[1]
    slots = amp_ref.shape[0]
    spread_ref[...] = jnp.zeros_like(spread_ref)
    pg_ref[...] = jnp.zeros_like(pg_ref)
    sums[...] = jnp.zeros_like(sums)
    light = jnp.zeros((n, n), F32)
    for k in range(modes):
        for part in range(2):
            light += probe_ref[part, k] * probe_ref[part, k]
    illum_ref[0] = jnp.max(light)

    def visit(s, carry):
        a = pos_ref[s, 0]
        b = pos_ref[s, 1]
        sums[s, 2] = cut(canvas_ref, patch, a, b)

        inten[...] = jnp.zeros_like(inten)

        def forward(k, c):
            pr, pi = probe_ref[0, k], probe_ref[1, k]
            pr_, pi_ = patch[0], patch[1]
            er = pr * pr_ - pi * pi_
            ei = pr * pi_ + pi * pr_
            up = jnp.concatenate([er[:h] + er[h:], ei[:h] + ei[h:]], 0)
            dn = jnp.concatenate([er[:h] - er[h:], ei[:h] - ei[h:]], 0)
            su = from_left(tab_ref[0], up)
            sd = from_left(tab_ref[1], dn)
            zr = jnp.concatenate([su[:h], sd[:h]], 0)
            zi = jnp.concatenate([su[h:], sd[h:]], 0)
            lf = jnp.concatenate([zr[:, :h] + zr[:, h:], zi[:, :h] + zi[:, h:]], 1)
            rt = jnp.concatenate([zr[:, :h] - zr[:, h:], zi[:, :h] - zi[:, h:]], 1)
            fa = from_right(lf, tab_ref[2])
            fb = from_right(rt, tab_ref[3])
            far[k, 0] = fa
            far[k, 1] = fb
            inten[:, :h] += fa[:, :h] * fa[:, :h] + fa[:, h:] * fa[:, h:]
            inten[:, h:] += fb[:, :h] * fb[:, :h] + fb[:, h:] * fb[:, h:]
            return c

        lax.fori_loop(0, modes, forward, 0, unroll=UNROLL)
        inten[...] = amp_ref[s] * lax.rsqrt(jnp.maximum(inten[...], INTENSITY_FLOOR)) - 1.0
        grad[...] = jnp.zeros_like(grad)

        def backward(k, c):
            ma, mb = inten[:, :h], inten[:, h:]
            e = from_right(far[k, 0] * jnp.concatenate([ma, ma], 1), tab_ref[0])
            o = from_right(far[k, 1] * jnp.concatenate([mb, mb], 1), tab_ref[1])
            lo = e + o
            hi = e - o
            ev = jnp.concatenate([jnp.concatenate([lo[:h, :h], hi[:h, :h]], 1),
                                  jnp.concatenate([lo[:h, h:], hi[:h, h:]], 1)], 0)
            od = jnp.concatenate([jnp.concatenate([lo[h:, :h], hi[h:, :h]], 1),
                                  jnp.concatenate([lo[h:, h:], hi[h:, h:]], 1)], 0)
            e2 = from_left(tab_ref[2], ev)
            o2 = from_left(tab_ref[3], od)
            for r, half in ((slice(0, h), e2 + o2), (slice(h, n), e2 - o2)):
                cr, ci = half[:h], half[h:]
                pr, pi = probe_ref[0, k, r], probe_ref[1, k, r]
                qr, qi = patch[0, r], patch[1, r]
                grad[0, r] += pr * cr + pi * ci
                grad[1, r] += pr * ci - pi * cr
                pg_ref[0, k, r] += qr * cr + qi * ci
                pg_ref[1, k, r] += qr * ci - qi * cr
            return c

        lax.fori_loop(0, modes, backward, 0, unroll=UNROLL)
        down, across = lay(canvas_ref, spread_ref, grad, a, b)
        sums[s, 0] = down
        sums[s, 1] = across
        return carry

    lax.fori_loop(0, count_ref[0], visit, 0)
    energy = jnp.zeros((8, 128), F32)
    for s in range(slots):
        energy += sums[s, 2]
        for kind in range(2):
            shift_ref[s, kind] = jnp.sum(sums[s, kind]) * (0.5 / n)
    energy_ref[...] = jnp.broadcast_to(jnp.sum(energy, keepdims=True) / (n * n), energy.shape)


def step(pos, count, canvas, probe, amp):
    n = probe.shape[2]
    modes = probe.shape[1]
    slots = amp.shape[0]
    rows = canvas.shape[1]
    vmem = pl.BlockSpec(memory_space=pltpu.VMEM)
    smem = pl.BlockSpec(memory_space=pltpu.SMEM)
    return pl.pallas_call(
        step_kernel,
        out_shape=(
            jax.ShapeDtypeStruct((2, rows, rows), F32),
            jax.ShapeDtypeStruct(probe.shape, F32),
            jax.ShapeDtypeStruct((slots, 2), F32),
            jax.ShapeDtypeStruct((8, 128), F32),
            jax.ShapeDtypeStruct((1,), F32),
        ),
        in_specs=[smem, smem, vmem, vmem, vmem, vmem],
        out_specs=(vmem, vmem, smem, vmem, smem),
        scratch_shapes=[
            pltpu.VMEM((2, n, n), F32),
            pltpu.VMEM((modes, 2, n, n), F32),
            pltpu.VMEM((n, n), F32),
            pltpu.VMEM((2, n, n), F32),
            pltpu.VMEM((slots, 3, 8, 128), F32),
        ],
        compiler_params=pltpu.CompilerParams(vmem_limit_bytes=60 * 2**20),
    )(pos, count, canvas, probe, amp, jnp.asarray(dft_tables(n)))


MESH = pl.DeviceIdType.MESH


def place():
    return lax.axis_index("row"), lax.axis_index("col")


def remote(src, dst, device, send, recv):
    return pltpu.make_async_remote_copy(src_ref=src, dst_ref=dst, send_sem=send, recv_sem=recv,
                                        device_id=device, device_id_type=MESH)


def landed(ref, sem):
    return pltpu.make_async_copy(ref, ref, sem)


def roles(limits):
    row, col = place()
    rows, cols = limits
    core = row % 2
    seam = cols // 2
    up, down = row > 0, row < rows - 1
    outer = jnp.where(core == 0, row - 1, row + 1)
    has_outer = jnp.logical_and(outer >= 0, outer < rows)
    near = {-1: jnp.logical_and(col > 0, col != seam), 1: jnp.logical_and(col < cols - 1, col != seam - 1)}
    at_seam = {-1: col == seam, 1: col == seam - 1}
    has = {-1: col > 0, 1: col < cols - 1}
    relay = {0: col == cols - 1, 1: col == 0}
    return dict(row=row, col=col, core=core, mate=(row + 1 - 2 * core, col), outer=(outer, col), has_outer=has_outer,
                near=near, at_seam=at_seam, has=has, relay=relay, seam=seam, cols=cols)


def greet(r):
    barrier = pltpu.get_barrier_semaphore()
    row, col, cols, seam = r["row"], r["col"], r["cols"], r["seam"]
    seam_any = jnp.logical_or(r["at_seam"][-1], r["at_seam"][1])
    relay_any = jnp.logical_or(r["relay"][0], r["relay"][1])
    pl.semaphore_signal(barrier, inc=1, device_id=r["mate"], device_id_type=MESH)
    total = jnp.int32(1)

    def to(cond, device):
        @pl.when(cond)
        def _():
            pl.semaphore_signal(barrier, inc=1, device_id=device, device_id_type=MESH)

        return cond.astype(jnp.int32)

    total += to(r["has_outer"], r["outer"])
    for dc in (-1, 1):
        total += to(r["has"][dc], (row, col + dc))
    for target in (0, cols - 1):
        total += to(seam_any, (row, target))
    for target in (seam - 1, seam):
        total += to(relay_any, (row, target))
    return barrier, total


def when(cond, *actions):
    @pl.when(cond)
    def _():
        for action in actions:
            action()


def halo_kernel(limits, source_ref, canvas_ref, obj_ref, zeros, passing, load_sem, own_sem, zero_sems, row_send, row_recv, col_send, col_recv,
                seam_send, seam_recv, pass_send, pass_recv, corner_send, corner_recv):
    cells = obj_ref.shape[1]
    half = cells // 2
    load = pltpu.make_async_copy(source_ref, obj_ref, load_sem)
    load.start()
    r = roles(limits)
    row, col, core, seam, cols = r["row"], r["col"], r["core"], r["seam"], r["cols"]
    barrier, total = greet(r)
    own = pltpu.make_async_copy(obj_ref, canvas_ref.at[:, pl.ds(HALO, cells), pl.ds(HALO, cells)], own_sem)
    zeros[...] = jnp.zeros_like(zeros)
    load.wait()
    own.start()
    pl.semaphore_wait(barrier, total)

    outer_from = pl.multiple_of(jnp.where(core == 0, 0, cells - HALO), HALO)
    inner_from = pl.multiple_of(jnp.where(core == 0, cells - HALO, 0), HALO)
    outer_at = pl.multiple_of(jnp.where(core == 0, 0, cells + HALO), HALO)
    inner_at = pl.multiple_of(jnp.where(core == 0, cells + HALO, 0), HALO)
    strips = ((0, HALO), (cells - HALO, HALO), (HALO, cells - 2 * HALO))
    edge_from = {-1: 0, 1: cells - HALO}
    rim_at = {-1: 0, 1: cells + HALO}
    side = {-1: 0, 1: 1}

    def canvas(top, tall, left, wide):
        return canvas_ref.at[:, pl.ds(top, tall), pl.ds(left, wide)]

    def tile(top, tall, left, wide):
        return obj_ref.at[:, pl.ds(top, tall), pl.ds(left, wide)]

    edges = {}
    seams = {}
    for dc in (-1, 1):
        edges[dc] = remote(tile(0, cells, edge_from[dc], HALO), canvas(HALO, cells, rim_at[-dc], HALO), (row, col + dc),
                           col_send.at[side[dc]], col_recv.at[side[-dc]])
        when(r["near"][dc], edges[dc].start)
        pair = []
        for part, target in ((0, cols - 1), (1, 0)):
            pair.append(remote(tile(part * half, half, edge_from[dc], HALO), passing.at[side[dc]], (row, target),
                               seam_send.at[part], seam_recv.at[side[dc]]))
        seams[dc] = pair
        when(r["at_seam"][dc], pair[0].start, pair[1].start)

    inner = remote(tile(inner_from, HALO, 0, cells), canvas(outer_at_of_mate(inner_at, cells), HALO, HALO, cells), r["mate"],
                   row_send.at[3], row_recv.at[3])
    inner.start()
    outers = []
    for i, (left, wide) in enumerate(strips):
        copy = remote(tile(outer_from, HALO, left, wide), canvas(outer_at_of_mate(outer_at, cells), HALO, HALO + left, wide), r["outer"],
                      row_send.at[i], row_recv.at[i])
        outers.append(copy)
        when(r["has_outer"], copy.start)
    blanks = []
    for i, (cond, ref) in enumerate((
        (jnp.logical_not(r["has_outer"]), canvas(outer_at, HALO, 0, cells + 2 * HALO)),
        (jnp.logical_not(r["has"][-1]), canvas(HALO, cells, 0, HALO)),
        (jnp.logical_not(r["has"][1]), canvas(HALO, cells, cells + HALO, HALO)),
    )):
        source = zeros.at[:, pl.ds(0, HALO), :] if i == 0 else zeros.at[:, pl.ds(0, cells), pl.ds(0, HALO)]
        copy = pltpu.make_async_copy(source, ref, zero_sems.at[i])
        blanks.append((cond, copy))
        when(cond, copy.start)
    for dc in (-1, 1):
        for k, top in ((0, inner_at), (1, outer_at)):
            need = jnp.logical_not(r["has"][dc])
            if k:
                need = jnp.logical_and(need, r["has_outer"])
            copy = pltpu.make_async_copy(zeros.at[:, pl.ds(0, HALO), pl.ds(0, HALO)], canvas(top, HALO, rim_at[dc], HALO),
                                         zero_sems.at[3 + 2 * side[dc] + k])
            blanks.append((need, copy))
            when(need, copy.start)

    def forward(part, dc):
        target = seam if dc == 1 else seam - 1
        return remote(passing.at[side[dc]], canvas(HALO + part * half, half, rim_at[-dc], HALO), (row, target),
                      pass_send.at[side[dc]], pass_recv.at[part])

    def relay(part, dc):
        when(r["relay"][part], landed(passing.at[side[dc]], seam_recv.at[side[dc]]).wait, forward(part, dc).start)

    relay(0, -1)
    relay(1, 1)
    corners = {}
    for dc in (-1, 1):
        i = side[dc]
        strip = canvas(outer_at, HALO, HALO + edge_from[dc], HALO)
        give = jnp.logical_and(r["has_outer"], r["has"][dc])
        corners[dc] = (give, remote(strip, canvas(outer_at, HALO, rim_at[-dc], HALO), (row, col + dc),
                                    corner_send.at[i], corner_recv.at[1 - i]))
        when(r["has_outer"], landed(strip, row_recv.at[i]).wait)
        when(give, corners[dc][1].start)
    relay(0, 1)
    relay(1, -1)
    inside = {}
    for dc in (-1, 1):
        i = side[dc]
        near_mate = pl.multiple_of(inner_from + HALO, HALO)
        when(r["near"][dc], landed(canvas(HALO, cells, rim_at[dc], HALO), col_recv.at[i]).wait)
        for part in range(2):
            when(r["at_seam"][dc], landed(canvas(HALO + part * half, half, rim_at[dc], HALO), pass_recv.at[part]).wait)
        inside[dc] = remote(canvas(near_mate, HALO, rim_at[dc], HALO), canvas(outer_at_of_mate(inner_at, cells), HALO, rim_at[dc], HALO),
                            r["mate"], corner_send.at[2 + i], corner_recv.at[2 + i])
        when(r["has"][dc], inside[dc].start)

    inner.wait_send()
    landed(canvas(inner_at, HALO, HALO, cells), row_recv.at[3]).wait()
    when(r["has_outer"], *[copy.wait_send for copy in outers])
    when(r["has_outer"], landed(canvas(outer_at, HALO, HALO + strips[2][0], strips[2][1]), row_recv.at[2]).wait)
    for dc in (-1, 1):
        i = side[dc]
        when(r["near"][dc], edges[dc].wait_send)
        when(r["at_seam"][dc], seams[dc][0].wait_send, seams[dc][1].wait_send)
        for part in range(2):
            when(r["relay"][part], forward(part, dc).wait_send)
        when(corners[dc][0], corners[dc][1].wait_send, landed(canvas(outer_at, HALO, rim_at[dc], HALO), corner_recv.at[i]).wait)
        when(r["has"][dc], inside[dc].wait_send, landed(canvas(inner_at, HALO, rim_at[dc], HALO), corner_recv.at[2 + i]).wait)
    for cond, copy in blanks:
        when(cond, copy.wait)
    own.wait()


def outer_at_of_mate(at, cells):
    return pl.multiple_of(cells + HALO - at, HALO)


def exchange_halo(obj, limits):
    cells = obj.shape[1]
    dma = pltpu.SemaphoreType.DMA
    return pl.pallas_call(
        functools.partial(halo_kernel, limits),
        out_shape=jax.ShapeDtypeStruct((2, cells + 2 * HALO, cells + 2 * HALO), F32),
        in_specs=[pl.BlockSpec(memory_space=pl.ANY)],
        out_specs=pl.BlockSpec(memory_space=pl.ANY),
        scratch_shapes=[
            pltpu.VMEM((2, cells, cells), F32),
            pltpu.VMEM((2, cells, cells + 2 * HALO), F32),
            pltpu.VMEM((2, 2, cells // 2, HALO), F32),
            dma, dma, dma((7,)), dma((4,)), dma((4,)), dma((2,)), dma((2,)), dma((2,)), dma((2,)), dma((2,)), dma((2,)),
            dma((4,)), dma((4,)),
        ],
        compiler_params=pltpu.CompilerParams(collective_id=0, has_side_effects=True, vmem_limit_bytes=60 * 2**20),
    )(obj)


def place():
    return lax.axis_index("row"), lax.axis_index("col")


def remote(src, dst, device, send, recv):
    return pltpu.make_async_remote_copy(src_ref=src, dst_ref=dst, send_sem=send, recv_sem=recv,
                                        device_id=device, device_id_type=MESH)


def landed(ref, sem):
    return pltpu.make_async_copy(ref, ref, sem)


def roles(limits):
    row, col = place()
    rows, cols = limits
    core = row % 2
    seam = cols // 2
    up, down = row > 0, row < rows - 1
    outer = jnp.where(core == 0, row - 1, row + 1)
    has_outer = jnp.logical_and(outer >= 0, outer < rows)
    near = {-1: jnp.logical_and(col > 0, col != seam), 1: jnp.logical_and(col < cols - 1, col != seam - 1)}
    at_seam = {-1: col == seam, 1: col == seam - 1}
    has = {-1: col > 0, 1: col < cols - 1}
    relay = {0: col == cols - 1, 1: col == 0}
    return dict(row=row, col=col, core=core, mate=(row + 1 - 2 * core, col), outer=(outer, col), has_outer=has_outer,
                near=near, at_seam=at_seam, has=has, relay=relay, seam=seam, cols=cols)


def greet(r):
    barrier = pltpu.get_barrier_semaphore()
    row, col, cols, seam = r["row"], r["col"], r["cols"], r["seam"]
    seam_any = jnp.logical_or(r["at_seam"][-1], r["at_seam"][1])
    relay_any = jnp.logical_or(r["relay"][0], r["relay"][1])
    pl.semaphore_signal(barrier, inc=1, device_id=r["mate"], device_id_type=MESH)
    total = jnp.int32(1)

    def to(cond, device):
        @pl.when(cond)
        def _():
            pl.semaphore_signal(barrier, inc=1, device_id=device, device_id_type=MESH)

        return cond.astype(jnp.int32)

    total += to(r["has_outer"], r["outer"])
    for dc in (-1, 1):
        total += to(r["has"][dc], (row, col + dc))
    for target in (0, cols - 1):
        total += to(seam_any, (row, target))
    for target in (seam - 1, seam):
        total += to(relay_any, (row, target))
    return barrier, total


def when(cond, *actions):
    @pl.when(cond)
    def _():
        for action in actions:
            action()


def halo_kernel(limits, source_ref, amp_ref, par_ref, flip_ref, canvas_ref, order_ref, obj_ref, amp, zeros, passing,
                amp_sem, load_sem, own_sem, zero_sems, row_send, row_recv, col_send, col_recv,
                seam_send, seam_recv, pass_send, pass_recv, corner_send, corner_recv):
    cells = obj_ref.shape[1]
    half = cells // 2
    load = pltpu.make_async_copy(source_ref, obj_ref, load_sem)
    load.start()
    take = pltpu.make_async_copy(amp_ref, amp, amp_sem)
    take.start()
    r = roles(limits)
    row, col, core, seam, cols = r["row"], r["col"], r["core"], r["seam"], r["cols"]
    barrier, total = greet(r)
    own = pltpu.make_async_copy(obj_ref, canvas_ref.at[:, pl.ds(HALO, cells), pl.ds(HALO, cells)], own_sem)
    zeros[...] = jnp.zeros_like(zeros)
    load.wait()
    own.start()
    pl.semaphore_wait(barrier, total)

    outer_from = pl.multiple_of(jnp.where(core == 0, 0, cells - HALO), HALO)
    inner_from = pl.multiple_of(jnp.where(core == 0, cells - HALO, 0), HALO)
    outer_at = pl.multiple_of(jnp.where(core == 0, 0, cells + HALO), HALO)
    inner_at = pl.multiple_of(jnp.where(core == 0, cells + HALO, 0), HALO)
    strips = ((0, HALO), (cells - HALO, HALO), (HALO, cells - 2 * HALO))
    edge_from = {-1: 0, 1: cells - HALO}
    rim_at = {-1: 0, 1: cells + HALO}
    side = {-1: 0, 1: 1}

    def canvas(top, tall, left, wide):
        return canvas_ref.at[:, pl.ds(top, tall), pl.ds(left, wide)]

    def tile(top, tall, left, wide):
        return obj_ref.at[:, pl.ds(top, tall), pl.ds(left, wide)]

    edges = {}
    seams = {}
    for dc in (-1, 1):
        edges[dc] = remote(tile(0, cells, edge_from[dc], HALO), canvas(HALO, cells, rim_at[-dc], HALO), (row, col + dc),
                           col_send.at[side[dc]], col_recv.at[side[-dc]])
        when(r["near"][dc], edges[dc].start)
        pair = []
        for part, target in ((0, cols - 1), (1, 0)):
            pair.append(remote(tile(part * half, half, edge_from[dc], HALO), passing.at[side[dc]], (row, target),
                               seam_send.at[part], seam_recv.at[side[dc]]))
        seams[dc] = pair
        when(r["at_seam"][dc], pair[0].start, pair[1].start)

    inner = remote(tile(inner_from, HALO, 0, cells), canvas(outer_at_of_mate(inner_at, cells), HALO, HALO, cells), r["mate"],
                   row_send.at[3], row_recv.at[3])
    inner.start()
    outers = []
    for i, (left, wide) in enumerate(strips):
        copy = remote(tile(outer_from, HALO, left, wide), canvas(outer_at_of_mate(outer_at, cells), HALO, HALO + left, wide), r["outer"],
                      row_send.at[i], row_recv.at[i])
        outers.append(copy)
        when(r["has_outer"], copy.start)
    blanks = []
    for i, (cond, ref) in enumerate((
        (jnp.logical_not(r["has_outer"]), canvas(outer_at, HALO, 0, cells + 2 * HALO)),
        (jnp.logical_not(r["has"][-1]), canvas(HALO, cells, 0, HALO)),
        (jnp.logical_not(r["has"][1]), canvas(HALO, cells, cells + HALO, HALO)),
    )):
        source = zeros.at[:, pl.ds(0, HALO), :] if i == 0 else zeros.at[:, pl.ds(0, cells), pl.ds(0, HALO)]
        copy = pltpu.make_async_copy(source, ref, zero_sems.at[i])
        blanks.append((cond, copy))
        when(cond, copy.start)
    for dc in (-1, 1):
        for k, top in ((0, inner_at), (1, outer_at)):
            need = jnp.logical_not(r["has"][dc])
            if k:
                need = jnp.logical_and(need, r["has_outer"])
            copy = pltpu.make_async_copy(zeros.at[:, pl.ds(0, HALO), pl.ds(0, HALO)], canvas(top, HALO, rim_at[dc], HALO),
                                         zero_sems.at[3 + 2 * side[dc] + k])
            blanks.append((need, copy))
            when(need, copy.start)

    def forward(part, dc):
        target = seam if dc == 1 else seam - 1
        return remote(passing.at[side[dc]], canvas(HALO + part * half, half, rim_at[-dc], HALO), (row, target),
                      pass_send.at[side[dc]], pass_recv.at[part])

    def relay(part, dc):
        when(r["relay"][part], landed(passing.at[side[dc]], seam_recv.at[side[dc]]).wait, forward(part, dc).start)

    relay(0, -1)
    relay(1, 1)
    corners = {}
    for dc in (-1, 1):
        i = side[dc]
        strip = canvas(outer_at, HALO, HALO + edge_from[dc], HALO)
        give = jnp.logical_and(r["has_outer"], r["has"][dc])
        corners[dc] = (give, remote(strip, canvas(outer_at, HALO, rim_at[-dc], HALO), (row, col + dc),
                                    corner_send.at[i], corner_recv.at[1 - i]))
        when(r["has_outer"], landed(strip, row_recv.at[i]).wait)
        when(give, corners[dc][1].start)
    relay(0, 1)
    relay(1, -1)
    take.wait()

    def sort(s, c):
        hi, lo = split(amp[s])
        hi, lo = split(mm(hi, par_ref[...]) + mm(lo, par_ref[...]))
        amp[s] = mm(flip_ref[...], hi) + mm(flip_ref[...], lo)
        return c

    lax.fori_loop(0, amp.shape[0], sort, 0)
    give_back = pltpu.make_async_copy(amp, order_ref, amp_sem)
    give_back.start()
    inside = {}
    for dc in (-1, 1):
        i = side[dc]
        near_mate = pl.multiple_of(inner_from + HALO, HALO)
        when(r["near"][dc], landed(canvas(HALO, cells, rim_at[dc], HALO), col_recv.at[i]).wait)
        for part in range(2):
            when(r["at_seam"][dc], landed(canvas(HALO + part * half, half, rim_at[dc], HALO), pass_recv.at[part]).wait)
        inside[dc] = remote(canvas(near_mate, HALO, rim_at[dc], HALO), canvas(outer_at_of_mate(inner_at, cells), HALO, rim_at[dc], HALO),
                            r["mate"], corner_send.at[2 + i], corner_recv.at[2 + i])
        when(r["has"][dc], inside[dc].start)

    inner.wait_send()
    landed(canvas(inner_at, HALO, HALO, cells), row_recv.at[3]).wait()
    when(r["has_outer"], *[copy.wait_send for copy in outers])
    when(r["has_outer"], landed(canvas(outer_at, HALO, HALO + strips[2][0], strips[2][1]), row_recv.at[2]).wait)
    for dc in (-1, 1):
        i = side[dc]
        when(r["near"][dc], edges[dc].wait_send)
        when(r["at_seam"][dc], seams[dc][0].wait_send, seams[dc][1].wait_send)
        for part in range(2):
            when(r["relay"][part], forward(part, dc).wait_send)
        when(corners[dc][0], corners[dc][1].wait_send, landed(canvas(outer_at, HALO, rim_at[dc], HALO), corner_recv.at[i]).wait)
        when(r["has"][dc], inside[dc].wait_send, landed(canvas(inner_at, HALO, rim_at[dc], HALO), corner_recv.at[2 + i]).wait)
    for cond, copy in blanks:
        when(cond, copy.wait)
    own.wait()
    give_back.wait()


def outer_at_of_mate(at, cells):
    return pl.multiple_of(cells + HALO - at, HALO)


def exchange_halo(obj, amp, limits):
    n = amp.shape[1]
    par = parity_table(n)
    vmem = pl.BlockSpec(memory_space=pltpu.VMEM)
    cells = obj.shape[1]
    dma = pltpu.SemaphoreType.DMA
    return pl.pallas_call(
        functools.partial(halo_kernel, limits),
        out_shape=(jax.ShapeDtypeStruct((2, cells + 2 * HALO, cells + 2 * HALO), F32), jax.ShapeDtypeStruct(amp.shape, F32)),
        in_specs=[pl.BlockSpec(memory_space=pl.ANY), pl.BlockSpec(memory_space=pl.ANY), vmem, vmem],
        out_specs=(pl.BlockSpec(memory_space=pl.ANY), pl.BlockSpec(memory_space=pl.ANY)),
        scratch_shapes=[
            pltpu.VMEM((2, cells, cells), F32),
            pltpu.VMEM(amp.shape, F32),
            pltpu.VMEM((2, cells, cells + 2 * HALO), F32),
            pltpu.VMEM((2, 2, cells // 2, HALO), F32),
            dma, dma, dma, dma((7,)), dma((4,)), dma((4,)), dma((2,)), dma((2,)), dma((2,)), dma((2,)), dma((2,)), dma((2,)),
            dma((4,)), dma((4,)),
        ],
        compiler_params=pltpu.CompilerParams(collective_id=0, has_side_effects=True, vmem_limit_bytes=60 * 2**20),
    )(obj, amp, jnp.asarray(par), jnp.asarray(np.ascontiguousarray(par.T)))


SIDES = [(-1, 0), (1, 0), (0, -1), (0, 1), (-1, -1), (-1, 1), (1, -1), (1, 1)]


ORDERS = [(0, 1, 2), (1, 2, 0), (2, 0, 1), (1, 0, 2)]


def spots():
    row, col = place()
    return (row // 2 % 2 * 2 + col // 4, row // 4, col % 4)


def along(axis, by):
    row, col = place()
    at = list(spots())
    at[axis] = (at[axis] + by) % 4
    return (at[1] * 4 + at[0] // 2 * 2 + row % 2, at[0] % 2 * 4 + at[2])


def finish_kernel(limits, spread_ref, pg_ref, energy_ref, obj_ref, probe_ref, illum_ref,
                  onew_ref, pnew_ref, land_rows, land_cols, land_inner, land_outer, out_cols, out_ends, passing, total_ref, mate_half, mate_energy, warm, heat,
                  box1, box2, box3, seam_send, seam_recv, pass_send, pass_recv, near_send, near_recv, row_send, row_recv,
                  corner_send, corner_recv, mate_send, mate_recv, down_send, down_recv, up_send, up_recv,
                  heat_send, heat_recv):
    cells = obj_ref.shape[1]
    row, col = place()
    core = row % 2
    mate = (row + 1 - 2 * core, col)
    at = spots()
    units = len(ORDERS)
    unit = pg_ref.shape[1] // units

    r = roles(limits)
    barrier, total = greet(r)
    pl.semaphore_signal(barrier, inc=1, device_id=mate, device_id_type=MESH)
    for axis in range(3):
        for by in (1, 2, 3):
            pl.semaphore_signal(barrier, inc=1, device_id=along(axis, by), device_id_type=MESH)
    pl.semaphore_wait(barrier, total + 10)

    firsts = [remote(energy_ref, mate_energy, mate, mate_send.at[0], mate_recv.at[0])]
    for u in range(units):
        rows = pl.ds(u * unit, unit)
        firsts.append(remote(pg_ref.at[1 - core, rows], mate_half.at[rows], mate, mate_send.at[1 + u], mate_recv.at[1 + u]))
    half = cells // 2
    seam, cols = r["seam"], r["cols"]
    outer_from = pl.multiple_of(jnp.where(core == 0, 0, cells - HALO), HALO)
    inner_from = pl.multiple_of(jnp.where(core == 0, cells - HALO, 0), HALO)
    outer_at = pl.multiple_of(jnp.where(core == 0, 0, cells + HALO), HALO)
    inner_at = pl.multiple_of(jnp.where(core == 0, cells + HALO, 0), HALO)
    edge_from = {-1: 0, 1: cells - HALO}
    rim_at = {-1: 0, 1: cells + HALO}
    side = {-1: 0, 1: 1}
    inside, nears, seams, ends, corners = {}, {}, {}, {}, {}

    def region(top, tall, left, wide):
        return spread_ref.at[:, pl.ds(top, tall), pl.ds(left, wide)]

    for dc in (-1, 1):
        i = side[dc]
        inside[dc] = remote(region(inner_at, HALO, rim_at[dc], HALO), land_inner.at[i], mate, corner_send.at[i], corner_recv.at[i])
        when(r["has"][dc], inside[dc].start)
    for copy in firsts:
        copy.start()
    for dc in (-1, 1):
        i = side[dc]

        @pl.when(r["has"][dc])
        def _(dc=dc, i=i):
            inside[dc].wait_recv()
            for part in range(2):
                out_cols[i, part] = spread_ref[part, HALO:HALO + cells, rim_at[dc]:rim_at[dc] + HALO]
                out_cols[i, part, pl.ds(inner_from, HALO), :] += land_inner[i, part]

        seams[dc] = [remote(out_cols.at[i, :, pl.ds(part * half, half), :], passing.at[i], (row, target),
                            seam_send.at[part], seam_recv.at[i]) for part, target in ((0, cols - 1), (1, 0))]
        when(r["at_seam"][dc], seams[dc][0].start, seams[dc][1].start)

    inner = remote(region(inner_at, HALO, HALO, cells), land_rows.at[1], mate, row_send.at[3], row_recv.at[3])
    middle = remote(region(outer_at, HALO, 2 * HALO, cells - 2 * HALO), land_rows.at[0, :, :, pl.ds(HALO, cells - 2 * HALO)], r["outer"],
                    row_send.at[2], row_recv.at[2])

    def start_fold():
        for dc in (-1, 1):
            i = side[dc]
            corners[dc] = (jnp.logical_and(r["has_outer"], r["has"][dc]),
                           remote(region(outer_at, HALO, rim_at[dc], HALO), land_outer.at[1 - i], (row, col + dc),
                                  corner_send.at[2 + i], corner_recv.at[3 - i]))
            when(corners[dc][0], corners[dc][1].start)
        when(r["has_outer"], middle.start)
        for dc in (-1, 1):
            i = side[dc]
            nears[dc] = remote(out_cols.at[i], land_cols.at[1 - i], (row, col + dc), near_send.at[i], near_recv.at[1 - i])
            when(r["near"][dc], nears[dc].start)
        inner.start()

    def forward(part, dc):
        i = side[dc]
        target = seam if dc == 1 else seam - 1
        return remote(passing.at[i], land_cols.at[1 - i, :, pl.ds(part * half, half), :], (row, target), pass_send.at[i], pass_recv.at[part])

    def relay(part, dc):
        when(r["relay"][part], landed(passing.at[side[dc]], seam_recv.at[side[dc]]).wait, forward(part, dc).start)

    def send_ends():
        for dc in (-1, 1):
            i = side[dc]
            ends[dc] = remote(out_ends.at[i], land_rows.at[0, :, :, pl.ds(edge_from[dc], HALO)], r["outer"], row_send.at[i], row_recv.at[i])

            @pl.when(r["has_outer"])
            def _(dc=dc, i=i):
                left = HALO + edge_from[dc]
                for part in range(2):
                    out_ends[i, part] = spread_ref[part, pl.ds(outer_at, HALO), left:left + HALO]

                @pl.when(r["has"][dc])
                def _():
                    landed(land_outer.at[i], corner_recv.at[2 + i]).wait()
                    for part in range(2):
                        out_ends[i, part] += land_outer[i, part]

                ends[dc].start()

    def piece(u, depth, spot):
        order = ORDERS[u]
        start = u * unit
        if depth == 1:
            return pl.ds(pl.multiple_of(start + spot * (unit // 4), unit // 4), unit // 4), slice(None)
        start = start + at[order[0]] * (unit // 4)
        if depth == 2:
            return pl.ds(pl.multiple_of(start + spot * (unit // 16), unit // 16), unit // 16), slice(None)
        start = start + at[order[1]] * (unit // 16)
        return (pl.ds(pl.multiple_of(start + spot // 2 * 8, 8), 8), pl.ds(pl.multiple_of(spot % 2 * 128, 128), 128))

    def own(u, depth):
        return piece(u, depth, at[ORDERS[u][depth - 1]])

    boxes = (box1, box2, box3)
    waiting = []

    def down(u, depth):
        axis = ORDERS[u][depth - 1]
        out = []
        for by in (1, 2, 3):
            copy = remote(total_ref.at[piece(u, depth, (at[axis] + by) % 4)], boxes[depth - 1].at[u, by - 1], along(axis, by),
                          down_send.at[u, depth - 1, by - 1], down_recv.at[u, depth - 1, by - 1])
            copy.start()
            out.append(copy)
        waiting.extend(out)
        return out

    def pass_heat(axis):
        out = []
        for by in (1, 2, 3):
            copy = remote(warm.at[axis], heat.at[axis, by - 1], along(axis, by), heat_send.at[axis, by - 1], heat_recv.at[axis, by - 1])
            copy.start()
            out.append(copy)
        waiting.extend(out)
        return out

    firsts[0].wait_recv()
    warm[0] = energy_ref[...] + mate_energy[...]
    hot = pass_heat(0)
    flying = []
    for u in range(units):
        rows = pl.ds(u * unit, unit)
        firsts[1 + u].wait_recv()
        total_ref[rows, :] = pg_ref[core, rows, :] + mate_half[rows, :]
        flying.append(down(u, 1))
    waiting.extend(firsts)
    start_fold()

    share = 1.0 / illum_ref[0]
    step_rows = 64

    def base(j, c):
        r = pl.ds(pl.multiple_of(j * step_rows, step_rows), step_rows)
        rr = pl.ds(pl.multiple_of(j * step_rows + HALO, step_rows), step_rows)
        for part in range(2):
            onew_ref[part, r, :] = obj_ref[part, r, :] + spread_ref[part, rr, HALO:HALO + cells] * share
        return c

    lax.fori_loop(0, cells // step_rows, base, 0)
    relay(0, -1)
    relay(1, 1)

    for depth in (1, 2, 3):
        if depth == 2:
            send_ends()
        if depth == 3:
            relay(0, 1)
            relay(1, -1)
        for copy in hot:
            copy.wait_recv()
        fresh = warm[depth - 1] + heat[depth - 1, 0] + heat[depth - 1, 1] + heat[depth - 1, 2]
        if depth < 3:
            warm[depth] = fresh
            hot = pass_heat(depth)
        for u in range(units):
            for copy in flying[u]:
                copy.wait_recv()
            box = boxes[depth - 1]
            where = own(u, depth)
            summed = total_ref[where] + box[u, 0] + box[u, 1] + box[u, 2]
            if depth < 3:
                total_ref[where] = summed
                flying[u] = down(u, depth + 1)
            else:
                pnew_ref[(core,) + where] = probe_ref[(core,) + where] + summed / (fresh[:, :128] + EPSILON)

    def up(u, depth):
        axis = ORDERS[u][depth - 1]
        spot = pnew_ref.at[(core,) + own(u, depth)]
        out = []
        for by in (1, 2, 3):
            landed = pnew_ref.at[(core,) + piece(u, depth, (at[axis] + 4 - by) % 4)]
            copy = remote(spot, spot, along(axis, by), up_send.at[u, depth - 1, by - 1], up_recv.at[u, depth - 1, by - 1])
            copy.start()
            waiting.append(copy)
            out.append(pltpu.make_async_copy(landed, landed, up_recv.at[u, depth - 1, by - 1]))
        return out

    for u in range(units):
        flying[u] = up(u, 3)
    lasts = []
    for depth in (3, 2, 1):
        for u in range(units):
            for copy in flying[u]:
                copy.wait()
            if depth > 1:
                flying[u] = up(u, depth - 1)
            else:
                rows = pl.ds(u * unit, unit)
                done = pnew_ref.at[core, rows]
                copy = remote(done, done, mate, mate_send.at[5 + u], mate_recv.at[5 + u])
                copy.start()
                waiting.append(copy)
                got = pnew_ref.at[1 - core, rows]
                lasts.append(pltpu.make_async_copy(got, got, mate_recv.at[5 + u]))

    inner.wait()
    for part in range(2):
        onew_ref[part, pl.ds(inner_from, HALO), :] += land_rows[1, part] * share

    @pl.when(r["has_outer"])
    def _():
        middle.wait()
        for dc in (-1, 1):
            ends[dc].wait()
        for part in range(2):
            onew_ref[part, pl.ds(outer_from, HALO), :] += land_rows[0, part] * share

    for dc in (-1, 1):
        i = side[dc]
        when(r["near"][dc], nears[dc].wait_send, landed(land_cols.at[i], near_recv.at[i]).wait)
        when(r["at_seam"][dc], seams[dc][0].wait_send, seams[dc][1].wait_send)
        for part in range(2):
            when(r["at_seam"][dc], landed(land_cols.at[i, :, pl.ds(part * half, half), :], pass_recv.at[part]).wait)
            when(r["relay"][part], forward(part, dc).wait_send)
        when(corners[dc][0], corners[dc][1].wait_send)

        @pl.when(r["has"][dc])
        def _(dc=dc, i=i):
            inside[dc].wait_send()
            for part in range(2):
                onew_ref[part, :, edge_from[dc]:edge_from[dc] + HALO] += land_cols[i, part] * share

    for copy in lasts:
        copy.wait()
    for copy in waiting:
        copy.wait_send()


def finish(spread, pg, energy, obj, probe, illum, limits):
    cells = obj.shape[1]
    rows, lanes = probe.shape[1], probe.shape[2]
    units = len(ORDERS)
    unit = rows // units
    vmem = pl.BlockSpec(memory_space=pltpu.VMEM)
    dma = pltpu.SemaphoreType.DMA
    return pl.pallas_call(
        functools.partial(finish_kernel, limits),
        out_shape=(jax.ShapeDtypeStruct(obj.shape, F32), jax.ShapeDtypeStruct(probe.shape, F32)),
        in_specs=[vmem, vmem, vmem, vmem, vmem, pl.BlockSpec(memory_space=pltpu.SMEM)],
        out_specs=(vmem, vmem),
        scratch_shapes=[
            pltpu.VMEM((2, 2, HALO, cells), F32),
            pltpu.VMEM((2, 2, cells, HALO), F32),
            pltpu.VMEM((2, 2, HALO, HALO), F32),
            pltpu.VMEM((2, 2, HALO, HALO), F32),
            pltpu.VMEM((2, 2, cells, HALO), F32),
            pltpu.VMEM((2, 2, HALO, HALO), F32),
            pltpu.VMEM((2, 2, cells // 2, HALO), F32),
            pltpu.VMEM((rows, lanes), F32),
            pltpu.VMEM((rows, lanes), F32),
            pltpu.VMEM((8, 128), F32),
            pltpu.VMEM((3, 8, 128), F32),
            pltpu.VMEM((3, 3, 8, 128), F32),
            pltpu.VMEM((units, 3, unit // 4, lanes), F32),
            pltpu.VMEM((units, 3, unit // 16, lanes), F32),
            pltpu.VMEM((units, 3, 8, 128), F32),
            dma((2,)), dma((2,)), dma((2,)), dma((2,)), dma((2,)), dma((2,)), dma((4,)), dma((4,)), dma((4,)), dma((4,)),
            dma((9,)), dma((9,)),
            dma((units, 3, 3)), dma((units, 3, 3)), dma((units, 3, 3)), dma((units, 3, 3)),
            dma((3, 3)), dma((3, 3)),
        ],
        compiler_params=pltpu.CompilerParams(collective_id=1, has_side_effects=True, vmem_limit_bytes=60 * 2**20),
    )(spread, pg, energy, obj, probe, illum)


def body(limits, object_field, probe, amplitudes, positions, counts):
    canvas, order = exchange_halo(object_field, amplitudes[0, 0], limits)
    spread, probe_grad, shift, energy, illum = step(positions[0, 0], counts[0], canvas, probe, order)
    n = probe.shape[2]
    flat = (2, probe.shape[1] * n, n)
    object_new, probe_new = finish(spread, probe_grad.reshape(flat), energy, object_field, probe.reshape(flat), illum, limits)
    return (object_new, probe_new.reshape(probe.shape), shift[None, None])


def solution(mesh):
    return jax.shard_map(
        functools.partial(body, (mesh.shape["row"], mesh.shape["col"])),
        mesh=mesh,
        in_specs=(
            P(None, "row", "col"),
            P(),
            P("row", "col", None, None, None),
            P("row", "col", None, None),
            P("row", "col"),
        ),
        out_specs=(P(None, "row", "col"), P(), P("row", "col", None, None)),
        check_vma=False,
    )
```
